32 devices in a mesh: rows: 8 (over y, x, core), blk: 4 (over z).
Axes of the slice: x: 2, y: 2, z: 4, core: 2. Of those that a mesh axis runs over, the one named last changes fastest.
Arguments:
- tokens: bfloat16 [8, 1024, 1024], P('rows', 'blk'), may hold values from -6 to 6
- segment_ids: int32 [8, 1024], P('rows', 'blk'), may hold values from 0 to 510, as said below
- out_grad: bfloat16 [8, 1024, 1024], P('rows', 'blk'), may hold values from -6 to 6
- qkv_weight: bfloat16 [2, 1024, 3072], P(None, ('rows', 'blk')), may hold values from -0.1875 to 0.1875
- qv_bias: bfloat16 [2, 2048], P(None, ('rows', 'blk')), may hold values from -2 to 2
- out_weight: bfloat16 [2, 1024, 1024], P(None, ('rows', 'blk')), may hold values from -0.75 to 0.75
- out_bias: bfloat16 [2, 1024], P(None, ('rows', 'blk')), may hold values from -2 to 2
- up_weight: bfloat16 [2, 1024, 4096], P(None, ('rows', 'blk')), may hold values from -0.1875 to 0.1875
- up_bias: bfloat16 [2, 4096], P(None, ('rows', 'blk')), may hold values from -2 to 2
- down_weight: bfloat16 [2, 4096, 1024], P(None, ('rows', 'blk')), may hold values from -0.1875 to 0.1875
- down_bias: bfloat16 [2, 1024], P(None, ('rows', 'blk')), may hold values from -2 to 2
- norm_gain: bfloat16 [2, 2, 1024], P(None, None, ('rows', 'blk')), may hold values from 0.25 to 1.75
- norm_shift: bfloat16 [2, 2, 1024], P(None, None, ('rows', 'blk')), may hold values from -3 to 3
Outputs:
- result: bfloat16 [8, 1024, 1024], P('rows', 'blk')
- input_grad: bfloat16 [8, 1024, 1024], P('rows', 'blk')
- qkv_weight_grad: float32 [2, 1024, 3072], P(None, ('rows', 'blk'))
- qv_bias_grad: float32 [2, 2048], P(None, ('rows', 'blk'))
- out_weight_grad: float32 [2, 1024, 1024], P(None, ('rows', 'blk'))
- out_bias_grad: float32 [2, 1024], P(None, ('rows', 'blk'))
- up_weight_grad: float32 [2, 1024, 4096], P(None, ('rows', 'blk'))
- up_bias_grad: float32 [2, 4096], P(None, ('rows', 'blk'))
- down_weight_grad: float32 [2, 4096, 1024], P(None, ('rows', 'blk'))
- down_bias_grad: float32 [2, 1024], P(None, ('rows', 'blk'))
- norm_gain_grad: float32 [2, 2, 1024], P(None, None, ('rows', 'blk'))
- norm_shift_grad: float32 [2, 2, 1024], P(None, None, ('rows', 'blk'))
The draws below stay inside these ranges and needn't reach their ends.
Inputs may be any that keep to these rules, and one draw needn't show every extreme that they name: `segment_ids`: along each row the ids start at 0 and never fall; in every row one article starts within the first 256 positions and runs into the last 256.
All inputs are finite; a program needn't handle non-finite values.
Results may differ from the reference program's by a relative error of at most 0.025.
Values may be sent and summed in bfloat16 or wider, within the bound.
No kernel may reach another device: no remote copies, remote signals or barrier semaphores. Data moves between devices by JAX's collectives and lax.ppermute only.
A program may use at most 256 MiB of HBM per device.

```python
import jax
import jax.numpy as jnp
from jax import lax

D = 1024
HEADS = 8
HEAD_DIM = 128
FF = 4096
LAYERS = 2
BLK_TOK = 256
ROWS = 8
LEN = 1024


def draw_segment_ids(key, part):
    key = jax.random.fold_in(key, 7)
    first_key, second_key, third_key, fourth_key = jax.random.split(key, 4)
    full_row = jax.random.randint(fourth_key, (), 0, ROWS)
    is_full = jnp.arange(ROWS, dtype=jnp.int32)[:, None] == full_row
    opening = jax.random.randint(first_key, (ROWS, 1), 1, BLK_TOK)
    closing = jax.random.randint(second_key, (ROWS, 1), LEN - BLK_TOK + 1, LEN)
    opening = jnp.where(is_full, BLK_TOK - 1, opening)
    closing = jnp.where(is_full, LEN - BLK_TOK + 1, closing)
    places = jnp.arange(LEN, dtype=jnp.int32)[None, :]
    coins = jax.random.randint(third_key, (ROWS, LEN), 0, 8)
    outside = (places < opening) | (places > closing)
    edges = (places == opening) | (places == closing) | outside & ((coins == 0) | is_full) & (places > 0)
    return jnp.cumsum(edges.astype(jnp.int32), axis=1).astype(jnp.int32)


def level_of(key, shape, cuts, least, largest):
    loudness = 1.0
    for axis_at, shards_of in cuts:
        steps = jax.random.uniform(jax.random.fold_in(jax.random.fold_in(key, 6), axis_at), (shards_of,), jnp.float32, least / len(cuts), largest / len(cuts))
        loudness = loudness * jnp.repeat(jnp.exp(steps), shape[axis_at] // shards_of).reshape((-1,) + (1,) * (len(shape) - 1 - axis_at))
    return loudness


def scatter_about(key, shape, width, most, cuts=(), kind=jnp.bfloat16):
    level = level_of(key, shape, cuts, -0.22, 0.18) if cuts else 1.0
    array = jax.random.normal(key, shape, jnp.float32) * width * level
    return jnp.minimum(jnp.maximum(array, -most), most).astype(kind)


def setup_inputs(seed: int = 0) -> dict:
    splits = jax.random.split(jax.random.key(seed), 14)
    tokens = scatter_about(splits[0], (ROWS, LEN, D), 1.0, 6.0, ((0, 8), (1, 4)))
    segment_ids = draw_segment_ids(jax.random.fold_in(splits[13], 71), 0)
    out_grad = scatter_about(splits[2], (ROWS, LEN, D), 1.0, 6.0, ((0, 8), (1, 4)))
    qkv_weight = scatter_about(splits[3], (LAYERS, D, 3 * D), D ** -0.5, 0.1875, ((1, 32),))
    qv_bias = scatter_about(splits[4], (LAYERS, 2 * D), 0.3, 2.0, ((1, 32),))
    out_weight = scatter_about(splits[5], (LAYERS, D, D), (D // 16) ** -0.5, 0.75, ((1, 32),))
    out_bias = scatter_about(splits[6], (LAYERS, D), 0.3, 2.0, ((1, 32),))
    up_weight = scatter_about(splits[7], (LAYERS, D, FF), D ** -0.5, 0.1875, ((1, 32),))
    up_bias = scatter_about(splits[8], (LAYERS, FF), 0.3, 2.0, ((1, 32),))
    down_weight = scatter_about(splits[9], (LAYERS, FF, D), (FF // 4) ** -0.5, 0.1875, ((1, 32),))
    down_bias = scatter_about(splits[10], (LAYERS, D), 0.3, 2.0, ((1, 32),))
    norm_gain = jnp.clip(1.0 + 0.15 * jax.random.normal(splits[11], (LAYERS, 2, D), jnp.float32), 0.25, 1.75).astype(jnp.bfloat16)
    norm_shift = scatter_about(splits[12], (LAYERS, 2, D), 0.5, 3.0, ((2, 32),))
    return {"tokens": tokens, "segment_ids": segment_ids, "out_grad": out_grad, "qkv_weight": qkv_weight, "qv_bias": qv_bias, "out_weight": out_weight, "out_bias": out_bias, "up_weight": up_weight, "up_bias": up_bias, "down_weight": down_weight, "down_bias": down_bias, "norm_gain": norm_gain, "norm_shift": norm_shift}


@jax.custom_vjp
def low(v):
    return lax.optimization_barrier(v.astype(jnp.bfloat16)).astype(jnp.float32)

@jax.custom_vjp
def low_back(v):
    return v

def low_keep(v):
    return (low(v), None)

def low_pass(kept, grad):
    return (grad,)

def back_keep(v):
    return (v, None)

def back_low(kept, grad):
    return (low(grad),)
low.defvjp(low_keep, low_pass)
low_back.defvjp(back_keep, back_low)
norm_eps = 1e-05
masked_score = -1e+30

def layer_norm(values, gain, shift):
    centre = values - lax.optimization_barrier(jnp.mean(values, axis=-1, keepdims=True))
    spread = lax.optimization_barrier(jnp.mean(centre * centre, axis=-1, keepdims=True))
    return centre * lax.rsqrt(spread + norm_eps) * gain + shift

def head_slopes(heads):
    return jnp.exp2(-8.0 * (jnp.arange(heads, dtype=jnp.float32) + 1.0) / heads)

def attend_row(pieces):
    query, keys, values, segments = pieces
    length = query.shape[0]
    places = jnp.arange(length, dtype=jnp.int32)
    scores = jnp.einsum('qhd,khd->hqk', query.reshape(length, HEADS, HEAD_DIM), keys.reshape(length, HEADS, HEAD_DIM), precision=lax.Precision.HIGHEST) * HEAD_DIM ** (-0.5)
    distance = (places[:, None] - places[None, :]).astype(jnp.float32)
    scores = low_back(scores - head_slopes(HEADS)[:, None, None] * distance[None])
    allowed = (segments[:, None] == segments[None, :]) & (places[None, :] <= places[:, None])
    probs_full = low(jax.nn.softmax(jnp.where(allowed[None], scores, masked_score), axis=-1))
    mixed = jnp.einsum('hqk,khd->qhd', probs_full, values.reshape(length, HEADS, HEAD_DIM), precision=lax.Precision.HIGHEST)
    return mixed.reshape(length, HEADS * HEAD_DIM)

def residual_block(stream, segment_ids, weights):
    w_qkv, b_qv, w_out, b_out, w_up, b_up, w_down, b_down, gains, shifts = weights
    row_count, length = segment_ids.shape
    model_width = stream.shape[1]
    highest = lax.Precision.HIGHEST
    normed = low(layer_norm(stream, gains[0], shifts[0]))
    bias_full = jnp.concatenate([b_qv[:model_width], jnp.zeros((model_width,), jnp.float32), b_qv[model_width:]])
    projected = low(low_back(jnp.dot(normed, w_qkv, precision=highest) + bias_full))
    query = projected[:, :model_width].reshape(row_count, length, model_width)
    keys = projected[:, model_width:2 * model_width].reshape(row_count, length, model_width)
    values = projected[:, 2 * model_width:].reshape(row_count, length, model_width)
    attended = lax.map(jax.checkpoint(attend_row), (query, keys, values, segment_ids))
    attended = low(low_back(attended.reshape(row_count * length, model_width)))
    middle = stream + low_back(jnp.dot(attended, w_out, precision=highest) + b_out)
    normed_two = low(layer_norm(middle, gains[1], shifts[1]))
    hidden = low(jax.nn.gelu(low_back(jnp.dot(normed_two, w_up, precision=highest) + b_up)))
    return middle + low_back(jnp.dot(hidden, w_down, precision=highest) + b_down)

def reference(tokens, segment_ids, out_grad, qkv_weight, qv_bias, out_weight, out_bias, up_weight, up_bias, down_weight, down_bias, norm_gain, norm_shift):
    row_count, length, model_width = tokens.shape
    params = tuple((item.astype(jnp.float32) for item in (qkv_weight, qv_bias, out_weight, out_bias, up_weight, up_bias, down_weight, down_bias, norm_gain, norm_shift)))

    def forward(stream, *weights):
        for layer_index in range(LAYERS):
            stream = residual_block(stream, segment_ids, tuple((item[layer_index] for item in weights)))
        return stream
    start = tokens.astype(jnp.float32).reshape(row_count * length, model_width)
    final, pull = jax.vjp(forward, start, *params)
    grads = pull(out_grad.astype(jnp.float32).reshape(row_count * length, model_width))
    return (final.astype(jnp.bfloat16).reshape(row_count, length, model_width), grads[0].astype(jnp.bfloat16).reshape(row_count, length, model_width), grads[1], grads[2], grads[3], grads[4], grads[5], grads[6], grads[7], grads[8], grads[9], grads[10])
```

```python
import functools

import jax
import jax.numpy as jnp
from jax import lax
from jax.experimental import pallas as pl
from jax.experimental.pallas import tpu as pltpu
from jax.sharding import Mesh
from jax.sharding import PartitionSpec as P

D = 1024
HEADS = 8
HEAD_DIM = 128
CORES = 2
norm_eps = 1e-05
masked_score = -1e30
BF = jnp.bfloat16
F32 = jnp.float32
VMEM_BYTES = 48 * 1024 * 1024

HI, XX, CORE, BLK = "hi", "xx", "core", "blk"


def nn(a, b):
    return lax.dot_general(a, b, (((1,), (0,)), ((), ())), preferred_element_type=F32)


def nt(a, b):
    return lax.dot_general(a, b, (((1,), (1,)), ((), ())), preferred_element_type=F32)


def tn(a, b):
    return lax.dot_general(a, b, (((0,), (0,)), ((), ())), preferred_element_type=F32)


def shape(dims, dtype):
    return jax.ShapeDtypeStruct(tuple(dims), dtype)


def run(kernel, outs, smem, arrays, scratch=(), flops=0, trans=0):
    size = lambda s: s.size * s.dtype.itemsize
    moved = sum(size(a) for a in arrays) + sum(size(o) for o in outs)
    return pl.pallas_call(
        kernel,
        out_shape=tuple(outs),
        in_specs=[pl.BlockSpec(memory_space=pltpu.SMEM)] * len(smem)
        + [pl.BlockSpec(memory_space=pltpu.VMEM)] * len(arrays),
        out_specs=tuple(pl.BlockSpec(memory_space=pltpu.VMEM) for _ in outs),
        scratch_shapes=list(scratch),
        compiler_params=pltpu.CompilerParams(vmem_limit_bytes=VMEM_BYTES),
        cost_estimate=pl.CostEstimate(flops=flops, bytes_accessed=moved, transcendentals=trans),
    )(*smem, *arrays)


def slots_of(xs):
    return [(k, dc) for k in range(xs) for dc in range(CORES)]


def lo_minus(me, xs, k, dc):
    return lax.rem(me[1] - k + xs, xs) * CORES + lax.rem(me[2] + dc, CORES)


def lo_plus(me, xs, k, dc):
    return lax.rem(me[1] + k, xs) * CORES + lax.rem(me[2] + dc, CORES)


def shift(x, axis, size, step):
    return lax.ppermute(x, axis, [(i, (i + step) % size) for i in range(size)])


def gather_lo(x, xs):
    out = {}
    for k in range(xs):
        out[k, 0] = x if k == 0 else shift(x, XX, xs, k)
    for k in range(xs):
        out[k, 1] = shift(out[k, 0], CORE, CORES, 1)
    return out


def scatter_lo(parts, xs):
    got = {}
    for k in list(range(1, xs)) + [0]:
        got[k] = shift(parts[k, 1].astype(BF), CORE, CORES, 1)
    terms = [parts[0, 0]]
    for k in range(1, xs):
        both = (parts[k, 0].astype(F32) + got[k].astype(F32)).astype(BF)
        terms.append(shift(both, XX, xs, -k))
    return terms + [got[0]]


def exchange_lo(blocks, xs, sign):
    got, out = {}, {}
    for k in list(range(1, xs)) + [0]:
        got[k] = shift(blocks[k, 1], CORE, CORES, 1)
    for k in range(xs):
        out[k, 0] = blocks[k, 0] if k == 0 else shift(blocks[k, 0], XX, xs, sign * k)
        out[k, 1] = got[k] if k == 0 else shift(got[k], XX, xs, sign * k)
    return out


def gather_hb(x, hs, ts):
    out = {}
    for kh in range(1, hs):
        out[kh, 0] = shift(x, HI, hs, kh)
    for kb in range(ts):
        out[0, kb] = x if kb == 0 else shift(x, BLK, ts, kb)
    for kh in range(1, hs):
        for kb in range(1, ts):
            out[kh, kb] = shift(out[0, kb], HI, hs, kh)
    return out


def scatter_hb(by_hi, hs, ts):
    got = [shift(by_hi[kh], HI, hs, kh) for kh in range(1, hs)]
    total = []
    for kb in range(ts):
        block = by_hi[0][kb].astype(F32)
        for g in got:
            block = block + g[kb].astype(F32)
        total.append(block)
    return [total[0]] + [shift(total[kb].astype(BF), BLK, ts, kb) for kb in range(1, ts)]


def norm_parts(values):
    centre = values - jnp.mean(values, axis=-1, keepdims=True)
    spread = jnp.mean(centre * centre, axis=-1, keepdims=True)
    rstd = lax.rsqrt(spread + norm_eps)
    return centre * rstd, rstd


def entry_kernel(tok, gain, shft, stream, normed):
    values = tok[...].astype(F32)
    stream[...] = values
    unit, _ = norm_parts(values)
    normed[...] = (unit * gain[...] + shft[...]).astype(BF)


def entry(tok, gain, shft):
    n = tok.shape[0]
    return run(entry_kernel, [shape((n, D), F32), shape((n, D), BF)], [], [tok, gain, shft])


def cut_kernel(xs, ts, layers, me, wq, wu, *outs):
    hs = wu.shape[2] // (ts * (outs[1].shape[1] // 1)) if False else None
    at = 0
    for layer in range(layers):
        for k, dc in slots_of(xs):
            lo = lo_plus(me, xs, k, dc)
            out_q, out_u = outs[at], outs[at + 1]
            at += 2
            wide = out_q.shape[1] // 3
            for j in range(3):
                off = pl.multiple_of(j * D + lo * wide, 128)
                out_q[:, j * wide : (j + 1) * wide] = wq[layer, :, pl.ds(off, wide)]
            full = wu.shape[2]
            mine = out_u.shape[1]
            parts = full // (ts * mine) if full // (ts * mine) > 0 else 1
            chunk = mine // 2
            for j in range(2):
                off = pl.multiple_of(j * (full // 2) + lo * chunk, 128)
                out_u[:, j * chunk : (j + 1) * chunk] = wu[layer, :, pl.ds(off, chunk)]


def cut(me, wq, wu, xs, ts):
    layers, rows, full = wu.shape
    outs = []
    for _ in range(layers):
        for _ in slots_of(xs):
            outs += [shape((rows, 3 * D // ts), BF), shape((rows, full // ts), BF)]
    got = run(functools.partial(cut_kernel, xs, ts, layers), outs, [me], [wq, wu])
    blocks = []
    at = 0
    for _ in range(layers):
        q, u = {}, {}
        for s in slots_of(xs):
            q[s], u[s] = got[at], got[at + 1]
            at += 2
        blocks.append((q, u))
    return blocks


def place_kernel(hs, ts, xs, me, *refs):
    out = refs[-1]
    at = 0
    for kh in range(hs):
        h = lax.rem(me[0] - kh + hs, hs)
        for kb in range(ts):
            b = lax.rem(me[3] - kb + ts, ts)
            if xs is None:
                out[h, b] = refs[at][...]
                at += 1
            else:
                for k, dc in slots_of(xs):
                    out[h, lo_minus(me, xs, k, dc), b] = refs[at][...]
                    at += 1


def place(me, pieces, hs, ts, xs):
    arrays = []
    for kh in range(hs):
        for kb in range(ts):
            if xs is None:
                arrays.append(pieces[kh, kb])
            else:
                arrays += [pieces[kh, kb][s] for s in slots_of(xs)]
    rows, cols = arrays[0].shape
    lead = (hs, ts) if xs is None else (hs, ts, ts)
    (out,) = run(
        functools.partial(place_kernel, hs, ts, xs), [shape(lead + (rows, cols), BF)], [me], arrays
    )
    return out.reshape(-1, cols)


def attn_fwd_kernel(ts, xs, heads, me, slopes, *refs):
    normed = refs[:ts]
    w, bias, seg_row, seg_col, qkv, out_t, lse = refs[ts : ts + 7]
    outs = refs[ts + 7 :]
    n = normed[0].shape[0]
    width = heads * HEAD_DIM
    for j, (k, dc) in enumerate(slots_of(xs)):
        lo = lo_minus(me, xs, k, dc)
        got = nn(normed[j][...], w[...]) + bias[...]
        qkv[pl.ds(pl.multiple_of(lo * n, n), n), :] = got.astype(BF)
    scale = HEAD_DIM ** (-0.5)
    for i in range(ts):
        length = (i + 1) * n
        key_at = lax.broadcasted_iota(jnp.int32, (length, n), 0)
        query_at = lax.broadcasted_iota(jnp.int32, (length, n), 1) + i * n
        allowed = (seg_col[:length, :] == seg_row[:, i * n : length]) & (key_at <= query_at)
        distance = (query_at - key_at).astype(F32)
        for h in range(heads):
            here = h * HEAD_DIM
            q = qkv[i * n : length, here : here + HEAD_DIM]
            keys = qkv[:length, width + here : width + here + HEAD_DIM]
            values = qkv[:length, 2 * width + here : 2 * width + here + HEAD_DIM]
            s = nt(keys, q) * scale - slopes[h] * distance
            s = jnp.where(allowed, s, masked_score)
            top = jnp.max(s, axis=0, keepdims=True)
            p = jnp.exp(s - top)
            total = jnp.sum(p, axis=0, keepdims=True)
            out_t[here : here + HEAD_DIM, i * n : length] = tn(values, p.astype(BF)) / total
            lse[h : h + 1, i * n : length] = top + jnp.log(total)
    for j, (k, dc) in enumerate(slots_of(xs)):
        off = pl.multiple_of(lo_minus(me, xs, k, dc) * n, n)
        outs[j][...] = out_t[:, pl.ds(off, n)].T.astype(BF)


def attn_fwd(me, slopes, normed, w, bias, seg_row, seg_col, xs):
    ts = len(normed)
    heads = slopes.shape[0]
    n = normed[0].shape[0]
    length, width = ts * n, heads * HEAD_DIM
    got = run(
        functools.partial(attn_fwd_kernel, ts, xs, heads),
        [shape((length, 3 * width), BF), shape((width, length), F32), shape((heads, length), F32)]
        + [shape((n, width), BF)] * ts,
        [me, slopes],
        normed + [w, bias, seg_row, seg_col],
        flops=2 * length * D * 3 * width + 3 * length * length * width,
    )
    return got[0], got[1], got[2], list(got[3:])


def attn_bwd_kernel(ts, xs, heads, me, slopes, *refs):
    grads = refs[:ts]
    qkv, out_t, lse, w, seg_row, seg_col = refs[ts : ts + 6]
    parts = refs[ts + 6 : 2 * ts + 6]
    souts = refs[2 * ts + 6 : 3 * ts + 6]
    gbuf, dq_buf, dk_buf, dv_buf = refs[3 * ts + 6 :]
    n = grads[0].shape[0]
    width = heads * HEAD_DIM
    scale = HEAD_DIM ** (-0.5)
    for j, (k, dc) in enumerate(slots_of(xs)):
        off = pl.multiple_of(lo_minus(me, xs, k, dc) * n, n)
        gbuf[pl.ds(off, n), :] = grads[j][...]
    dk_buf[...] = jnp.zeros_like(dk_buf)
    dv_buf[...] = jnp.zeros_like(dv_buf)
    for i in range(ts):
        length = (i + 1) * n
        key_at = lax.broadcasted_iota(jnp.int32, (length, n), 0)
        query_at = lax.broadcasted_iota(jnp.int32, (length, n), 1) + i * n
        allowed = (seg_col[:length, :] == seg_row[:, i * n : length]) & (key_at <= query_at)
        distance = (query_at - key_at).astype(F32)
        for h in range(heads):
            here = h * HEAD_DIM
            q = qkv[i * n : length, here : here + HEAD_DIM]
            keys = qkv[:length, width + here : width + here + HEAD_DIM]
            values = qkv[:length, 2 * width + here : 2 * width + here + HEAD_DIM]
            g = gbuf[i * n : length, here : here + HEAD_DIM]
            delta = jnp.sum(
                g.astype(F32).T * out_t[here : here + HEAD_DIM, i * n : length], axis=0, keepdims=True
            )
            s = nt(keys, q) * scale - slopes[h] * distance
            p = jnp.where(allowed, jnp.exp(s - lse[h : h + 1, i * n : length]), 0.0)
            ds = (p * (nt(values, g) - delta)).astype(BF)
            dq_buf[i * n : length, here : here + HEAD_DIM] = tn(ds, keys) * scale
            dk_buf[:length, here : here + HEAD_DIM] += nn(ds, q)
            dv_buf[:length, here : here + HEAD_DIM] += nn(p.astype(BF), g)
    for j, (k, dc) in enumerate(slots_of(xs)):
        off = pl.multiple_of(lo_minus(me, xs, k, dc) * n, n)
        rows = pl.ds(off, n)
        parts[j][:, :width] = dq_buf[rows, :].astype(BF)
        parts[j][:, width : 2 * width] = (dk_buf[rows, :] * scale).astype(BF)
        parts[j][:, 2 * width :] = dv_buf[rows, :].astype(BF)
        souts[j][...] = nt(parts[j][...], w[...]).astype(souts[j].dtype)


def attn_bwd(me, slopes, grads, qkv, out_t, lse, w, seg_row, seg_col, xs):
    ts = len(grads)
    heads = slopes.shape[0]
    n = grads[0].shape[0]
    length, width = ts * n, heads * HEAD_DIM
    got = run(
        functools.partial(attn_bwd_kernel, ts, xs, heads),
        [shape((n, 3 * width), BF)] * ts + [shape((n, D), F32)] + [shape((n, D), BF)] * (ts - 1),
        [me, slopes],
        grads + [qkv, out_t, lse, w, seg_row, seg_col],
        scratch=[pltpu.VMEM((length, width), BF)] + [pltpu.VMEM((length, width), F32)] * 3,
        flops=2 * length * D * 3 * width + 6 * length * length * width,
    )
    return list(got[:ts]), list(got[ts:])


def out_kernel(ts, xs, me, *refs):
    heads = refs[:ts]
    w, bias, stream, gain, shft, middle, normed = refs[ts:]
    width = heads[0].shape[1]
    total = stream[...] + bias[...]
    for j, (k, dc) in enumerate(slots_of(xs)):
        off = pl.multiple_of(lo_plus(me, xs, k, dc) * width, width)
        total = total + nn(heads[j][...], w[pl.ds(off, width), :])
    middle[...] = total
    unit, _ = norm_parts(total)
    normed[...] = (unit * gain[...] + shft[...]).astype(BF)


def out_project(me, heads, w, bias, stream, gain, shft, xs):
    n = stream.shape[0]
    return run(
        functools.partial(out_kernel, len(heads), xs),
        [shape((n, D), F32), shape((n, D), BF)],
        [me],
        heads + [w, bias, stream, gain, shft],
        flops=2 * n * D * D,
    )


def ffn_fwd_kernel(count, *refs):
    normed = refs[:count]
    up, bias, down = refs[count : count + 3]
    outs = refs[count + 3 :]
    root, cubic = 0.7978845608028654, 0.044715
    for j in range(count):
        hidden, slope, part = outs[3 * j : 3 * j + 3]
        u = nn(normed[j][...], up[...]) + bias[...]
        square = u * u
        t = jnp.tanh(root * (u + cubic * square * u))
        half = 0.5 * (1.0 + t)
        hidden[...] = (u * half).astype(BF)
        slope[...] = (half + 0.5 * u * (1.0 - t * t) * (root * (1.0 + 3.0 * cubic * square))).astype(BF)
        part[...] = nn(hidden[...], down[...]).astype(part.dtype)


def ffn_fwd(normed, up, bias, down, kinds):
    n = normed[0].shape[0]
    wide = up.shape[1]
    outs = []
    for kind in kinds:
        outs += [shape((n, wide), BF), shape((n, wide), BF), shape((n, D), kind)]
    got = run(
        functools.partial(ffn_fwd_kernel, len(normed)),
        outs,
        [],
        normed + [up, bias, down],
        flops=4 * n * D * wide * len(normed),
    )
    return list(got[0::3]), list(got[1::3]), list(got[2::3])


def ffn_bwd_kernel(count, *refs):
    grads, slopes = refs[:count], refs[count : 2 * count]
    up, down = refs[2 * count : 2 * count + 2]
    outs = refs[2 * count + 2 :]
    for j in range(count):
        du, part = outs[2 * j : 2 * j + 2]
        du[...] = (nt(grads[j][...], down[...]) * slopes[j][...].astype(F32)).astype(BF)
        part[...] = nt(du[...], up[...]).astype(part.dtype)


def ffn_bwd(grads, slopes, up, down, kinds):
    n = grads[0].shape[0]
    wide = up.shape[1]
    outs = []
    for kind in kinds:
        outs += [shape((n, wide), BF), shape((n, D), kind)]
    got = run(
        functools.partial(ffn_bwd_kernel, len(grads)),
        outs,
        [],
        grads + slopes + [up, down],
        flops=4 * n * D * wide * len(grads),
    )
    return list(got[0::2]), list(got[1::2])


def end_kernel(count, last, *refs):
    terms = refs[:count]
    middle, bias = refs[count : count + 2]
    total = middle[...] + bias[...]
    for t in terms:
        total = total + t[...].astype(F32)
    if last:
        refs[-1][...] = total.astype(BF)
        return
    gain, shft, stream, normed = refs[count + 2 :]
    stream[...] = total
    unit, _ = norm_parts(total)
    normed[...] = (unit * gain[...] + shft[...]).astype(BF)


def layer_end(terms, middle, bias, norm):
    n = middle.shape[0]
    outs = [shape((n, D), BF)] if norm is None else [shape((n, D), F32), shape((n, D), BF)]
    return run(
        functools.partial(end_kernel, len(terms), norm is None),
        outs,
        [],
        terms + [middle, bias] + ([] if norm is None else list(norm)),
    )


def norm_back(values, gain, grad):
    unit, rstd = norm_parts(values)
    scaled = grad * gain
    lead = jnp.mean(scaled, axis=-1, keepdims=True)
    along = jnp.mean(scaled * unit, axis=-1, keepdims=True)
    back = rstd * (scaled - lead - unit * along)
    return back, jnp.sum(grad * unit, axis=0, keepdims=True), jnp.sum(grad, axis=0, keepdims=True)


def mid_back_kernel(count, ts, xs, me, *refs):
    terms = refs[:count]
    grad, middle, gain, w = refs[count : count + 4]
    dh, dy, sums = refs[count + 4 : count + 7]
    outs = refs[count + 7 :]
    total = terms[0][...].astype(F32)
    for t in terms[1:]:
        total = total + t[...].astype(F32)
    back, gains, shifts = norm_back(middle[...], gain[...], total)
    now = grad[...].astype(F32) + back
    dh[...] = now
    dy[...] = now.astype(BF)
    sums[0:1, :] = gains
    sums[1:2, :] = shifts
    sums[2:3, :] = jnp.sum(dy[...].astype(F32), axis=0, keepdims=True)
    width = outs[0].shape[1]
    for j, (k, dc) in enumerate(slots_of(xs)):
        off = pl.multiple_of(lo_plus(me, xs, k, dc) * width, width)
        outs[j][...] = nt(dy[...], w[pl.ds(off, width), :]).astype(BF)


def mid_back(me, terms, grad, middle, gain, w, ts, xs):
    n = middle.shape[0]
    got = run(
        functools.partial(mid_back_kernel, len(terms), ts, xs),
        [shape((n, D), F32), shape((n, D), BF), shape((3, D), F32)] + [shape((n, D // ts), BF)] * ts,
        [me],
        terms + [grad, middle, gain, w],
        flops=2 * n * D * D,
    )
    return got[0], got[1], got[2], list(got[3:])


def start_back_kernel(count, *refs):
    terms = refs[:count]
    grad, stream, gain, dh, dz, sums = refs[count:]
    total = terms[0][...].astype(F32)
    for t in terms[1:]:
        total = total + t[...].astype(F32)
    back, gains, shifts = norm_back(stream[...], gain[...], total)
    now = grad[...] + back
    dh[...] = now
    dz[...] = now.astype(BF)
    sums[0:1, :] = gains
    sums[1:2, :] = shifts
    sums[2:3, :] = jnp.sum(dz[...].astype(F32), axis=0, keepdims=True)


def start_back(terms, grad, stream, gain):
    n = stream.shape[0]
    return run(
        functools.partial(start_back_kernel, len(terms)),
        [shape((n, D), F32), shape((n, D), BF), shape((3, D), F32)],
        [],
        terms + [grad, stream, gain],
    )


def wgrad_cols_kernel(ts, xs, hs, rows, me, *refs):
    left, right = refs[:ts], refs[ts : 2 * ts]
    sums = refs[2 * ts]
    outs = refs[2 * ts + 1 :]
    total = jnp.sum(right[0][...].astype(F32), axis=0, keepdims=True)
    for b in right[1:]:
        total = total + jnp.sum(b[...].astype(F32), axis=0, keepdims=True)
    sums[...] = total
    tile = CORES * ts * rows
    for kh in list(range(1, hs)) + [0]:
        h = lax.rem(me[0] + kh, hs)
        for k in range(xs):
            place_at = (h * ts + lax.rem(me[1] + k, xs) * CORES) * ts * rows
            cols = pl.ds(pl.multiple_of(place_at, tile), tile)
            got = tn(left[0][:, cols], right[0][...])
            for j in range(1, ts):
                got = got + tn(left[j][:, cols], right[j][...])
            for c in range(CORES):
                dc = lax.rem(me[2] + c, CORES)
                for b in range(ts):
                    kb = lax.rem(b - me[3] + ts, ts)
                    at = (c * ts + b) * rows
                    outs[kh][kb, dc, k] = got[at : at + rows, :].astype(BF)


def wgrad_cols(me, left, right, hs, xs):
    ts = len(left)
    rows = D // (hs * ts * ts)
    n, wide = right[0].shape
    got = run(
        functools.partial(wgrad_cols_kernel, ts, xs, hs, rows),
        [shape((1, wide), F32)] + [shape((ts, CORES, xs, rows, wide), BF)] * hs,
        [me],
        left + right,
        flops=2 * ts * n * D * wide,
    )
    return got[0], list(got[1:])


def wgrad_rows_kernel(ts, hs, rows, me, *refs):
    left, right = refs[:ts], refs[ts : 2 * ts]
    outs = refs[2 * ts :]
    group = min(ts, max(1, 256 // rows))
    for kh in list(range(1, hs)) + [0]:
        h = lax.rem(me[0] + kh, hs)
        for first in range(0, ts, group):
            cols = pl.ds(pl.multiple_of((h * ts + first) * rows, group * rows), group * rows)
            got = tn(left[0][:, cols], right[0][...])
            for j in range(1, ts):
                got = got + tn(left[j][:, cols], right[j][...])
            for b in range(group):
                kb = lax.rem(first + b - me[3] + ts, ts)
                outs[kh][kb] = got[b * rows : (b + 1) * rows, :].astype(BF)


def wgrad_rows(me, left, right, hs):
    ts = len(left)
    n, wide = left[0].shape
    rows = wide // (hs * ts)
    return list(
        run(
            functools.partial(wgrad_rows_kernel, ts, hs, rows),
            [shape((ts, rows, D), BF)] * hs,
            [me],
            left + right,
            flops=2 * ts * n * D * wide,
        )
    )


def wgrad_out_kernel(ts, xs, hs, rows, me, *refs):
    left = refs[:ts]
    right, out = refs[ts], refs[ts + 1]
    width = left[0].shape[1]
    for j, (k, dc) in enumerate(slots_of(xs)):
        got = tn(left[j][...], right[...])
        first = lo_plus(me, xs, k, dc) * (width // rows)
        for g in range(width // rows):
            i = first + g
            h = lax.div(i, ts * ts)
            lo = lax.rem(lax.div(i, ts), ts)
            b = lax.rem(i, ts)
            kk = lax.rem(lax.div(lo, CORES) - me[1] + xs, xs)
            dd = lax.rem(lax.rem(lo, CORES) + me[2], CORES)
            kh = lax.rem(h - me[0] + hs, hs)
            kb = lax.rem(b - me[3] + ts, ts)
            out[dd, kk, kh, kb] = got[g * rows : (g + 1) * rows, :].astype(BF)


def wgrad_out(me, left, right, hs, xs):
    ts = len(left)
    rows = D // (hs * ts * ts)
    (got,) = run(
        functools.partial(wgrad_out_kernel, ts, xs, hs, rows),
        [shape((CORES, xs, hs, ts, rows, D), BF)],
        [me],
        left + [right],
        flops=2 * right.shape[0] * D * D,
    )
    return got


def join_kernel(ts, xs, layers, me, *refs):
    out_q, out_u = refs[-2:]
    at = 0
    for layer in range(layers):
        for k, dc in slots_of(xs):
            lo = lo_minus(me, xs, k, dc)
            q, u = refs[at], refs[at + 1]
            at += 2
            wide = q.shape[1] // 3
            for j in range(3):
                off = pl.multiple_of(j * D + lo * wide, 128)
                out_q[layer, :, pl.ds(off, wide)] = q[:, j * wide : (j + 1) * wide].astype(F32)
            chunk = u.shape[1] // 2
            for j in range(2):
                off = pl.multiple_of(j * (chunk * ts) + lo * chunk, 128)
                out_u[layer, :, pl.ds(off, chunk)] = u[:, j * chunk : (j + 1) * chunk].astype(F32)


def join(me, grads, ts, xs):
    layers = len(grads)
    arrays = []
    for q, u in grads:
        for s in slots_of(xs):
            arrays += [q[s], u[s]]
    rows = arrays[0].shape[0]
    return run(
        functools.partial(join_kernel, ts, xs, layers),
        [shape((layers, rows, arrays[0].shape[1] * ts), F32), shape((layers, rows, arrays[1].shape[1] * ts), F32)],
        [me],
        arrays,
    )


def gather_params(flat, index, hs, ts, xs):
    count = hs * ts * ts
    parts = [flat] + [shift(flat, BLK, ts, kb) for kb in range(1, ts)]
    stack = jnp.concatenate(parts, 0)
    stack = jnp.concatenate([stack] + [shift(stack, HI, hs, kh) for kh in range(1, hs)], 0)
    stack = jnp.concatenate([stack] + [shift(stack, XX, xs, k) for k in range(1, xs)], 0)
    stack = jnp.concatenate([stack, shift(stack, CORE, CORES, 1)], 0)
    hi, xx, core, blk = index
    dc, k, kh, kb = jnp.meshgrid(
        jnp.arange(CORES), jnp.arange(xs), jnp.arange(hs), jnp.arange(ts), indexing="ij"
    )
    lo = lax.rem(xx - k + xs, xs) * CORES + lax.rem(core + dc, CORES)
    owner = (lax.rem(hi - kh + hs, hs) * ts + lo) * ts + lax.rem(blk - kb + ts, ts)
    pick = (jnp.arange(count)[:, None] == owner.reshape(1, -1)).astype(BF)
    return jnp.dot(pick, stack, preferred_element_type=F32)


def sum_small(mine, shared, hs, ts, xs):
    mine = mine + shift(mine, CORE, CORES, 1)
    for_all = mine
    for k in range(1, xs):
        for_all = for_all + shift(mine, XX, xs, k)
    both = jnp.concatenate([for_all, shared], 0)
    total = both
    for kh in range(1, hs):
        total = total + shift(both, HI, hs, kh)
    out = total
    for kb in range(1, ts):
        out = out + shift(total, BLK, ts, kb)
    return out


def on_device(
    hs,
    ts,
    xs,
    tokens,
    segment_ids,
    out_grad,
    qkv_weight,
    qv_bias,
    out_weight,
    out_bias,
    up_weight,
    up_bias,
    down_weight,
    down_bias,
    norm_gain,
    norm_shift,
):
    layers = qkv_weight.shape[0]
    n = tokens.shape[1]
    length = ts * n
    heads = HEADS // ts
    index = tuple(lax.axis_index(a) for a in (HI, XX, CORE, BLK))
    hi, xx, core, blk = index
    lo = xx * CORES + core
    me = jnp.stack(index).astype(jnp.int32)
    slots = slots_of(xs)
    turn = [(a * ts + b, b * ts + a) for a in range(ts) for b in range(ts)]
    turned = lambda x: lax.ppermute(x, (XX, CORE, BLK), turn)

    tokens_own = turned(tokens[0])
    segments_own = turned(segment_ids)
    grad_own = turned(out_grad[0])

    flat = jnp.concatenate(
        [
            jnp.concatenate(
                [qv_bias[l], out_bias[l], up_bias[l], down_bias[l], norm_gain[l].reshape(-1), norm_shift[l].reshape(-1)]
            )
            for l in range(layers)
        ]
    )[None]
    params = gather_params(flat, index, hs, ts, xs)
    per = flat.shape[1] // layers
    sizes = [qv_bias.shape[1], out_bias.shape[1], up_bias.shape[1], down_bias.shape[1]] + [out_bias.shape[1]] * 4
    small = []
    for l in range(layers):
        at, fields = l * per, []
        for s in sizes:
            fields.append(params[:, at : at + s])
            at += s
        qv = lax.dynamic_index_in_dim(fields[0].reshape(2, ts, -1), lo, 1, False)
        up = lax.dynamic_index_in_dim(fields[2].reshape(hs, ts, -1), lo, 1, False)
        row = lambda x: x.reshape(1, -1)
        small.append(
            dict(
                qkv=row(jnp.concatenate([qv[0], jnp.zeros_like(qv[0]), qv[1]])),
                up=row(up),
                out=row(fields[1]),
                down=row(fields[3]),
                gains=[row(fields[4]), row(fields[5])],
                shifts=[row(fields[6]), row(fields[7])],
            )
        )

    cuts = cut(me, qkv_weight, up_weight, xs, ts)

    def fetch_cols(blocks):
        mine = exchange_lo(blocks, xs, 1)
        mine = jnp.stack([mine[s] for s in slots])
        got = gather_hb(mine, hs, ts)
        pieces = {key: {s: got[key][j] for j, s in enumerate(slots)} for key in got}
        return place(me, pieces, hs, ts, xs)

    def fetch_rows(block):
        return place(me, gather_hb(block, hs, ts), hs, ts, None)

    def fetch_out(block):
        got = gather_hb(block, hs, ts)
        mine = jnp.stack([got[kh, kb] for kh in range(hs) for kb in range(ts)])
        group = gather_lo(mine, xs)
        pieces = {
            (kh, kb): {s: group[s][kh * ts + kb] for s in slots} for kh in range(hs) for kb in range(ts)
        }
        return place(me, pieces, hs, ts, xs)

    weights = []
    for l in range(layers):
        weights.append(
            dict(
                qkv=fetch_cols(cuts[l][0]),
                out=fetch_out(out_weight[l]),
                up=fetch_cols(cuts[l][1]),
                down=fetch_rows(down_weight[l]),
            )
        )

    seg_by = gather_lo(segments_own, xs)
    seg = jnp.zeros((ts, n), jnp.int32)
    for s in slots:
        seg = lax.dynamic_update_slice(seg, seg_by[s], (lo_minus(me, xs, *s), 0))
    seg_row, seg_col = seg.reshape(1, length), seg.reshape(length, 1)
    slopes = jnp.exp2(-8.0 * (lo * heads + jnp.arange(heads, dtype=F32) + 1.0) / HEADS)

    stream, normed = entry(tokens_own, small[0]["gains"][0], small[0]["shifts"][0])
    stored = []
    for l in range(layers):
        w, sm = weights[l], small[l]
        by = gather_lo(normed, xs)
        all_one = [by[s] for s in slots]
        qkv, out_t, lse, heads_by = attn_fwd(me, slopes, all_one, w["qkv"], sm["qkv"], seg_row, seg_col, xs)
        own = exchange_lo({s: heads_by[j] for j, s in enumerate(slots)}, xs, -1)
        own = [own[s] for s in slots]
        middle, normed_two = out_project(
            me, own, w["out"], sm["out"], stream, sm["gains"][1], sm["shifts"][1], xs
        )
        by = gather_lo(normed_two, xs)
        all_two = [by[s] for s in slots]
        near, far = all_two[:CORES], all_two[CORES:]
        hid_a, gel_a, part_a = ffn_fwd(near, w["up"], sm["up"], w["down"], [F32] + [BF] * (CORES - 1))
        hid_b, gel_b, part_b = ffn_fwd(far, w["up"], sm["up"], w["down"], [BF] * len(far))
        part = dict(zip(slots, part_a + part_b))
        terms = scatter_lo(part, xs)
        stored.append((stream, all_one, qkv, out_t, lse, own, middle, all_two, hid_a + hid_b, gel_a + gel_b))
        if l + 1 < layers:
            stream, normed = layer_end(
                terms, middle, sm["down"], (small[l + 1]["gains"][0], small[l + 1]["shifts"][0])
            )
        else:
            (final,) = layer_end(terms, middle, sm["down"], None)
    result = turned(final)

    dh, dz = grad_own, grad_own
    down_sum = jnp.sum(grad_own.astype(F32), axis=0, keepdims=True)
    mine_sums, shared_sums = [None] * layers, [None] * layers
    q_grads, u_grads, d_grads, o_grads = [[None] * layers for _ in range(4)]

    def reduce_cols(by_hi):
        terms = scatter_hb(by_hi, hs, ts)
        blocks = {}
        for k, dc in slots:
            total = terms[0][dc, k]
            for t in terms[1:]:
                total = total + t[dc, k].astype(F32)
            blocks[k, dc] = total.astype(BF)
        return exchange_lo(blocks, xs, 1)

    def reduce_rows(by_hi):
        terms = scatter_hb(by_hi, hs, ts)
        total = terms[0]
        for t in terms[1:]:
            total = total + t.astype(F32)
        return total

    def reduce_out(g):
        got = shift(g[1], CORE, CORES, 1)
        both = [g[0, k].astype(F32) + got[k].astype(F32) for k in range(xs)]
        total = both[0]
        for k in range(1, xs):
            total = total + shift(both[k].astype(BF), XX, xs, k).astype(F32)
        by_hi = [total[0]] + [total[kh].astype(BF) for kh in range(1, hs)]
        return reduce_rows(by_hi)

    for l in reversed(range(layers)):
        w, sm = weights[l], small[l]
        stream, all_one, qkv, out_t, lse, own, middle, all_two, hidden, gel = stored[l]
        by = gather_lo(dz, xs)
        all_dz = [by[s] for s in slots]
        du_a, part_a = ffn_bwd(all_dz[:CORES], gel[:CORES], w["up"], w["down"], [F32] + [BF] * (CORES - 1))
        du_b, part_b = ffn_bwd(all_dz[CORES:], gel[CORES:], w["up"], w["down"], [BF] * (ts - CORES))
        all_du = du_a + du_b
        terms = scatter_lo(dict(zip(slots, part_a + part_b)), xs)
        d_grads[l] = reduce_rows(wgrad_rows(me, hidden, all_dz, hs))
        up_sum, up_parts = wgrad_cols(me, all_two, all_du, hs, xs)
        u_grads[l] = reduce_cols(up_parts)
        dh1, dy, mid_sums, d_heads = mid_back(me, terms, dh, middle, sm["gains"][1], w["out"], ts, xs)
        by = exchange_lo(dict(zip(slots, d_heads)), xs, 1)
        d_out = [by[s] for s in slots]
        o_grads[l] = reduce_out(wgrad_out(me, own, dy, hs, xs))
        dqkv, parts = attn_bwd(me, slopes, d_out, qkv, out_t, lse, w["qkv"], seg_row, seg_col, xs)
        terms = scatter_lo(dict(zip(slots, parts)), xs)
        qkv_sum, qkv_parts = wgrad_cols(me, all_one, dqkv, hs, xs)
        q_grads[l] = reduce_cols(qkv_parts)
        dh, dz, start_sums = start_back(terms, dh1, stream, sm["gains"][0])
        mine_sums[l] = jnp.concatenate([down_sum, mid_sums, start_sums[:2]], 0)
        width = qkv_sum.shape[1] // 3
        shared_sums[l] = (up_sum, qkv_sum[:, :width], qkv_sum[:, 2 * width :])
        down_sum = start_sums[2:3]
    input_grad = turned(dz)

    wide = max(D, shared_sums[0][0].shape[1])
    rows = []
    for l in range(layers):
        up_sum, q_sum, v_sum = shared_sums[l]
        rows.append(jnp.pad(up_sum, ((0, 0), (0, wide - up_sum.shape[1]))))
        qv = jnp.concatenate([q_sum, v_sum], 1)
        rows.append(jnp.pad(qv, ((0, 0), (0, wide - qv.shape[1]))))
    sums = sum_small(jnp.concatenate(mine_sums, 0), jnp.concatenate(rows, 0), hs, ts, xs)
    device = (hi * ts + lo) * ts + blk
    each = out_bias.shape[1]
    vectors = lax.dynamic_slice(sums[: 6 * layers, :D], (0, device * each), (6 * layers, each))
    vectors = vectors.reshape(layers, 6, each)
    shared = sums[6 * layers :].reshape(layers, 2, wide)
    up_each, qv_each = up_bias.shape[1], qv_bias.shape[1]
    up_grad = lax.dynamic_slice(shared[:, 0], (0, (hi * ts + blk) * up_each), (layers, up_each))
    qv_grad = lax.dynamic_slice(shared[:, 1], (0, (hi * ts + blk) * qv_each), (layers, qv_each))
    q_grad, u_grad = join(me, list(zip(q_grads, u_grads)), ts, xs)
    return (
        result[None],
        input_grad[None],
        q_grad,
        qv_grad,
        jnp.stack(o_grads),
        vectors[:, 3],
        u_grad,
        up_grad,
        jnp.stack(d_grads),
        vectors[:, 0],
        jnp.stack([vectors[:, 4], vectors[:, 1]], 1),
        jnp.stack([vectors[:, 5], vectors[:, 2]], 1),
    )


def solution(mesh):
    ts = mesh.shape["blk"]
    hs = mesh.shape["rows"] // ts
    xs = ts // CORES
    fine = Mesh(mesh.devices.reshape(hs, xs, CORES, ts), (HI, XX, CORE, BLK))
    rows, every = (HI, XX, CORE), (HI, XX, CORE, BLK)
    row_cut = P(None, every, None)
    vec_cut = P(None, every)
    norm_cut = P(None, None, every)
    cuts = (row_cut, vec_cut, row_cut, vec_cut, row_cut, vec_cut, row_cut, vec_cut, norm_cut, norm_cut)
    acts = P(rows, BLK, None)
    return jax.shard_map(
        functools.partial(on_device, hs, ts, xs),
        mesh=fine,
        in_specs=(acts, P(rows, BLK), acts) + cuts,
        out_specs=(acts, acts) + cuts,
        check_vma=False,
    )
```

```python
import functools

import jax
import jax.numpy as jnp
from jax import lax
from jax.experimental import pallas as pl
from jax.experimental.pallas import tpu as pltpu
from jax.sharding import Mesh
from jax.sharding import PartitionSpec as P

D = 1024
HEADS = 8
HEAD_DIM = 128
CORES = 2
norm_eps = 1e-05
masked_score = -1e30
BF = jnp.bfloat16
F32 = jnp.float32
TILE = 16
VMEM_BYTES = 32 * 1024 * 1024

HI, XX, CORE, BLK = "hi", "xx", "core", "blk"


def nn(a, b):
    return lax.dot_general(a, b, (((1,), (0,)), ((), ())), preferred_element_type=F32)


def nt(a, b):
    return lax.dot_general(a, b, (((1,), (1,)), ((), ())), preferred_element_type=F32)


def tn(a, b):
    return lax.dot_general(a, b, (((0,), (0,)), ((), ())), preferred_element_type=F32)


def shape(dims, dtype):
    return jax.ShapeDtypeStruct(tuple(dims), dtype)


def run(kernel, outs, smem, arrays, scratch=(), flops=0, trans=0):
    size = lambda s: s.size * s.dtype.itemsize
    moved = sum(size(a) for a in arrays) + sum(size(o) for o in outs)
    return pl.pallas_call(
        kernel,
        out_shape=tuple(outs),
        in_specs=[pl.BlockSpec(memory_space=pltpu.SMEM)] * len(smem)
        + [pl.BlockSpec(memory_space=pltpu.VMEM)] * len(arrays),
        out_specs=tuple(pl.BlockSpec(memory_space=pltpu.VMEM) for _ in outs),
        scratch_shapes=list(scratch),
        compiler_params=pltpu.CompilerParams(vmem_limit_bytes=VMEM_BYTES),
        cost_estimate=pl.CostEstimate(flops=flops, bytes_accessed=moved, transcendentals=trans),
    )(*smem, *arrays)


def slots_of(xs):
    return [(k, dc) for k in range(xs) for dc in range(CORES)]


def lo_minus(me, xs, k, dc):
    return lax.rem(me[1] - k + xs, xs) * CORES + lax.rem(me[2] + dc, CORES)


def lo_plus(me, xs, k, dc):
    return lax.rem(me[1] + k, xs) * CORES + lax.rem(me[2] + dc, CORES)


def block_minus(me, xs, k, dc):
    return lax.rem(me[2] + dc, CORES) * xs + lax.rem(me[1] - k + xs, xs)


def tie(x, *after):
    return lax.optimization_barrier((x, after))[0]


def shift(x, axis, size, step):
    return lax.ppermute(x, axis, [(i, (i + step) % size) for i in range(size)])


def gather_lo(x, xs):
    out = {}
    for k in range(xs):
        out[k, 0] = x if k == 0 else shift(x, XX, xs, k)
    for k in range(xs):
        out[k, 1] = shift(out[k, 0], CORE, CORES, 1)
    return out


def scatter_lo(parts, xs):
    got = {}
    for k in list(range(1, xs)) + [0]:
        got[k] = shift(parts[k, 1].astype(BF), CORE, CORES, 1)
    terms = [parts[0, 0]]
    for k in range(1, xs):
        both = (parts[k, 0].astype(F32) + got[k].astype(F32)).astype(BF)
        terms.append(shift(both, XX, xs, -k))
    return terms + [got[0]]


def send_lo(x, xs, k, dc):
    if k == 0 and dc == 0:
        return x
    pairs = [
        (a * CORES + c, ((a + k) % xs) * CORES + (c + dc) % CORES) for a in range(xs) for c in range(CORES)
    ]
    return lax.ppermute(x, (XX, CORE), pairs)


def exchange_lo(blocks, xs, sign):
    order = [s for s in slots_of(xs) if s[0]] + [s for s in slots_of(xs) if not s[0]]
    return {(k, dc): send_lo(blocks[k, dc], xs, sign * k, dc) for k, dc in order}


class Work:
    def __init__(self, steps):
        self.steps = steps
        next(steps)

    def step(self, *after):
        try:
            return self.steps.send(after)
        except StopIteration as end:
            return end.value


def fetch(x, out, hs, ts):
    out[0, 0] = way = x
    for kb in range(ts):
        came = way
        up = [shift(came, HI, hs, kh) for kh in range(1, hs)]
        if kb + 1 < ts:
            way = shift(came, BLK, ts, 1)
        after = yield came
        up, way = tie((up, way), after)
        for kh in range(1, hs):
            out[kh, kb] = up[kh - 1]
        if kb + 1 < ts:
            out[0, kb + 1] = way
    return up


def reduce(parts, out, hs, ts):
    got = [shift(parts[kh], HI, hs, kh) for kh in range(1, hs)]
    after = yield parts
    got = tie(got, after)
    total = []
    for kb in range(ts):
        block = parts[0][kb].astype(F32)
        for g in got:
            block = block + g[kb].astype(F32)
        total.append(block if kb == 0 else block.astype(BF))
    out.append(total[0])
    for kb in range(1, ts):
        way = shift(total[kb], BLK, ts, kb)
        after = yield total
        way = tie(way, after)
        out.append(way)
    return way


def pieces_of(out, hs, ts):
    return [out[kh, kb] for kh in range(hs) for kb in range(ts)]


def total_of(terms, at=slice(None)):
    total = terms[0][at].astype(F32)
    for t in terms[1:]:
        total = total + t[at].astype(F32)
    return total


def norm_parts(values):
    centre = values - jnp.mean(values, axis=-1, keepdims=True)
    spread = jnp.mean(centre * centre, axis=-1, keepdims=True)
    rstd = lax.rsqrt(spread + norm_eps)
    return centre * rstd, rstd


def near_kernel(xs, ts, each, me, wq, *refs):
    given, outs, line = refs[:6], refs[6:-9], refs[-9]
    weight, fields, sems = refs[-8], refs[-7:-1], refs[-1]
    copies = [pltpu.make_async_copy(wq.at[0], weight, sems.at[0])]
    for j in range(6):
        copies.append(pltpu.make_async_copy(given[j], fields[j], sems.at[j + 1]))
    for c in copies:
        c.start()
    line[...] = jnp.zeros_like(line)
    for c in copies:
        c.wait()
    layers, rows, _ = wq.shape
    for layer in range(layers):
        at = layer * each * 12
        for f in fields[:4]:
            wide = f.shape[1]
            line[0:1, at : at + wide] = f[layer : layer + 1, :].astype(F32)
            at += wide
        for f in fields[4:]:
            for j in range(2):
                line[0:1, at : at + each] = f[layer, j : j + 1, :].astype(F32)
                at += each
    small = line[...].astype(BF)
    chunk = outs[0].shape[1] // 3
    for out, (k, dc) in zip(outs, slots_of(xs)):
        lo = lo_plus(me, xs, k, dc)
        for j in range(3):
            off = pl.multiple_of((j * ts + lo) * chunk, 128)
            out[:rows, j * chunk : (j + 1) * chunk] = weight[:, pl.ds(off, chunk)]
        out[rows:, :] = small


def near_cuts_of(me, wq, fields, xs, ts):
    _, rows, full = wq.shape
    outs = [shape((rows + TILE, full // ts), BF)] * ts
    got = pl.pallas_call(
        functools.partial(near_kernel, xs, ts, fields[1].shape[1]),
        out_shape=tuple(outs),
        in_specs=[pl.BlockSpec(memory_space=pltpu.SMEM)] + [pl.BlockSpec(memory_space=pl.ANY)] * 7,
        out_specs=tuple(pl.BlockSpec(memory_space=pltpu.VMEM) for _ in outs),
        scratch_shapes=[pltpu.VMEM((TILE, full // ts), F32), pltpu.VMEM(wq.shape[1:], BF)]
        + [pltpu.VMEM(f.shape, BF) for f in fields]
        + [pltpu.SemaphoreType.DMA((7,))],
        compiler_params=pltpu.CompilerParams(vmem_limit_bytes=VMEM_BYTES),
    )(me, wq, *fields)
    return dict(zip(slots_of(xs), got))


def message_kernel(tok, ids, msg):
    n = tok.shape[0]
    msg[:n, :] = tok[...]
    high = ids[...] // 256
    below = jnp.concatenate([high, ids[...] - high * 256], 0).astype(F32)
    fill = jnp.concatenate([below, jnp.zeros((TILE - 2, n), F32)], 0)
    msg[n:, :] = jnp.zeros((TILE, D), BF)
    msg[n:, :n] = fill.astype(BF)


def message_of(tok, ids):
    (got,) = run(message_kernel, [shape((tok.shape[0] + TILE, D), BF)], [], [tok, ids])
    return got


def rest_kernel(xs, ts, me, wq, wu, *outs):
    layers = wq.shape[0]
    chunk = wq.shape[2] // (3 * ts)
    half = wu.shape[2] // (2 * ts)
    for rest, (k, dc) in zip(outs, slots_of(xs)):
        lo = lo_plus(me, xs, k, dc)
        at = 0
        for layer in range(layers):
            if layer:
                for j in range(3):
                    got = wq[layer, :, pl.ds(pl.multiple_of((j * ts + lo) * chunk, 128), chunk)]
                    rest[:, at : at + chunk] = got
                    at += chunk
            for j in range(2):
                got = wu[layer, :, pl.ds(pl.multiple_of((j * ts + lo) * half, 128), half)]
                rest[:, at : at + half] = got
                at += half


def rest_cuts_of(me, wq, wu, xs, ts):
    layers, rows, full = wu.shape
    wide = 3 * D // ts
    got = run(
        functools.partial(rest_kernel, xs, ts),
        [shape((rows, layers * (wide + full // ts) - wide), BF)] * ts,
        [me],
        [wq, wu],
    )
    return dict(zip(slots_of(xs), got))


def fold_in(out, block, at, cols):
    rows = block.shape[0]
    for p in range(block.shape[1] // cols):
        out[p * rows : (p + 1) * rows, at : at + cols] = block[:, p * cols : (p + 1) * cols]


def pack_first_kernel(count, rows, *refs):
    blocks, out_w, out = refs[:count], refs[count], refs[count + 1]
    wide = blocks[0].shape[1]
    for j, block in enumerate(blocks):
        out[j * rows : (j + 1) * rows, :wide] = block[:rows, :]
    fold_in(out, out_w.at[0], wide, out.shape[1] - wide)
    tail = jnp.concatenate([b[rows : rows + 1, :].astype(F32) for b in blocks], 0)
    tail = jnp.concatenate([tail, jnp.zeros((TILE - count, wide), F32)], 0)
    out[count * rows :, :wide] = tail.astype(BF)
    out[count * rows :, wide:] = jnp.zeros((TILE, out.shape[1] - wide), BF)


def pack_first(blocks, out_w):
    count = len(blocks)
    rows, wide = blocks[0].shape[0] - TILE, blocks[0].shape[1]
    (got,) = run(
        functools.partial(pack_first_kernel, count, rows),
        [shape((count * rows + TILE, wide + D // count), BF)],
        [],
        blocks + [out_w],
    )
    return got


def pack_rest_kernel(count, layers, wide, *refs):
    blocks, down, out_w = refs[:count], refs[count], refs[count + 1]
    outs = refs[count + 2 :]
    rows = blocks[0].shape[0]
    cols = outs[0].shape[1] // 2
    at = 0
    for layer in range(layers):
        if layer:
            attn = outs[2 * layer - 1]
            for j, block in enumerate(blocks):
                attn[j * rows : (j + 1) * rows, :wide] = block[:, at : at + wide]
            fold_in(attn, out_w.at[layer], wide, D // count)
            at += wide
        ffn = outs[2 * layer]
        for j, block in enumerate(blocks):
            ffn[j * rows : (j + 1) * rows, :cols] = block[:, at : at + cols]
        fold_in(ffn, down.at[layer], cols, cols)
        at += cols


def pack_rest(blocks, down, out_w, wide, cols):
    count = len(blocks)
    rows = blocks[0].shape[0]
    layers = down.shape[0]
    outs = []
    for layer in range(layers):
        if layer:
            outs.append(shape((count * rows, wide + D // count), BF))
        outs.append(shape((count * rows, 2 * cols), BF))
    return run(
        functools.partial(pack_rest_kernel, count, layers, wide), outs, [], blocks + [down, out_w]
    )


def params_kernel(hs, ts, xs, rows, layers, each, me, *refs):
    pieces = refs[: hs * ts]
    vec, up, qkv = refs[hs * ts :]
    count = hs * ts * ts
    values = jnp.concatenate([p[ts * rows : ts * rows + ts, : qkv.shape[1]].astype(F32) for p in pieces], 0).astype(BF)
    at = lax.broadcasted_iota(jnp.int32, (1, count), 1)
    kh, kb, slot = at // (ts * ts), (at // ts) % ts, at % ts
    k, dc = slot // CORES, slot % CORES
    h = lax.rem(me[0] - kh + hs, hs)
    l = lax.rem(me[1] - k + xs, xs) * CORES + lax.rem(me[2] + dc, CORES)
    b = lax.rem(me[3] - kb + ts, ts)
    owner = (h * ts + l) * ts + b
    pick = (lax.broadcasted_iota(jnp.int32, (count, count), 0) == owner).astype(BF)
    table = nn(pick, values).astype(BF)
    lo = me[1] * CORES + me[2]

    def spread(first, size, wide):
        tile = lax.broadcasted_iota(jnp.int32, (size, wide), 1) % size
        same = (tile == lax.broadcasted_iota(jnp.int32, (size, wide), 0)).astype(BF)
        return nn(table[:, first : first + size], same)

    def keep(x, mask):
        return jnp.sum(jnp.where(mask, x, 0.0), axis=0, keepdims=True)

    row = lambda wide: lax.broadcasted_iota(jnp.int32, (count, wide), 0)
    col = lambda wide: lax.broadcasted_iota(jnp.int32, (count, wide), 1)
    full = each * count
    own_up, own_q = full * up.shape[1] // D, qkv.shape[1] // 3
    for layer in range(layers):
        first = layer * each * 12
        member = row(own_q) // ts % ts == lo
        part = row(own_q) % ts == col(own_q) // (2 * each)
        half = row(own_q) // (ts * ts)
        q = spread(first, 2 * each, own_q)
        qkv[layer : layer + 1, :own_q] = keep(q, member & part & (half == 0))
        qkv[layer : layer + 1, own_q : 2 * own_q] = jnp.zeros((1, own_q), F32)
        qkv[layer : layer + 1, 2 * own_q :] = keep(q, member & part & (half == 1))
        first = first + 2 * each
        mine = col(full) // each == row(full)
        for f, skip in enumerate((0, 5, 6, 7, 8, 9)):
            vec[layer * 6 + f : layer * 6 + f + 1, :] = keep(spread(first + skip * each, each, full), mine)
        here = (row(own_up) // ts % ts == lo) & (
            (row(own_up) // (ts * ts)) * ts + row(own_up) % ts == col(own_up) // (4 * each)
        )
        up[layer : layer + 1, :] = keep(spread(first + each, 4 * each, own_up), here)


def params(me, pieces, rows, layers, each, own_up, own_q, hs, ts, xs):
    return run(
        functools.partial(params_kernel, hs, ts, xs, rows, layers, each),
        [shape((layers * 6, D), F32), shape((layers, own_up), F32), shape((layers, 3 * own_q), F32)],
        [me],
        pieces,
    )


def fold_out(piece, rows, at, cols, parts):
    return jnp.concatenate([piece[p * rows : (p + 1) * rows, at : at + cols] for p in range(parts)], 1)


def piece_at(refs, at, whole, hs, ts, me):
    kh, kb = at // ts, at % ts
    h = lax.rem(me[0] - kh + hs, hs)
    if whole:
        return refs[kh].at[kb], h, kb
    return refs[at], h, lax.rem(me[3] - kb + ts, ts)


def place_attn_kernel(hs, ts, xs, whole, with_out, me, *refs):
    qkv = refs[-2] if with_out else refs[-1]
    rows, wide = qkv.shape[3:]
    for at in range(hs * ts):
        piece, h, b = piece_at(refs, at, whole, hs, ts, me)
        for j, (k, dc) in enumerate(slots_of(xs)):
            qkv[h, lo_minus(me, xs, k, dc), b] = piece[j * rows : (j + 1) * rows, :wide]
        if with_out:
            out = refs[-1]
            cols = out.shape[3] // ts
            for p in range(ts):
                out[h, b, :, p * cols : (p + 1) * cols] = piece[p * rows : (p + 1) * rows, wide : wide + cols]


def place_attn(me, pieces, rows, hs, ts, xs, with_out):
    whole = len(pieces) == hs
    wide = 3 * D // ts
    got = run(
        functools.partial(place_attn_kernel, hs, ts, xs, whole, with_out),
        [shape((hs, ts, ts, rows, wide), BF)] + ([shape((hs, ts, rows, D), BF)] if with_out else []),
        [me],
        pieces,
    )
    return (got[0].reshape(D, wide),) + tuple(got[1:])


def place_ffn_kernel(hs, ts, xs, whole, me, *refs):
    up, down = refs[-2:]
    rows, cols = up.shape[3:]
    tall = down.shape[2]
    for at in range(hs * ts):
        piece, h, b = piece_at(refs, at, whole, hs, ts, me)
        for j, (k, dc) in enumerate(slots_of(xs)):
            up[h, lo_minus(me, xs, k, dc), b] = piece[j * rows : (j + 1) * rows, :cols]
        for p in range(D // cols):
            down[h, b, :, p * cols : (p + 1) * cols] = piece[p * tall : (p + 1) * tall, cols:]


def place_ffn(me, pieces, hs, ts, xs):
    whole = len(pieces) == hs
    tall, wide = pieces[0].shape[-2:]
    cols = wide // 2
    up, down = run(
        functools.partial(place_ffn_kernel, hs, ts, xs, whole),
        [shape((hs, ts, ts, tall // ts, cols), BF), shape((hs, ts, tall * cols // D, D), BF)],
        [me],
        pieces,
    )
    return up.reshape(D, cols), down.reshape(-1, D)


def place_out_kernel(hs, ts, xs, me, *refs):
    out = refs[-1]
    for j, (k, dc) in enumerate(slots_of(xs)):
        out[:, lo_minus(me, xs, k, dc)] = refs[j][...]


def place_out(me, group, hs, ts, xs):
    _, _, rows, wide = group[0].shape
    (got,) = run(
        functools.partial(place_out_kernel, hs, ts, xs), [shape((hs, ts, ts, rows, wide), BF)], [me], group
    )
    return got.reshape(-1, wide)


def attn_fwd_kernel(ts, xs, heads, raw, layer, me, slopes, *refs):
    given = refs[:ts]
    if raw:
        w, bias, vec = refs[ts : ts + 3]
        qkv, out_t, lse, seg_row, seg_col = refs[ts + 3 : ts + 8]
        outs, normed = refs[ts + 8 : 2 * ts + 8], refs[2 * ts + 8 : 3 * ts + 8]
    else:
        normed = given
        w, bias, seg_row, seg_col = refs[ts : ts + 4]
        qkv, out_t, lse = refs[ts + 4 : ts + 7]
        outs = refs[ts + 7 :]
    n = normed[0].shape[0]
    width = heads * HEAD_DIM
    for j, (k, dc) in enumerate(slots_of(xs)):
        off = pl.multiple_of(block_minus(me, xs, k, dc) * n, n)
        if raw:
            unit, _ = norm_parts(given[j][:n, :].astype(F32))
            normed[j][...] = (unit * vec[2:3, :] + vec[4:5, :]).astype(BF)
            ids = given[j][n : n + 8, :n].astype(F32)
            ids = ids[0:1, :] * 256.0 + ids[1:2, :]
            seg_row[:, pl.ds(off, n)] = ids
            seg_col[pl.ds(off, n), :] = jnp.broadcast_to(ids, (128, n)).T
        got = nn(normed[j][...], w[...]) + bias[layer : layer + 1, :]
        qkv[pl.ds(off, n), :] = got.astype(BF)
    scale = HEAD_DIM ** (-0.5)
    for i in range(ts):
        length = (i + 1) * n
        key_at = lax.broadcasted_iota(jnp.int32, (length, n), 0)
        query_at = lax.broadcasted_iota(jnp.int32, (length, n), 1) + i * n
        allowed = (seg_col[:length, 0:1] == seg_row[:, i * n : length]) & (key_at <= query_at)
        distance = (query_at - key_at).astype(F32)
        for h in range(heads):
            here = h * HEAD_DIM
            q = qkv[i * n : length, here : here + HEAD_DIM]
            keys = qkv[:length, width + here : width + here + HEAD_DIM]
            values = qkv[:length, 2 * width + here : 2 * width + here + HEAD_DIM]
            s = nt(keys, q) * scale - slopes[h] * distance
            s = jnp.where(allowed, s, masked_score)
            top = jnp.max(s, axis=0, keepdims=True)
            p = jnp.exp(s - top)
            total = jnp.sum(p, axis=0, keepdims=True)
            out_t[here : here + HEAD_DIM, i * n : length] = tn(values, p.astype(BF)) / total
            lse[h : h + 1, i * n : length] = top + jnp.log(total)
    for j, (k, dc) in enumerate(slots_of(xs)):
        off = pl.multiple_of(block_minus(me, xs, k, dc) * n, n)
        outs[j][...] = out_t[:, pl.ds(off, n)].T.astype(BF)


def attn_fwd(me, slopes, given, w, bias, layer, xs, vec=None, segs=None):
    ts = len(given)
    raw = vec is not None
    heads = slopes.shape[0]
    n = given[0].shape[0] - (TILE if raw else 0)
    length, width = ts * n, heads * HEAD_DIM
    got = run(
        functools.partial(attn_fwd_kernel, ts, xs, heads, raw, layer),
        [shape((length, 3 * width), BF), shape((width, length), F32), shape((heads, length), F32)]
        + ([shape((1, length), F32), shape((length, 128), F32)] if raw else [])
        + [shape((n, width), BF)] * ts
        + ([shape((n, D), BF)] * ts if raw else []),
        [me, slopes],
        given + [w, bias] + ([vec] if raw else list(segs)),
        flops=2 * length * D * 3 * width + 3 * length * length * width,
    )
    if raw:
        return got[0], got[1], got[2], list(got[5 : 5 + ts]), list(got[5 + ts :]), (got[3], got[4])
    return got[0], got[1], got[2], list(got[3:]), given, segs


def attn_bwd_kernel(ts, xs, heads, me, slopes, *refs):
    grads = refs[:ts]
    qkv, out_t, lse, w, seg_row, seg_col = refs[ts : ts + 6]
    parts = refs[ts + 6 : 2 * ts + 6]
    souts = refs[2 * ts + 6 : 3 * ts + 6]
    gbuf, dq_buf, dk_buf, dv_buf = refs[3 * ts + 6 :]
    n = grads[0].shape[0]
    width = heads * HEAD_DIM
    scale = HEAD_DIM ** (-0.5)
    for j, (k, dc) in enumerate(slots_of(xs)):
        off = pl.multiple_of(block_minus(me, xs, k, dc) * n, n)
        gbuf[pl.ds(off, n), :] = grads[j][...]
    dk_buf[...] = jnp.zeros_like(dk_buf)
    dv_buf[...] = jnp.zeros_like(dv_buf)
    for i in range(ts):
        length = (i + 1) * n
        key_at = lax.broadcasted_iota(jnp.int32, (length, n), 0)
        query_at = lax.broadcasted_iota(jnp.int32, (length, n), 1) + i * n
        allowed = (seg_col[:length, 0:1] == seg_row[:, i * n : length]) & (key_at <= query_at)
        distance = (query_at - key_at).astype(F32)
        for h in range(heads):
            here = h * HEAD_DIM
            q = qkv[i * n : length, here : here + HEAD_DIM]
            keys = qkv[:length, width + here : width + here + HEAD_DIM]
            values = qkv[:length, 2 * width + here : 2 * width + here + HEAD_DIM]
            g = gbuf[i * n : length, here : here + HEAD_DIM]
            delta = jnp.sum(
                g.astype(F32).T * out_t[here : here + HEAD_DIM, i * n : length], axis=0, keepdims=True
            )
            s = nt(keys, q) * scale - slopes[h] * distance
            p = jnp.where(allowed, jnp.exp(s - lse[h : h + 1, i * n : length]), 0.0)
            ds = (p * (nt(values, g) - delta)).astype(BF)
            dq_buf[i * n : length, here : here + HEAD_DIM] = tn(ds, keys) * scale
            dk_buf[:length, here : here + HEAD_DIM] += nn(ds, q)
            dv_buf[:length, here : here + HEAD_DIM] += nn(p.astype(BF), g)
    for j, (k, dc) in enumerate(slots_of(xs)):
        off = pl.multiple_of(block_minus(me, xs, k, dc) * n, n)
        rows = pl.ds(off, n)
        parts[j][:, :width] = dq_buf[rows, :].astype(BF)
        parts[j][:, width : 2 * width] = (dk_buf[rows, :] * scale).astype(BF)
        parts[j][:, 2 * width :] = dv_buf[rows, :].astype(BF)
        souts[j][...] = nt(parts[j][...], w[...]).astype(souts[j].dtype)


def attn_bwd(me, slopes, grads, qkv, out_t, lse, w, seg_row, seg_col, xs):
    ts = len(grads)
    heads = slopes.shape[0]
    n = grads[0].shape[0]
    length, width = ts * n, heads * HEAD_DIM
    got = run(
        functools.partial(attn_bwd_kernel, ts, xs, heads),
        [shape((n, 3 * width), BF)] * ts + [shape((n, D), F32)] + [shape((n, D), BF)] * (ts - 1),
        [me, slopes],
        grads + [qkv, out_t, lse, w, seg_row, seg_col],
        scratch=[pltpu.VMEM((length, width), BF)] + [pltpu.VMEM((length, width), F32)] * 3,
        flops=2 * length * D * 3 * width + 6 * length * length * width,
    )
    return list(got[:ts]), list(got[ts:])


def out_kernel(ts, xs, at, me, *refs):
    heads = refs[:ts]
    w, vec, stream, middle, normed = refs[ts:]
    width = heads[0].shape[1]
    total = stream[: middle.shape[0], :].astype(F32) + vec[at : at + 1, :]
    for j, (k, dc) in enumerate(slots_of(xs)):
        off = pl.multiple_of(lo_plus(me, xs, k, dc) * width, width)
        total = total + nn(heads[j][...], w[pl.ds(off, width), :])
    middle[...] = total
    unit, _ = norm_parts(total)
    normed[...] = (unit * vec[at + 3 : at + 4, :] + vec[at + 5 : at + 6, :]).astype(BF)


def out_project(me, heads, w, vec, layer, stream, xs):
    n = heads[0].shape[0]
    return run(
        functools.partial(out_kernel, len(heads), xs, 6 * layer),
        [shape((n, D), F32), shape((n, D), BF)],
        [me],
        heads + [w, vec, stream],
        flops=2 * n * D * D,
    )


def ffn_fwd_kernel(count, layer, *refs):
    normed = refs[:count]
    up, bias, down = refs[count : count + 3]
    outs = refs[count + 3 :]
    root, cubic = 0.7978845608028654, 0.044715
    for j in range(count):
        hidden, slope, part = outs[3 * j : 3 * j + 3]
        u = nn(normed[j][...], up[...]) + bias[layer : layer + 1, :]
        square = u * u
        t = jnp.tanh(root * (u + cubic * square * u))
        half = 0.5 * (1.0 + t)
        hidden[...] = (u * half).astype(BF)
        slope[...] = (half + 0.5 * u * (1.0 - t * t) * (root * (1.0 + 3.0 * cubic * square))).astype(BF)
        part[...] = nn(hidden[...], down[...]).astype(part.dtype)


def ffn_fwd(normed, up, bias, layer, down, kinds):
    n = normed[0].shape[0]
    wide = up.shape[1]
    outs = []
    for kind in kinds:
        outs += [shape((n, wide), BF), shape((n, wide), BF), shape((n, D), kind)]
    got = run(
        functools.partial(ffn_fwd_kernel, len(normed), layer),
        outs,
        [],
        normed + [up, bias, down],
        flops=4 * n * D * wide * len(normed),
    )
    return list(got[0::3]), list(got[1::3]), list(got[2::3])


def ffn_bwd_kernel(count, *refs):
    grads, slopes = refs[:count], refs[count : 2 * count]
    up, down = refs[2 * count : 2 * count + 2]
    outs = refs[2 * count + 2 :]
    for j in range(count):
        du, part = outs[2 * j : 2 * j + 2]
        du[...] = (nt(grads[j][...], down[...]) * slopes[j][...].astype(F32)).astype(BF)
        part[...] = nt(du[...], up[...]).astype(part.dtype)


def ffn_bwd(grads, slopes, up, down, kinds):
    n = grads[0].shape[0]
    wide = up.shape[1]
    outs = []
    for kind in kinds:
        outs += [shape((n, wide), BF), shape((n, D), kind)]
    got = run(
        functools.partial(ffn_bwd_kernel, len(grads)),
        outs,
        [],
        grads + slopes + [up, down],
        flops=4 * n * D * wide * len(grads),
    )
    return list(got[0::2]), list(got[1::2])


def end_kernel(count, at, last, *refs):
    terms = refs[:count]
    middle, vec = refs[count : count + 2]
    total = middle[...] + vec[at + 1 : at + 2, :]
    for t in terms:
        total = total + t[...].astype(F32)
    if last:
        refs[-1][...] = total.astype(BF)
        return
    stream, normed = refs[count + 2 :]
    stream[...] = total
    unit, _ = norm_parts(total)
    normed[...] = (unit * vec[at + 8 : at + 9, :] + vec[at + 10 : at + 11, :]).astype(BF)


def layer_end(terms, middle, vec, layer, last):
    n = middle.shape[0]
    outs = [shape((n, D), BF)] if last else [shape((n, D), F32), shape((n, D), BF)]
    return run(functools.partial(end_kernel, len(terms), 6 * layer, last), outs, [], terms + [middle, vec])


def norm_back(values, gain, grad):
    unit, rstd = norm_parts(values)
    scaled = grad * gain
    lead = jnp.mean(scaled, axis=-1, keepdims=True)
    along = jnp.mean(scaled * unit, axis=-1, keepdims=True)
    back = rstd * (scaled - lead - unit * along)
    return back, jnp.sum(grad * unit, axis=0, keepdims=True), jnp.sum(grad, axis=0, keepdims=True)


def mid_back_kernel(count, ts, xs, at, me, *refs):
    terms = refs[:count]
    grad, middle, vec, w = refs[count : count + 4]
    dh, dy, sums = refs[count + 4 : count + 7]
    outs = refs[count + 7 :]
    total = terms[0][...].astype(F32)
    for t in terms[1:]:
        total = total + t[...].astype(F32)
    back, gains, shifts = norm_back(middle[...], vec[at : at + 1, :], total)
    now = grad[...].astype(F32) + back
    dh[...] = now
    dy[...] = now.astype(BF)
    sums[0:1, :] = gains
    sums[1:2, :] = shifts
    sums[2:3, :] = jnp.sum(dy[...].astype(F32), axis=0, keepdims=True)
    width = outs[0].shape[1]
    for j, (k, dc) in enumerate(slots_of(xs)):
        off = pl.multiple_of(lo_plus(me, xs, k, dc) * width, width)
        outs[j][...] = nt(dy[...], w[pl.ds(off, width), :]).astype(BF)


def mid_back(me, terms, grad, middle, vec, layer, w, ts, xs):
    n = middle.shape[0]
    got = run(
        functools.partial(mid_back_kernel, len(terms), ts, xs, 6 * layer + 3),
        [shape((n, D), F32), shape((n, D), BF), shape((3, D), F32)] + [shape((n, D // ts), BF)] * ts,
        [me],
        terms + [grad, middle, vec, w],
        flops=2 * n * D * D,
    )
    return got[0], got[1], got[2], list(got[3:])


def start_back_kernel(count, at, *refs):
    terms = refs[:count]
    grad, stream, vec, dh, dz, sums = refs[count:]
    total = terms[0][...].astype(F32)
    for t in terms[1:]:
        total = total + t[...].astype(F32)
    back, gains, shifts = norm_back(stream[: dh.shape[0], :].astype(F32), vec[at : at + 1, :], total)
    now = grad[...] + back
    dh[...] = now
    dz[...] = now.astype(BF)
    sums[0:1, :] = gains
    sums[1:2, :] = shifts
    sums[2:3, :] = jnp.sum(dz[...].astype(F32), axis=0, keepdims=True)


def start_back(terms, grad, stream, vec, layer):
    n = grad.shape[0]
    return run(
        functools.partial(start_back_kernel, len(terms), 6 * layer + 2),
        [shape((n, D), F32), shape((n, D), BF), shape((3, D), F32)],
        [],
        terms + [grad, stream, vec],
    )


def column_sums(refs):
    total = jnp.sum(refs[0][...].astype(F32), axis=0, keepdims=True)
    for b in refs[1:]:
        total = total + jnp.sum(b[...].astype(F32), axis=0, keepdims=True)
    return total


def cols_part(ts, xs, hs, rows, me, left, right, put):
    tile = CORES * ts * rows
    for kh in list(range(1, hs)) + [0]:
        h = lax.rem(me[0] + kh, hs)
        for k in range(xs):
            place_at = (h * ts + lax.rem(me[1] + k, xs) * CORES) * ts * rows
            cols = pl.ds(pl.multiple_of(place_at, tile), tile)
            got = tn(left[0][:, cols], right[0][...])
            for j in range(1, ts):
                got = got + tn(left[j][:, cols], right[j][...])
            for c in range(CORES):
                dc = lax.rem(me[2] + c, CORES)
                for b in range(ts):
                    kb = lax.rem(b - me[3] + ts, ts)
                    at = (c * ts + b) * rows
                    put(kh, kb, dc, k, got[at : at + rows, :].astype(BF))


def wgrad_cols_kernel(ts, xs, hs, rows, beside, me, *refs):
    left, right = refs[:ts], refs[ts : 2 * ts]
    refs = refs[2 * ts :]
    if beside:
        near, refs = refs[0], refs[1:]
    refs[0][...] = column_sums(right)
    outs = refs[1:]
    wide = right[0].shape[1]

    def put(kh, kb, dc, k, block):
        outs[kh][kb, k * CORES + dc, :, :wide] = block

    cols_part(ts, xs, hs, rows, me, left, right, put)
    if beside:
        cols = outs[0].shape[3] - wide
        for kh in range(hs):
            for kb in range(ts):
                for p in range(ts):
                    outs[kh][kb, p, :, wide:] = near[kh, kb, :, p * cols : (p + 1) * cols]


def wgrad_cols(me, left, right, hs, xs, near=None):
    ts = len(left)
    rows = D // (hs * ts * ts)
    n, wide = right[0].shape
    beside = near is not None
    got = run(
        functools.partial(wgrad_cols_kernel, ts, xs, hs, rows, beside),
        [shape((1, wide), F32)] + [shape((ts, ts, rows, wide + (D // ts if beside else 0)), BF)] * hs,
        [me],
        left + right + ([near] if beside else []),
        flops=2 * ts * n * D * wide,
    )
    return got[0], list(got[1:])


def wgrad_down_kernel(ts, hs, rows, tall, me, *refs):
    hidden, dz = refs[:ts], refs[ts : 2 * ts]
    outs = refs[2 * ts :]
    cols = outs[0].shape[3]
    group = min(ts, max(1, 256 // tall))
    for kh in list(range(1, hs)) + [0]:
        h = lax.rem(me[0] + kh, hs)
        for first in range(0, ts, group):
            take = pl.ds(pl.multiple_of((h * ts + first) * tall, group * tall), group * tall)
            got = tn(hidden[0][:, take], dz[0][...])
            for j in range(1, ts):
                got = got + tn(hidden[j][:, take], dz[j][...])
            for b in range(group):
                kb = lax.rem(first + b - me[3] + ts, ts)
                for g in range(ts):
                    p, low = (g * rows) // tall, (g * rows) % tall
                    outs[kh][kb, g] = got[
                        b * tall + low : b * tall + low + rows, p * cols : (p + 1) * cols
                    ].astype(BF)


def wgrad_down(me, hidden, dz, hs):
    ts = len(hidden)
    rows = D // (hs * ts * ts)
    n, wide = hidden[0].shape
    return list(
        run(
            functools.partial(wgrad_down_kernel, ts, hs, rows, wide // (hs * ts)),
            [shape((ts, ts, rows, wide), BF)] * hs,
            [me],
            hidden + dz,
            flops=2 * ts * n * D * wide,
        )
    )


def wgrad_out_kernel(ts, xs, hs, rows, me, *refs):
    left = refs[:ts]
    right, out = refs[ts], refs[ts + 1]
    width = left[0].shape[1]
    for j, (k, dc) in enumerate(slots_of(xs)):
        got = tn(left[j][...], right[...])
        first = lo_plus(me, xs, k, dc) * (width // rows)
        for g in range(width // rows):
            i = first + g
            h = lax.div(i, ts * ts)
            lo = lax.rem(lax.div(i, ts), ts)
            b = lax.rem(i, ts)
            kk = lax.rem(lax.div(lo, CORES) - me[1] + xs, xs)
            dd = lax.rem(lax.rem(lo, CORES) + me[2], CORES)
            kh = lax.rem(h - me[0] + hs, hs)
            kb = lax.rem(b - me[3] + ts, ts)
            out[dd, kk, kh, kb] = got[g * rows : (g + 1) * rows, :].astype(BF)


def wgrad_out(me, left, right, hs, xs):
    ts = len(left)
    rows = D // (hs * ts * ts)
    (got,) = run(
        functools.partial(wgrad_out_kernel, ts, xs, hs, rows),
        [shape((CORES, xs, hs, ts, rows, D), BF)],
        [me],
        left + [right],
        flops=2 * right.shape[0] * D * D,
    )
    return got


def join_kernel(ts, xs, layers, me, *refs):
    out_q, out_u = refs[-2:]
    wide = out_q.shape[2] // (3 * ts)
    chunk = out_u.shape[2] // (2 * ts)
    at = 0
    for layer in range(layers):
        for k, dc in slots_of(xs):
            lo = lo_minus(me, xs, k, dc)
            q, u = refs[at], refs[at + 1]
            at += 2
            for j in range(3):
                off = pl.multiple_of(j * D + lo * wide, 128)
                out_q[layer, :, pl.ds(off, wide)] = q[:, j * wide : (j + 1) * wide].astype(F32)
            for j in range(2):
                off = pl.multiple_of(j * (chunk * ts) + lo * chunk, 128)
                out_u[layer, :, pl.ds(off, chunk)] = u[:, j * chunk : (j + 1) * chunk].astype(F32)


def join(me, grads, ts, xs):
    layers = len(grads)
    arrays = []
    for q, u in grads:
        for s in slots_of(xs):
            arrays += [q[s], u[s]]
    rows = arrays[0].shape[0]
    return run(
        functools.partial(join_kernel, ts, xs, layers),
        [shape((layers, rows, arrays[0].shape[1] * ts), F32), shape((layers, rows, arrays[1].shape[1] * ts), F32)],
        [me],
        arrays,
    )


def sum_small(mine, shared, hs, ts, xs):
    mine = mine + shift(mine, CORE, CORES, 1)
    for_all = mine
    for k in range(1, xs):
        for_all = for_all + shift(mine, XX, xs, k)
    both = jnp.concatenate([for_all, shared], 0)
    total = both
    for kh in range(1, hs):
        total = total + shift(both, HI, hs, kh)
    out = total
    for kb in range(1, ts):
        out = out + shift(total, BLK, ts, kb)
    return out


def on_device(
    hs,
    ts,
    xs,
    tokens,
    segment_ids,
    out_grad,
    qkv_weight,
    qv_bias,
    out_weight,
    out_bias,
    up_weight,
    up_bias,
    down_weight,
    down_bias,
    norm_gain,
    norm_shift,
):
    layers = qkv_weight.shape[0]
    n = tokens.shape[1]
    length = ts * n
    heads = HEADS // ts
    index = tuple(lax.axis_index(a) for a in (HI, XX, CORE, BLK))
    hi, xx, core, blk = index
    lo = xx * CORES + core
    me = jnp.stack(index).astype(jnp.int32)
    slots = slots_of(xs)
    place_of = [(a % xs) * CORES + a // xs for a in range(ts)]
    turn = [(place_of[a] * ts + b, place_of[b] * ts + a) for a in range(ts) for b in range(ts)]
    turned = lambda x: lax.ppermute(x, (XX, CORE, BLK), turn)
    rows, each = qkv_weight.shape[1], out_bias.shape[1]
    wide, cols = 3 * D // ts, up_weight.shape[2] // ts
    fields = (qv_bias, out_bias, up_bias, down_bias, norm_gain, norm_shift)
    slopes = jnp.exp2(-8.0 * (lo * heads + jnp.arange(heads, dtype=F32) + 1.0) / HEADS)

    def own_columns(cuts):
        mine = exchange_lo(cuts, xs, 1)
        return [mine[s] for s in slots]

    def gather_out(near):
        group = gather_lo(near, xs)
        return place_out(me, [group[s] for s in slots], hs, ts, xs)

    mine = own_columns(near_cuts_of(me, qkv_weight, fields, xs, ts))
    tokens_own = turned(tie(message_of(tokens[0], segment_ids), mine))
    attn_out, ffn_out = {}, {}
    attn_work = Work(fetch(pack_first(mine, out_weight), attn_out, hs, ts))
    late_q, late_u = tie((qkv_weight, up_weight), mine)
    rest = own_columns(rest_cuts_of(me, late_q, late_u, xs, ts))
    packed = pack_rest(rest, down_weight, out_weight, wide, cols)
    for _ in range(ts):
        attn_work.step()
    by = gather_lo(tokens_own, xs)
    given = [by[s] for s in slots]
    attn_pieces = pieces_of(attn_out, hs, ts)
    ffn_work = Work(fetch(packed[0], ffn_out, hs, ts))
    w_qkv, out_near = place_attn(me, attn_pieces, rows, hs, ts, xs, True)
    vec, up_vec, qkv_vec = params(me, attn_pieces, rows, layers, each, cols, wide // 3, hs, ts, xs)

    stream = tokens_own
    stored, weights = [], []
    segs = None
    for l in range(layers):
        more = l + 1 < layers
        given = tie(given, ffn_work.step(w_qkv))
        if l + 1 == layers:
            grad_own = turned(tie(out_grad[0], given))
        w_out = gather_out(out_near)
        qkv, out_t, lse, heads_by, all_one, segs = attn_fwd(
            me, slopes, given, w_qkv, qkv_vec, l, xs, vec if l == 0 else None, segs
        )
        own = exchange_lo({s: heads_by[j] for j, s in enumerate(slots)}, xs, -1)
        own = tie([own[s] for s in slots], ffn_work.step(heads_by))
        if l + 1 == layers:
            own = tie(own, grad_own)
        middle, normed_two = out_project(me, own, w_out, vec, l, stream, xs)
        by = gather_lo(normed_two, xs)
        all_two = [by[s] for s in slots]
        near, far = all_two[:CORES], all_two[CORES:]
        if l == 0:
            near = tie(near, ffn_work.step(middle))
        while ffn_work.step() is not None and (hs - 1, ts - 1) not in ffn_out:
            pass
        ffn_pieces = pieces_of(ffn_out, hs, ts)
        if more:
            next_attn, next_ffn = {}, {}
            attn_work = Work(fetch(tie(packed[2 * l + 1], ffn_out[0, ts - 1]), next_attn, hs, ts))
        w_up, w_down = place_ffn(me, ffn_pieces, hs, ts, xs)
        hid_a, gel_a, part_a = ffn_fwd(near, w_up, up_vec, l, w_down, [F32] + [BF] * (CORES - 1))
        far = tie(far, part_a)
        if more:
            far = tie(far, attn_work.step(part_a))
        else:
            grad_by = gather_lo(tie(grad_own, all_two), xs)
        hid_b, gel_b, part_b = ffn_fwd(far, w_up, up_vec, l, w_down, [BF] * len(far))
        terms = scatter_lo(dict(zip(slots, part_a + part_b)), xs)
        stored.append((stream, all_one, qkv, out_t, lse, own, middle, all_two, hid_a + hid_b, gel_a + gel_b))
        weights.append((w_qkv, w_out, w_up, w_down))
        if more:
            terms = tie(terms, attn_work.step(part_b))
            ffn_work = Work(fetch(tie(packed[2 * l + 2], part_b), next_ffn, hs, ts))
            stream, normed = layer_end(terms, middle, vec, l, False)
            by = gather_lo(normed, xs)
            given = [by[s] for s in slots]
            given = tie(given, attn_work.step(normed), ffn_work.step(normed))
            while (hs - 1, ts - 1) not in next_attn:
                attn_work.step()
            w_qkv, out_near = place_attn(me, pieces_of(next_attn, hs, ts), rows, hs, ts, xs, True)
            attn_out, ffn_out = next_attn, next_ffn
        else:
            (final,) = layer_end(terms, middle, vec, l, True)
    result = turned(final)

    dh, dz = grad_own, grad_own
    down_sum = jnp.sum(grad_own.astype(F32), axis=0, keepdims=True)
    mine_sums, shared_sums = [None] * layers, [None] * layers
    q_grads, u_grads, d_grads, o_grads = [[None] * layers for _ in range(4)]

    def send_cols(terms, at=slice(None)):
        blocks = {s: total_of(terms, (j, slice(None), at)).astype(BF) for j, s in enumerate(slots)}
        return exchange_lo(blocks, xs, 1)

    def unfolded(terms, at=slice(None), count=D // cols):
        total = total_of(terms, (slice(None), slice(None), at))
        total = total.reshape(count, -1, total.shape[-1])
        return jnp.concatenate([total[p] for p in range(count)], 1)

    def marker(parts):
        return parts[-1][0, 0, :8, :128]

    class Sums:
        def __init__(self, parts, *after):
            self.terms = []
            if after:
                parts = parts[:1] + list(tie(parts[1:], after))
            self.work = Work(reduce(parts, self.terms, hs, ts))
            self.step = self.work.step

        def finish(self, *after):
            while len(self.terms) < ts:
                self.step(*after)
            return self.terms

    late = None
    for l in reversed(range(layers)):
        w_qkv, w_out, w_up, w_down = weights[l]
        stream, all_one, qkv, out_t, lse, own, middle, all_two, hidden, gel = stored[l]
        first_layer = l == 0
        by = grad_by if late is None else gather_lo(dz, xs)
        all_dz = [by[s] for s in slots]
        near, far = all_dz[:CORES], all_dz[CORES:]
        if late:
            near = tie(near, late["d"].step(dz), late["u"].step(dz))
            late["a"] = Sums(late["a_parts"], near)
        else:
            near = tie(near, final)
        du_a, part_a = ffn_bwd(near, gel[:CORES], w_up, w_down, [F32] + [BF] * (CORES - 1))
        far = tie(far, part_a)
        if late:
            far = tie(far, late["d"].step(part_a))
        du_b, part_b = ffn_bwd(far, gel[CORES:], w_up, w_down, [BF] * (ts - CORES))
        all_du = du_a + du_b
        terms = scatter_lo(dict(zip(slots, part_a + part_b)), xs)
        d_parts = wgrad_down(me, hidden, tie(all_dz, part_b), hs)
        d_sums = Sums(d_parts)
        up_sum, u_parts = wgrad_cols(me, all_two, tie(all_du, marker(d_parts)), hs, xs)
        terms = tie(terms, up_sum)
        if late:
            terms = tie(terms, late["u"].step(part_b), late["a"].step(up_sum))
        dh1, dy, mid_sums, d_heads = mid_back(me, terms, dh, middle, vec, l, w_out, ts, xs)
        by = exchange_lo(dict(zip(slots, d_heads)), xs, 1)
        d_out = [by[s] for s in slots]
        out_part = wgrad_out(me, own, dy, hs, xs)
        got = shift(out_part[1], CORE, CORES, 1)
        both = [(out_part[0, k].astype(F32) + got[k].astype(F32)) for k in range(xs)]
        o_sent = [both[k].astype(BF) for k in range(1, xs)]
        o_got = [shift(o_sent[k - 1], XX, xs, k) for k in range(1, xs)]
        d_out = tie(d_out, o_sent)
        if late:
            d_out = tie(d_out, late["u"].step(dy), late["a"].step(dy))
        else:
            d_out = tie(d_out, d_sums.step(dy))
            u_sums = Sums(u_parts, d_out)
        dqkv, parts = attn_bwd(me, slopes, d_out, qkv, out_t, lse, w_qkv, *segs, xs)
        o_near = both[0]
        for g in tie(o_got, dqkv):
            o_near = o_near + g.astype(F32)
        o_near = o_near.astype(BF)
        terms = scatter_lo(dict(zip(slots, tie(parts, o_near))), xs)
        qkv_sum, a_parts = wgrad_cols(me, all_one, dqkv, hs, xs, o_near)
        terms = tie(terms, qkv_sum, d_sums.step(dqkv))
        if late:
            u_sums = Sums(u_parts, qkv_sum)
        dh, dz, start_sums = start_back(terms, dh1, stream, vec, l)
        mine_sums[l] = jnp.concatenate([down_sum, mid_sums, start_sums[:2]], 0)
        third = wide // 3
        shared_sums[l] = (up_sum, qkv_sum[:, :third], qkv_sum[:, 2 * third :])
        down_sum = start_sums[2:3]
        if not first_layer:
            late = dict(d=d_sums, u=u_sums, a_parts=a_parts)
    u_sums.step(dz)
    a_sums = Sums(a_parts, u_sums.terms)
    late["a"].step(dz)
    d_sums.finish(dz)
    d_grads[0] = unfolded(d_sums.terms)
    a_sums.step()
    u_grads[0] = send_cols(u_sums.finish())
    d_grads[1] = unfolded(late["d"].finish(dz))
    u_grads[1] = send_cols(late["u"].finish(dz))
    q_grads[1] = send_cols(late["a"].finish(dz), slice(0, wide))
    o_grads[1] = unfolded(late["a"].terms, slice(wide, None), ts)
    a_sums.finish()
    q_grads[0] = send_cols(a_sums.terms, slice(0, wide))
    o_grads[0] = unfolded(a_sums.terms, slice(wide, None), ts)
    input_grad = turned(dz)

    full = max(D, shared_sums[0][0].shape[1])
    pad = lambda x: jnp.pad(x, ((0, 0), (0, full - x.shape[1])))
    both = []
    for l in range(layers):
        up_sum, q_sum, v_sum = shared_sums[l]
        both += [pad(up_sum), pad(jnp.concatenate([q_sum, v_sum], 1))]
    sums = sum_small(jnp.concatenate(mine_sums, 0), jnp.concatenate(both, 0), hs, ts, xs)
    device = (hi * ts + lo) * ts + blk
    vectors = lax.dynamic_slice(sums[: 6 * layers, :D], (0, device * each), (6 * layers, each))
    vectors = vectors.reshape(layers, 6, each)
    shared = sums[6 * layers :].reshape(layers, 2, full)
    up_each, qv_each = up_bias.shape[1], qv_bias.shape[1]
    up_grad = lax.dynamic_slice(shared[:, 0], (0, (hi * ts + blk) * up_each), (layers, up_each))
    qv_grad = lax.dynamic_slice(shared[:, 1], (0, (hi * ts + blk) * qv_each), (layers, qv_each))
    q_grad, u_grad = join(me, list(zip(q_grads, u_grads)), ts, xs)
    return (
        result[None],
        input_grad[None],
        q_grad,
        qv_grad,
        jnp.stack(o_grads),
        vectors[:, 3],
        u_grad,
        up_grad,
        jnp.stack(d_grads),
        vectors[:, 0],
        jnp.stack([vectors[:, 4], vectors[:, 1]], 1),
        jnp.stack([vectors[:, 5], vectors[:, 2]], 1),
    )


def solution(mesh):
    ts = mesh.shape["blk"]
    hs = mesh.shape["rows"] // ts
    xs = ts // CORES
    fine = Mesh(mesh.devices.reshape(hs, xs, CORES, ts), (HI, XX, CORE, BLK))
    rows, every = (HI, XX, CORE), (HI, XX, CORE, BLK)
    row_cut = P(None, every, None)
    vec_cut = P(None, every)
    norm_cut = P(None, None, every)
    cuts = (row_cut, vec_cut, row_cut, vec_cut, row_cut, vec_cut, row_cut, vec_cut, norm_cut, norm_cut)
    acts = P(rows, BLK, None)
    return jax.shard_map(
        functools.partial(on_device, hs, ts, xs),
        mesh=fine,
        in_specs=(acts, P(rows, BLK), acts) + cuts,
        out_specs=(acts, acts) + cuts,
        check_vma=False,
    )
```

```python
import functools

import jax
import jax.numpy as jnp
from jax import lax
from jax.experimental import pallas as pl
from jax.experimental.pallas import tpu as pltpu
from jax.sharding import Mesh
from jax.sharding import PartitionSpec as P

D = 1024
HEADS = 8
HEAD_DIM = 128
CORES = 2
norm_eps = 1e-05
masked_score = -1e30
BF = jnp.bfloat16
F32 = jnp.float32
TILE = 16
VMEM_BYTES = 32 * 1024 * 1024

HI, XX, CORE, BLK = "hi", "xx", "core", "blk"


def nn(a, b):
    return lax.dot_general(a, b, (((1,), (0,)), ((), ())), preferred_element_type=F32)


def nt(a, b):
    return lax.dot_general(a, b, (((1,), (1,)), ((), ())), preferred_element_type=F32)


def tn(a, b):
    return lax.dot_general(a, b, (((0,), (0,)), ((), ())), preferred_element_type=F32)


def shape(dims, dtype):
    return jax.ShapeDtypeStruct(tuple(dims), dtype)


def run(kernel, outs, smem, arrays, scratch=(), flops=0, trans=0):
    size = lambda s: s.size * s.dtype.itemsize
    moved = sum(size(a) for a in arrays) + sum(size(o) for o in outs)
    return pl.pallas_call(
        kernel,
        out_shape=tuple(outs),
        in_specs=[pl.BlockSpec(memory_space=pltpu.SMEM)] * len(smem)
        + [pl.BlockSpec(memory_space=pltpu.VMEM)] * len(arrays),
        out_specs=tuple(pl.BlockSpec(memory_space=pltpu.VMEM) for _ in outs),
        scratch_shapes=list(scratch),
        compiler_params=pltpu.CompilerParams(vmem_limit_bytes=VMEM_BYTES),
        cost_estimate=pl.CostEstimate(flops=flops, bytes_accessed=moved, transcendentals=trans),
    )(*smem, *arrays)


def slots_of(xs):
    return [(k, dc) for k in range(xs) for dc in range(CORES)]


def lo_minus(me, xs, k, dc):
    return lax.rem(me[1] - k + xs, xs) * CORES + lax.rem(me[2] + dc, CORES)


def lo_plus(me, xs, k, dc):
    return lax.rem(me[1] + k, xs) * CORES + lax.rem(me[2] + dc, CORES)


def block_minus(me, xs, k, dc):
    return lax.rem(me[2] + dc, CORES) * xs + lax.rem(me[1] - k + xs, xs)


def tie(x, *after):
    return lax.optimization_barrier((x, after))[0]


def shift(x, axis, size, step):
    return lax.ppermute(x, axis, [(i, (i + step) % size) for i in range(size)])


def gather_lo(x, xs):
    out = {}
    for k in range(xs):
        out[k, 0] = x if k == 0 else shift(x, XX, xs, k)
    for k in range(xs):
        out[k, 1] = shift(out[k, 0], CORE, CORES, 1)
    return out


def scatter_lo(parts, xs):
    got = {}
    for k in list(range(1, xs)) + [0]:
        got[k] = shift(parts[k, 1].astype(BF), CORE, CORES, 1)
    terms, sent = [parts[0, 0]], []
    for k in range(1, xs):
        both = (parts[k, 0].astype(F32) + got[k].astype(F32)).astype(BF)
        sent.append(both)
        terms.append(shift(both, XX, xs, -k))
    return terms + [got[0]], sent


def send_lo(x, xs, k, dc):
    if k == 0 and dc == 0:
        return x
    pairs = [
        (a * CORES + c, ((a + k) % xs) * CORES + (c + dc) % CORES) for a in range(xs) for c in range(CORES)
    ]
    return lax.ppermute(x, (XX, CORE), pairs)


def exchange_lo(blocks, xs, sign):
    order = [s for s in slots_of(xs) if s[0]] + [s for s in slots_of(xs) if not s[0]]
    return {(k, dc): send_lo(blocks[k, dc], xs, sign * k, dc) for k, dc in order}


class Work:
    def __init__(self, steps):
        self.steps = steps
        next(steps)

    def step(self, *after):
        try:
            return self.steps.send(after)
        except StopIteration as end:
            return end.value


def fetch(x, out, hs, ts):
    out[0, 0] = way = x
    behind = None
    for kb in range(ts):
        came = way
        up = [shift(came, HI, hs, kh) for kh in range(1, hs)]
        if kb + 1 < ts:
            way = shift(came, BLK, ts, 1)
        after = yield came
        if after:
            behind, way = tie((behind, way), after)
        if behind is not None:
            for kh in range(1, hs):
                out[kh, kb - 1] = behind[kh - 1]
        behind = up
        if kb + 1 < ts:
            out[0, kb + 1] = way
    for kh in range(1, hs):
        out[kh, ts - 1] = up[kh - 1]
    return up


def pieces_of(out, hs, ts):
    return [out[kh, kb] for kh in range(hs) for kb in range(ts)]


def total_of(terms, at=slice(None)):
    total = terms[0][at].astype(F32)
    for t in terms[1:]:
        total = total + t[at].astype(F32)
    return total


def norm_parts(values):
    centre = values - jnp.mean(values, axis=-1, keepdims=True)
    spread = jnp.mean(centre * centre, axis=-1, keepdims=True)
    rstd = lax.rsqrt(spread + norm_eps)
    return centre * rstd, rstd


def near_kernel(xs, ts, each, me, wq, *refs):
    given, outs, line = refs[:6], refs[6:-9], refs[-9]
    weight, fields, sems = refs[-8], refs[-7:-1], refs[-1]
    copies = [pltpu.make_async_copy(wq.at[0], weight, sems.at[0])]
    for j in range(6):
        copies.append(pltpu.make_async_copy(given[j], fields[j], sems.at[j + 1]))
    for c in copies:
        c.start()
    line[...] = jnp.zeros_like(line)
    for c in copies:
        c.wait()
    layers, rows, _ = wq.shape
    for layer in range(layers):
        at = layer * each * 12
        for f in fields[:4]:
            wide = f.shape[1]
            line[0:1, at : at + wide] = f[layer : layer + 1, :].astype(F32)
            at += wide
        for f in fields[4:]:
            for j in range(2):
                line[0:1, at : at + each] = f[layer, j : j + 1, :].astype(F32)
                at += each
    small = line[...].astype(BF)
    chunk = outs[0].shape[1] // 3
    for out, (k, dc) in zip(outs, slots_of(xs)):
        lo = lo_plus(me, xs, k, dc)
        for j in range(3):
            off = pl.multiple_of((j * ts + lo) * chunk, 128)
            out[:rows, j * chunk : (j + 1) * chunk] = weight[:, pl.ds(off, chunk)]
        out[rows:, :] = small


def near_cuts_of(me, wq, fields, xs, ts):
    _, rows, full = wq.shape
    outs = [shape((rows + TILE, full // ts), BF)] * ts
    got = pl.pallas_call(
        functools.partial(near_kernel, xs, ts, fields[1].shape[1]),
        out_shape=tuple(outs),
        in_specs=[pl.BlockSpec(memory_space=pltpu.SMEM)] + [pl.BlockSpec(memory_space=pl.ANY)] * 7,
        out_specs=tuple(pl.BlockSpec(memory_space=pltpu.VMEM) for _ in outs),
        scratch_shapes=[pltpu.VMEM((TILE, full // ts), F32), pltpu.VMEM(wq.shape[1:], BF)]
        + [pltpu.VMEM(f.shape, BF) for f in fields]
        + [pltpu.SemaphoreType.DMA((7,))],
        compiler_params=pltpu.CompilerParams(vmem_limit_bytes=VMEM_BYTES),
    )(me, wq, *fields)
    return dict(zip(slots_of(xs), got))


def message_kernel(tok, ids, msg):
    n = tok.shape[0]
    msg[:n, :] = tok[...]
    high = ids[...] // 256
    below = jnp.concatenate([high, ids[...] - high * 256], 0).astype(F32)
    fill = jnp.concatenate([below, jnp.zeros((TILE - 2, n), F32)], 0)
    msg[n:, :] = jnp.zeros((TILE, D), BF)
    msg[n:, :n] = fill.astype(BF)


def message_of(tok, ids):
    (got,) = run(message_kernel, [shape((tok.shape[0] + TILE, D), BF)], [], [tok, ids])
    return got


def rest_kernel(xs, ts, me, wq, wu, *outs):
    layers = wq.shape[0]
    chunk = wq.shape[2] // (3 * ts)
    half = wu.shape[2] // (2 * ts)
    for k, dc in slots_of(xs):
        lo = lo_plus(me, xs, k, dc)
        rest = outs[dc].at[k]
        at = 0
        for layer in range(layers):
            if layer:
                for j in range(3):
                    got = wq[layer, :, pl.ds(pl.multiple_of((j * ts + lo) * chunk, 128), chunk)]
                    rest[:, at : at + chunk] = got
                    at += chunk
            for j in range(2):
                got = wu[layer, :, pl.ds(pl.multiple_of((j * ts + lo) * half, 128), half)]
                rest[:, at : at + half] = got
                at += half


def rest_cuts_of(me, wq, wu, xs, ts):
    layers, rows, full = wu.shape
    wide = 3 * D // ts
    return run(
        functools.partial(rest_kernel, xs, ts),
        [shape((xs, rows, layers * (wide + full // ts) - wide), BF)] * CORES,
        [me],
        [wq, wu],
    )


def fold_in(out, block, at, cols):
    rows = block.shape[0]
    for p in range(block.shape[1] // cols):
        out[p * rows : (p + 1) * rows, at : at + cols] = block[:, p * cols : (p + 1) * cols]


def pack_first_kernel(count, rows, *refs):
    blocks, out_w, out = refs[:count], refs[count], refs[count + 1]
    wide = blocks[0].shape[1]
    for j, block in enumerate(blocks):
        out[j * rows : (j + 1) * rows, :wide] = block[:rows, :]
    fold_in(out, out_w.at[0], wide, out.shape[1] - wide)
    tail = jnp.concatenate([b[rows : rows + 1, :].astype(F32) for b in blocks], 0)
    tail = jnp.concatenate([tail, jnp.zeros((TILE - count, wide), F32)], 0)
    out[count * rows :, :wide] = tail.astype(BF)
    out[count * rows :, wide:] = jnp.zeros((TILE, out.shape[1] - wide), BF)


def pack_first(blocks, out_w):
    count = len(blocks)
    rows, wide = blocks[0].shape[0] - TILE, blocks[0].shape[1]
    (got,) = run(
        functools.partial(pack_first_kernel, count, rows),
        [shape((count * rows + TILE, wide + D // count), BF)],
        [],
        blocks + [out_w],
    )
    return got


def pack_rest_kernel(count, layers, wide, *refs):
    blocks, down, out_w = refs[:count], refs[count], refs[count + 1]
    outs = refs[count + 2 :]
    rows = blocks[0].shape[0]
    cols = outs[0].shape[1] // 2
    at = 0
    for layer in range(layers):
        if layer:
            attn = outs[2 * layer - 1]
            for j, block in enumerate(blocks):
                attn[j * rows : (j + 1) * rows, :wide] = block[:, at : at + wide]
            fold_in(attn, out_w.at[layer], wide, D // count)
            at += wide
        ffn = outs[2 * layer]
        for j, block in enumerate(blocks):
            ffn[j * rows : (j + 1) * rows, :cols] = block[:, at : at + cols]
        fold_in(ffn, down.at[layer], cols, cols)
        at += cols


def pack_rest(blocks, down, out_w, wide, cols):
    count = len(blocks)
    rows = blocks[0].shape[0]
    layers = down.shape[0]
    outs = []
    for layer in range(layers):
        if layer:
            outs.append(shape((count * rows, wide + D // count), BF))
        outs.append(shape((count * rows, 2 * cols), BF))
    return run(
        functools.partial(pack_rest_kernel, count, layers, wide), outs, [], blocks + [down, out_w]
    )


def params_kernel(hs, ts, xs, rows, layers, each, me, *refs):
    pieces = refs[: hs * ts]
    vec, up, qkv = refs[hs * ts :]
    count = hs * ts * ts
    values = jnp.concatenate([p[ts * rows : ts * rows + ts, : qkv.shape[1]].astype(F32) for p in pieces], 0).astype(BF)
    at = lax.broadcasted_iota(jnp.int32, (1, count), 1)
    kh, kb, slot = at // (ts * ts), (at // ts) % ts, at % ts
    k, dc = slot // CORES, slot % CORES
    h = lax.rem(me[0] - kh + hs, hs)
    l = lax.rem(me[1] - k + xs, xs) * CORES + lax.rem(me[2] + dc, CORES)
    b = lax.rem(me[3] - kb + ts, ts)
    owner = (h * ts + l) * ts + b
    pick = (lax.broadcasted_iota(jnp.int32, (count, count), 0) == owner).astype(BF)
    table = nn(pick, values).astype(BF)
    lo = me[1] * CORES + me[2]

    def spread(first, size, wide):
        tile = lax.broadcasted_iota(jnp.int32, (size, wide), 1) % size
        same = (tile == lax.broadcasted_iota(jnp.int32, (size, wide), 0)).astype(BF)
        return nn(table[:, first : first + size], same)

    def keep(x, mask):
        return jnp.sum(jnp.where(mask, x, 0.0), axis=0, keepdims=True)

    row = lambda wide: lax.broadcasted_iota(jnp.int32, (count, wide), 0)
    col = lambda wide: lax.broadcasted_iota(jnp.int32, (count, wide), 1)
    full = each * count
    own_up, own_q = full * up.shape[1] // D, qkv.shape[1] // 3
    for layer in range(layers):
        first = layer * each * 12
        member = row(own_q) // ts % ts == lo
        part = row(own_q) % ts == col(own_q) // (2 * each)
        half = row(own_q) // (ts * ts)
        q = spread(first, 2 * each, own_q)
        qkv[layer : layer + 1, :own_q] = keep(q, member & part & (half == 0))
        qkv[layer : layer + 1, own_q : 2 * own_q] = jnp.zeros((1, own_q), F32)
        qkv[layer : layer + 1, 2 * own_q :] = keep(q, member & part & (half == 1))
        first = first + 2 * each
        mine = col(full) // each == row(full)
        for f, skip in enumerate((0, 5, 6, 7, 8, 9)):
            vec[layer * 6 + f : layer * 6 + f + 1, :] = keep(spread(first + skip * each, each, full), mine)
        here = (row(own_up) // ts % ts == lo) & (
            (row(own_up) // (ts * ts)) * ts + row(own_up) % ts == col(own_up) // (4 * each)
        )
        up[layer : layer + 1, :] = keep(spread(first + each, 4 * each, own_up), here)


def params(me, pieces, rows, layers, each, own_up, own_q, hs, ts, xs):
    return run(
        functools.partial(params_kernel, hs, ts, xs, rows, layers, each),
        [shape((layers * 6, D), F32), shape((layers, own_up), F32), shape((layers, 3 * own_q), F32)],
        [me],
        pieces,
    )


def fold_out(piece, rows, at, cols, parts):
    return jnp.concatenate([piece[p * rows : (p + 1) * rows, at : at + cols] for p in range(parts)], 1)


def piece_at(refs, at, whole, hs, ts, me):
    kh, kb = at // ts, at % ts
    h = lax.rem(me[0] - kh + hs, hs)
    if whole:
        return refs[kh].at[kb], h, kb
    return refs[at], h, lax.rem(me[3] - kb + ts, ts)


def place_attn_kernel(hs, ts, xs, whole, with_out, me, *refs):
    qkv = refs[-2] if with_out else refs[-1]
    rows, wide = qkv.shape[3:]
    for at in range(hs * ts):
        piece, h, b = piece_at(refs, at, whole, hs, ts, me)
        for j, (k, dc) in enumerate(slots_of(xs)):
            qkv[h, lo_minus(me, xs, k, dc), b] = piece[j * rows : (j + 1) * rows, :wide]
        if with_out:
            out = refs[-1]
            cols = out.shape[3] // ts
            for p in range(ts):
                out[h, b, :, p * cols : (p + 1) * cols] = piece[p * rows : (p + 1) * rows, wide : wide + cols]


def place_attn(me, pieces, rows, hs, ts, xs, with_out):
    whole = len(pieces) == hs
    wide = 3 * D // ts
    got = run(
        functools.partial(place_attn_kernel, hs, ts, xs, whole, with_out),
        [shape((hs, ts, ts, rows, wide), BF)] + ([shape((hs, ts, rows, D), BF)] if with_out else []),
        [me],
        pieces,
    )
    return (got[0].reshape(D, wide),) + tuple(got[1:])


def place_ffn_kernel(hs, ts, xs, whole, me, *refs):
    up, down = refs[-2:]
    rows, cols = up.shape[3:]
    tall = down.shape[2]
    for at in range(hs * ts):
        piece, h, b = piece_at(refs, at, whole, hs, ts, me)
        for j, (k, dc) in enumerate(slots_of(xs)):
            up[h, lo_minus(me, xs, k, dc), b] = piece[j * rows : (j + 1) * rows, :cols]
        for p in range(D // cols):
            down[h, b, :, p * cols : (p + 1) * cols] = piece[p * tall : (p + 1) * tall, cols:]


def place_ffn(me, pieces, hs, ts, xs):
    whole = len(pieces) == hs
    tall, wide = pieces[0].shape[-2:]
    cols = wide // 2
    up, down = run(
        functools.partial(place_ffn_kernel, hs, ts, xs, whole),
        [shape((hs, ts, ts, tall // ts, cols), BF), shape((hs, ts, tall * cols // D, D), BF)],
        [me],
        pieces,
    )
    return up.reshape(D, cols), down.reshape(-1, D)


def place_out_kernel(hs, ts, xs, me, *refs):
    out = refs[-1]
    for j, (k, dc) in enumerate(slots_of(xs)):
        out[:, lo_minus(me, xs, k, dc)] = refs[j][...]


def place_out(me, group, hs, ts, xs):
    _, _, rows, wide = group[0].shape
    (got,) = run(
        functools.partial(place_out_kernel, hs, ts, xs), [shape((hs, ts, ts, rows, wide), BF)], [me], group
    )
    return got.reshape(-1, wide)


def attn_fwd_kernel(ts, xs, heads, raw, layer, me, slopes, *refs):
    given = refs[:ts]
    if raw:
        w, bias, vec = refs[ts : ts + 3]
        qkv, out_t, lse, seg_row, seg_col = refs[ts + 3 : ts + 8]
        outs, normed = refs[ts + 8 : 2 * ts + 8], refs[2 * ts + 8 : 3 * ts + 8]
    else:
        normed = given
        w, bias, seg_row, seg_col = refs[ts : ts + 4]
        qkv, out_t, lse = refs[ts + 4 : ts + 7]
        outs = refs[ts + 7 :]
    n = normed[0].shape[0]
    width = heads * HEAD_DIM
    for j, (k, dc) in enumerate(slots_of(xs)):
        off = pl.multiple_of(block_minus(me, xs, k, dc) * n, n)
        if raw:
            unit, _ = norm_parts(given[j][:n, :].astype(F32))
            normed[j][...] = (unit * vec[2:3, :] + vec[4:5, :]).astype(BF)
            ids = given[j][n : n + 8, :n].astype(F32)
            ids = ids[0:1, :] * 256.0 + ids[1:2, :]
            seg_row[:, pl.ds(off, n)] = ids
            seg_col[pl.ds(off, n), :] = jnp.broadcast_to(ids, (128, n)).T
        got = nn(normed[j][...], w[...]) + bias[layer : layer + 1, :]
        qkv[pl.ds(off, n), :] = got.astype(BF)
    scale = HEAD_DIM ** (-0.5)
    for i in range(ts):
        length = (i + 1) * n
        key_at = lax.broadcasted_iota(jnp.int32, (length, n), 0)
        query_at = lax.broadcasted_iota(jnp.int32, (length, n), 1) + i * n
        allowed = (seg_col[:length, 0:1] == seg_row[:, i * n : length]) & (key_at <= query_at)
        distance = (query_at - key_at).astype(F32)
        for h in range(heads):
            here = h * HEAD_DIM
            q = qkv[i * n : length, here : here + HEAD_DIM]
            keys = qkv[:length, width + here : width + here + HEAD_DIM]
            values = qkv[:length, 2 * width + here : 2 * width + here + HEAD_DIM]
            s = nt(keys, q) * scale - slopes[h] * distance
            s = jnp.where(allowed, s, masked_score)
            top = jnp.max(s, axis=0, keepdims=True)
            p = jnp.exp(s - top)
            total = jnp.sum(p, axis=0, keepdims=True)
            out_t[here : here + HEAD_DIM, i * n : length] = tn(values, p.astype(BF)) / total
            lse[h : h + 1, i * n : length] = top + jnp.log(total)
    for j, (k, dc) in enumerate(slots_of(xs)):
        off = pl.multiple_of(block_minus(me, xs, k, dc) * n, n)
        outs[j][...] = out_t[:, pl.ds(off, n)].T.astype(BF)


def attn_fwd(me, slopes, given, w, bias, layer, xs, vec=None, segs=None):
    ts = len(given)
    raw = vec is not None
    heads = slopes.shape[0]
    n = given[0].shape[0] - (TILE if raw else 0)
    length, width = ts * n, heads * HEAD_DIM
    got = run(
        functools.partial(attn_fwd_kernel, ts, xs, heads, raw, layer),
        [shape((length, 3 * width), BF), shape((width, length), F32), shape((heads, length), F32)]
        + ([shape((1, length), F32), shape((length, 128), F32)] if raw else [])
        + [shape((n, width), BF)] * ts
        + ([shape((n, D), BF)] * ts if raw else []),
        [me, slopes],
        given + [w, bias] + ([vec] if raw else list(segs)),
        flops=2 * length * D * 3 * width + 3 * length * length * width,
    )
    if raw:
        return got[0], got[1], got[2], list(got[5 : 5 + ts]), list(got[5 + ts :]), (got[3], got[4])
    return got[0], got[1], got[2], list(got[3:]), given, segs


def attn_bwd_kernel(ts, xs, heads, me, slopes, *refs):
    grads = refs[:ts]
    qkv, out_t, lse, w, seg_row, seg_col = refs[ts : ts + 6]
    parts = refs[ts + 6 : 2 * ts + 6]
    souts = refs[2 * ts + 6 : 3 * ts + 6]
    gbuf, dq_buf, dk_buf, dv_buf = refs[3 * ts + 6 :]
    n = grads[0].shape[0]
    width = heads * HEAD_DIM
    scale = HEAD_DIM ** (-0.5)
    for j, (k, dc) in enumerate(slots_of(xs)):
        off = pl.multiple_of(block_minus(me, xs, k, dc) * n, n)
        gbuf[pl.ds(off, n), :] = grads[j][...]
    dk_buf[...] = jnp.zeros_like(dk_buf)
    dv_buf[...] = jnp.zeros_like(dv_buf)
    for i in range(ts):
        length = (i + 1) * n
        key_at = lax.broadcasted_iota(jnp.int32, (length, n), 0)
        query_at = lax.broadcasted_iota(jnp.int32, (length, n), 1) + i * n
        allowed = (seg_col[:length, 0:1] == seg_row[:, i * n : length]) & (key_at <= query_at)
        distance = (query_at - key_at).astype(F32)
        for h in range(heads):
            here = h * HEAD_DIM
            q = qkv[i * n : length, here : here + HEAD_DIM]
            keys = qkv[:length, width + here : width + here + HEAD_DIM]
            values = qkv[:length, 2 * width + here : 2 * width + here + HEAD_DIM]
            g = gbuf[i * n : length, here : here + HEAD_DIM]
            delta = jnp.sum(
                g.astype(F32).T * out_t[here : here + HEAD_DIM, i * n : length], axis=0, keepdims=True
            )
            s = nt(keys, q) * scale - slopes[h] * distance
            p = jnp.where(allowed, jnp.exp(s - lse[h : h + 1, i * n : length]), 0.0)
            ds = (p * (nt(values, g) - delta)).astype(BF)
            dq_buf[i * n : length, here : here + HEAD_DIM] = tn(ds, keys) * scale
            dk_buf[:length, here : here + HEAD_DIM] += nn(ds, q)
            dv_buf[:length, here : here + HEAD_DIM] += nn(p.astype(BF), g)
    for j, (k, dc) in enumerate(slots_of(xs)):
        off = pl.multiple_of(block_minus(me, xs, k, dc) * n, n)
        rows = pl.ds(off, n)
        parts[j][:, :width] = dq_buf[rows, :].astype(BF)
        parts[j][:, width : 2 * width] = (dk_buf[rows, :] * scale).astype(BF)
        parts[j][:, 2 * width :] = dv_buf[rows, :].astype(BF)
        souts[j][...] = nt(parts[j][...], w[...]).astype(souts[j].dtype)


def attn_bwd(me, slopes, grads, qkv, out_t, lse, w, seg_row, seg_col, xs):
    ts = len(grads)
    heads = slopes.shape[0]
    n = grads[0].shape[0]
    length, width = ts * n, heads * HEAD_DIM
    got = run(
        functools.partial(attn_bwd_kernel, ts, xs, heads),
        [shape((n, 3 * width), BF)] * ts + [shape((n, D), F32)] + [shape((n, D), BF)] * (ts - 1),
        [me, slopes],
        grads + [qkv, out_t, lse, w, seg_row, seg_col],
        scratch=[pltpu.VMEM((length, width), BF)] + [pltpu.VMEM((length, width), F32)] * 3,
        flops=2 * length * D * 3 * width + 6 * length * length * width,
    )
    return list(got[:ts]), list(got[ts:])


def out_kernel(ts, xs, at, me, *refs):
    heads = refs[:ts]
    w, vec, stream, middle, normed = refs[ts:]
    width = heads[0].shape[1]
    total = stream[: middle.shape[0], :].astype(F32) + vec[at : at + 1, :]
    for j, (k, dc) in enumerate(slots_of(xs)):
        off = pl.multiple_of(lo_plus(me, xs, k, dc) * width, width)
        total = total + nn(heads[j][...], w[pl.ds(off, width), :])
    middle[...] = total
    unit, _ = norm_parts(total)
    normed[...] = (unit * vec[at + 3 : at + 4, :] + vec[at + 5 : at + 6, :]).astype(BF)


def out_project(me, heads, w, vec, layer, stream, xs):
    n = heads[0].shape[0]
    return run(
        functools.partial(out_kernel, len(heads), xs, 6 * layer),
        [shape((n, D), F32), shape((n, D), BF)],
        [me],
        heads + [w, vec, stream],
        flops=2 * n * D * D,
    )


def ffn_fwd_kernel(count, layer, *refs):
    normed = refs[:count]
    up, bias, down = refs[count : count + 3]
    outs = refs[count + 3 :]
    root, cubic = 0.7978845608028654, 0.044715
    for j in range(count):
        hidden, slope, part = outs[3 * j : 3 * j + 3]
        u = nn(normed[j][...], up[...]) + bias[layer : layer + 1, :]
        square = u * u
        t = jnp.tanh(root * (u + cubic * square * u))
        half = 0.5 * (1.0 + t)
        hidden[...] = (u * half).astype(BF)
        slope[...] = (half + 0.5 * u * (1.0 - t * t) * (root * (1.0 + 3.0 * cubic * square))).astype(BF)
        part[...] = nn(hidden[...], down[...]).astype(part.dtype)


def ffn_fwd(normed, up, bias, layer, down, kinds):
    n = normed[0].shape[0]
    wide = up.shape[1]
    outs = []
    for kind in kinds:
        outs += [shape((n, wide), BF), shape((n, wide), BF), shape((n, D), kind)]
    got = run(
        functools.partial(ffn_fwd_kernel, len(normed), layer),
        outs,
        [],
        normed + [up, bias, down],
        flops=4 * n * D * wide * len(normed),
    )
    return list(got[0::3]), list(got[1::3]), list(got[2::3])


def ffn_bwd_kernel(count, *refs):
    grads, slopes = refs[:count], refs[count : 2 * count]
    up, down = refs[2 * count : 2 * count + 2]
    outs = refs[2 * count + 2 :]
    for j in range(count):
        du, part = outs[2 * j : 2 * j + 2]
        du[...] = (nt(grads[j][...], down[...]) * slopes[j][...].astype(F32)).astype(BF)
        part[...] = nt(du[...], up[...]).astype(part.dtype)


def ffn_bwd(grads, slopes, up, down, kinds):
    n = grads[0].shape[0]
    wide = up.shape[1]
    outs = []
    for kind in kinds:
        outs += [shape((n, wide), BF), shape((n, D), kind)]
    got = run(
        functools.partial(ffn_bwd_kernel, len(grads)),
        outs,
        [],
        grads + slopes + [up, down],
        flops=4 * n * D * wide * len(grads),
    )
    return list(got[0::2]), list(got[1::2])


def end_kernel(count, at, last, *refs):
    terms = refs[:count]
    middle, vec = refs[count : count + 2]
    total = middle[...] + vec[at + 1 : at + 2, :]
    for t in terms:
        total = total + t[...].astype(F32)
    if last:
        refs[-1][...] = total.astype(BF)
        return
    stream, normed = refs[count + 2 :]
    stream[...] = total
    unit, _ = norm_parts(total)
    normed[...] = (unit * vec[at + 8 : at + 9, :] + vec[at + 10 : at + 11, :]).astype(BF)


def layer_end(terms, middle, vec, layer, last):
    n = middle.shape[0]
    outs = [shape((n, D), BF)] if last else [shape((n, D), F32), shape((n, D), BF)]
    return run(functools.partial(end_kernel, len(terms), 6 * layer, last), outs, [], terms + [middle, vec])


def norm_back(values, gain, grad):
    unit, rstd = norm_parts(values)
    scaled = grad * gain
    lead = jnp.mean(scaled, axis=-1, keepdims=True)
    along = jnp.mean(scaled * unit, axis=-1, keepdims=True)
    back = rstd * (scaled - lead - unit * along)
    return back, jnp.sum(grad * unit, axis=0, keepdims=True), jnp.sum(grad, axis=0, keepdims=True)


def mid_back_kernel(count, ts, xs, at, me, *refs):
    terms = refs[:count]
    grad, middle, vec, w = refs[count : count + 4]
    dh, dy, sums = refs[count + 4 : count + 7]
    outs = refs[count + 7 :]
    total = terms[0][...].astype(F32)
    for t in terms[1:]:
        total = total + t[...].astype(F32)
    back, gains, shifts = norm_back(middle[...], vec[at : at + 1, :], total)
    now = grad[...].astype(F32) + back
    dh[...] = now
    dy[...] = now.astype(BF)
    sums[0:1, :] = gains
    sums[1:2, :] = shifts
    sums[2:3, :] = jnp.sum(dy[...].astype(F32), axis=0, keepdims=True)
    width = outs[0].shape[2]
    for k, dc in slots_of(xs):
        off = pl.multiple_of(lo_plus(me, xs, k, dc) * width, width)
        outs[dc][k] = nt(dy[...], w[pl.ds(off, width), :]).astype(BF)


def mid_back(me, terms, grad, middle, vec, layer, w, ts, xs):
    n = middle.shape[0]
    got = run(
        functools.partial(mid_back_kernel, len(terms), ts, xs, 6 * layer + 3),
        [shape((n, D), F32), shape((n, D), BF), shape((3, D), F32)] + [shape((xs, n, D // ts), BF)] * CORES,
        [me],
        terms + [grad, middle, vec, w],
        flops=2 * n * D * D,
    )
    return got[0], got[1], got[2], list(got[3:])


def start_back_kernel(count, at, *refs):
    terms = refs[:count]
    grad, stream, vec, dh, dz, sums = refs[count:]
    total = terms[0][...].astype(F32)
    for t in terms[1:]:
        total = total + t[...].astype(F32)
    back, gains, shifts = norm_back(stream[: dh.shape[0], :].astype(F32), vec[at : at + 1, :], total)
    now = grad[...] + back
    dh[...] = now
    dz[...] = now.astype(BF)
    sums[0:1, :] = gains
    sums[1:2, :] = shifts
    sums[2:3, :] = jnp.sum(dz[...].astype(F32), axis=0, keepdims=True)


def start_back(terms, grad, stream, vec, layer):
    n = grad.shape[0]
    return run(
        functools.partial(start_back_kernel, len(terms), 6 * layer + 2),
        [shape((n, D), F32), shape((n, D), BF), shape((3, D), F32)],
        [],
        terms + [grad, stream, vec],
    )


def column_sums(refs):
    total = jnp.sum(refs[0][...].astype(F32), axis=0, keepdims=True)
    for b in refs[1:]:
        total = total + jnp.sum(b[...].astype(F32), axis=0, keepdims=True)
    return total


def cols_part(ts, xs, hs, rows, own, me, left, right, put):
    tile = CORES * ts * rows
    for kh in list(range(1, hs)) + [0]:
        h = kh if own else lax.rem(me[0] + kh, hs)
        for k in range(xs):
            place_at = (h * ts + lax.rem(me[1] + k, xs) * CORES) * ts * rows
            cols = pl.ds(pl.multiple_of(place_at, tile), tile)
            got = tn(left[0][:, cols], right[0][...])
            for j in range(1, ts):
                got = got + tn(left[j][:, cols], right[j][...])
            for c in range(CORES):
                dc = lax.rem(me[2] + c, CORES)
                for b in range(ts):
                    kb = b if own else lax.rem(b - me[3] + ts, ts)
                    at = (c * ts + b) * rows
                    put(kh, kb, dc, k, got[at : at + rows, :].astype(BF))


def wgrad_cols_kernel(ts, xs, hs, rows, beside, own, me, *refs):
    left, right = refs[:ts], refs[ts : 2 * ts]
    refs = refs[2 * ts :]
    if beside:
        near, refs = refs[0], refs[1:]
    refs[0][...] = column_sums(right)
    outs = refs[1:]
    wide = right[0].shape[1]

    def put(kh, kb, dc, k, block):
        outs[kh][kb, k * CORES + dc, :, :wide] = block

    cols_part(ts, xs, hs, rows, own, me, left, right, put)
    if beside:
        cols = outs[0].shape[3] - wide
        for kh in range(hs):
            for kb in range(ts):
                to = lax.rem(me[3] + kb, ts) if own else kb
                where = lax.rem(kh - me[0] + hs, hs) if own else kh
                for p in range(ts):
                    outs[kh][to, p, :, wide:] = near[where, kb, :, p * cols : (p + 1) * cols]


def wgrad_cols(me, left, right, hs, xs, own, near=None):
    ts = len(left)
    rows = D // (hs * ts * ts)
    n, wide = right[0].shape
    beside = near is not None
    outs = [shape((ts, ts, rows, wide + (D // ts if beside else 0)), BF)] * hs
    if own:
        outs = [shape((hs,) + outs[0].shape, BF)]
    got = run(
        functools.partial(whole_kernel(wgrad_cols_kernel) if own else wgrad_cols_kernel, ts, xs, hs, rows, beside, own),
        [shape((1, wide), F32)] + outs,
        [me],
        left + right + ([near] if beside else []),
        flops=2 * ts * n * D * wide,
    )
    return got[0], list(got[1:])


def wgrad_ffn_kernel(ts, xs, hs, rows, tall, own, me, *refs):
    normed, du, hidden, dz = [refs[j * ts : (j + 1) * ts] for j in range(4)]
    refs[4 * ts][...] = column_sums(du)
    outs = refs[4 * ts + 1 :]
    cols = du[0].shape[1]

    def put(kh, kb, dc, k, block):
        outs[kh][kb, k * CORES + dc] = block

    cols_part(ts, xs, hs, rows, own, me, normed, du, put)
    group = min(ts, max(1, 256 // tall))
    for kh in list(range(1, hs)) + [0]:
        h = kh if own else lax.rem(me[0] + kh, hs)
        for first in range(0, ts, group):
            take = pl.ds(pl.multiple_of((h * ts + first) * tall, group * tall), group * tall)
            got = tn(hidden[0][:, take], dz[0][...])
            for j in range(1, ts):
                got = got + tn(hidden[j][:, take], dz[j][...])
            for b in range(group):
                kb = first + b if own else lax.rem(first + b - me[3] + ts, ts)
                for g in range(ts):
                    p, low = (g * rows) // tall, (g * rows) % tall
                    outs[kh][kb, ts + g] = got[
                        b * tall + low : b * tall + low + rows, p * cols : (p + 1) * cols
                    ].astype(BF)


def wgrad_ffn(me, normed, du, hidden, dz, hs, xs, own):
    ts = len(normed)
    rows = D // (hs * ts * ts)
    n, wide = du[0].shape
    outs = [shape((ts, 2 * ts, rows, wide), BF)] * hs
    if own:
        outs = [shape((hs, ts, 2 * ts, rows, wide), BF)]
    got = run(
        functools.partial(wgrad_ffn_kernel if not own else whole_kernel(wgrad_ffn_kernel), ts, xs, hs, rows, wide // (hs * ts), own),
        [shape((1, wide), F32)] + outs,
        [me],
        normed + du + hidden + dz,
        flops=4 * ts * n * D * wide,
    )
    return got[0], list(got[1:])


def whole_kernel(kernel):
    def wrapped(ts, xs, hs, *rest):
        return kernel(ts, xs, hs, *rest[:-1], *[rest[-1].at[h] for h in range(hs)])

    return wrapped


def wgrad_out_kernel(ts, xs, hs, rows, me, *refs):
    left = refs[:ts]
    right, out = refs[ts], refs[ts + 1]
    width = left[0].shape[1]
    for j, (k, dc) in enumerate(slots_of(xs)):
        got = tn(left[j][...], right[...])
        first = lo_plus(me, xs, k, dc) * (width // rows)
        for g in range(width // rows):
            i = first + g
            h = lax.div(i, ts * ts)
            lo = lax.rem(lax.div(i, ts), ts)
            b = lax.rem(i, ts)
            kk = lax.rem(lax.div(lo, CORES) - me[1] + xs, xs)
            dd = lax.rem(lax.rem(lo, CORES) + me[2], CORES)
            kh = lax.rem(h - me[0] + hs, hs)
            kb = lax.rem(b - me[3] + ts, ts)
            out[dd, kk, kh, kb] = got[g * rows : (g + 1) * rows, :].astype(BF)


def wgrad_out(me, left, right, hs, xs):
    ts = len(left)
    rows = D // (hs * ts * ts)
    (got,) = run(
        functools.partial(wgrad_out_kernel, ts, xs, hs, rows),
        [shape((CORES, xs, hs, ts, rows, D), BF)],
        [me],
        left + [right],
        flops=2 * right.shape[0] * D * D,
    )
    return got


def finish_kernel(counts, wide, ts, xs, *refs):
    layers = len(counts)
    outs = refs[-ts - 2 : -2]
    out_out, out_down = refs[-2:]
    rows, cols = refs[0].shape[1:]
    at = 0

    def total(count, j):
        got = refs[at][j].astype(F32)
        for t in refs[at + 1 : at + count]:
            got = got + t[j].astype(F32)
        return got

    for layer in range(layers):
        for j in range(ts):
            got = total(counts[layer], j)
            outs[j][layer * rows : (layer + 1) * rows, wide:] = got.astype(BF)
            got = total(counts[layer], ts + j)
            tall = out_down.shape[1]
            p, low = (j * rows) // tall, (j * rows) % tall
            out_down[layer, low : low + rows, p * cols : (p + 1) * cols] = got
        at += counts[layer]
    for layer in range(layers):
        for j in range(ts):
            got = total(counts[layer], j)
            outs[j][layer * rows : (layer + 1) * rows, :wide] = got[:, :wide].astype(BF)
            more = got.shape[1] - wide
            out_out[layer, :, j * more : (j + 1) * more] = got[:, wide:]
        at += counts[layer]


def finish(f_all, a_all, wide, ts, xs):
    layers = len(f_all)
    rows, cols = f_all[0][0].shape[1:]
    tall = ts * rows * cols // D
    got = run(
        functools.partial(finish_kernel, [len(f) for f in f_all], wide, ts, xs),
        [shape((layers * rows, wide + cols), BF)] * ts
        + [shape((layers, rows, D), F32), shape((layers, tall, D), F32)],
        [],
        [x for terms in f_all + a_all for x in terms],
    )
    return dict(zip(slots_of(xs), got)), got[ts], got[ts + 1]


def join_kernel(ts, xs, layers, me, *refs):
    out_q, out_u = refs[-2:]
    wide = out_q.shape[2] // (3 * ts)
    chunk = out_u.shape[2] // (2 * ts)
    rows = out_q.shape[1]
    for block, (k, dc) in zip(refs, slots_of(xs)):
        lo = lo_minus(me, xs, k, dc)
        for layer in range(layers):
            at = pl.ds(layer * rows, rows)
            for j in range(3):
                off = pl.multiple_of((j * ts + lo) * wide, 128)
                out_q[layer, :, pl.ds(off, wide)] = block[at, j * wide : (j + 1) * wide].astype(F32)
            for j in range(2):
                off = pl.multiple_of((j * ts + lo) * chunk, 128)
                have = 3 * wide + j * chunk
                out_u[layer, :, pl.ds(off, chunk)] = block[at, have : have + chunk].astype(F32)


def join(me, blocks, layers, ts, xs):
    arrays = [blocks[s] for s in slots_of(xs)]
    rows = arrays[0].shape[0] // layers
    wide = 3 * D // ts
    return run(
        functools.partial(join_kernel, ts, xs, layers),
        [shape((layers, rows, 3 * D), F32), shape((layers, rows, (arrays[0].shape[1] - wide) * ts), F32)],
        [me],
        arrays,
    )


def on_device(
    hs,
    ts,
    xs,
    tokens,
    segment_ids,
    out_grad,
    qkv_weight,
    qv_bias,
    out_weight,
    out_bias,
    up_weight,
    up_bias,
    down_weight,
    down_bias,
    norm_gain,
    norm_shift,
):
    layers = qkv_weight.shape[0]
    n = tokens.shape[1]
    length = ts * n
    heads = HEADS // ts
    index = tuple(lax.axis_index(a) for a in (HI, XX, CORE, BLK))
    hi, xx, core, blk = index
    lo = xx * CORES + core
    me = jnp.stack(index).astype(jnp.int32)
    slots = slots_of(xs)
    place_of = [(a % xs) * CORES + a // xs for a in range(ts)]
    turn = [(place_of[a] * ts + b, place_of[b] * ts + a) for a in range(ts) for b in range(ts)]
    turned = lambda x: lax.ppermute(x, (XX, CORE, BLK), turn)
    rows, each = qkv_weight.shape[1], out_bias.shape[1]
    wide, cols = 3 * D // ts, up_weight.shape[2] // ts
    fields = (qv_bias, out_bias, up_bias, down_bias, norm_gain, norm_shift)
    slopes = jnp.exp2(-8.0 * (lo * heads + jnp.arange(heads, dtype=F32) + 1.0) / HEADS)

    def own_columns(cuts):
        mine = exchange_lo(cuts, xs, 1)
        return [mine[s] for s in slots]

    def gather_out(near):
        group = gather_lo(near, xs)
        return place_out(me, [group[s] for s in slots], hs, ts, xs)

    def along_blk(x):
        return lax.all_gather(x, BLK, axis=0, tiled=False)

    def with_hi(x):
        return [x] + [shift(x, HI, hs, kh) for kh in range(1, hs)]

    tokens_own = turned(message_of(tokens[0], segment_ids))
    attn_out, ffn_out = {}, {}
    mine = own_columns(near_cuts_of(me, qkv_weight, fields, xs, ts))
    attn_work = Work(fetch(pack_first(mine, out_weight), attn_out, hs, ts))
    late_q, late_u = tie((qkv_weight, up_weight), mine)
    same, other = rest_cuts_of(me, late_q, late_u, xs, ts)
    other = shift(other, CORE, CORES, 1)
    rest = [same[0], other[0]]
    for k in range(1, xs):
        pair = shift(jnp.stack([same[k], other[k]]), XX, xs, k)
        rest += [pair[0], pair[1]]
    packed = pack_rest(rest, down_weight, out_weight, wide, cols)
    attn_work.step(tokens_own)
    by = gather_lo(tokens_own, xs)
    given = [by[s] for s in slots]
    for kb in range(1, ts):
        attn_work.step(*([packed[0]] if kb == 1 else [by[xs - 1, 0]] if kb == 2 else []))
    attn_pieces = pieces_of(attn_out, hs, ts)
    ffn_work = Work(fetch(packed[0], ffn_out, hs, ts))
    stacks = []
    for l in range(1, layers):
        attn_stack = along_blk(packed[2 * l - 1])
        stacks.append((attn_stack, along_blk(tie(packed[2 * l], attn_stack))))
    w_qkv, out_near = place_attn(me, attn_pieces, rows, hs, ts, xs, True)
    vec, up_vec, qkv_vec = params(me, attn_pieces, rows, layers, each, cols, wide // 3, hs, ts, xs)

    stream = tokens_own
    stored, weights = [], []
    segs = None
    for l in range(layers):
        more = l + 1 < layers
        if l == 0:
            given = tie(given, ffn_work.step(w_qkv))
        w_out = gather_out(out_near)
        qkv, out_t, lse, heads_by, all_one, segs = attn_fwd(
            me, slopes, given, w_qkv, qkv_vec, l, xs, vec if l == 0 else None, segs
        )
        own = exchange_lo({s: heads_by[j] for j, s in enumerate(slots)}, xs, -1)
        own = [own[s] for s in slots]
        if l == 0:
            own = tie(own, ffn_work.step(heads_by))
        if not more:
            own = tie(own, grad_x)
        middle, normed_two = out_project(me, own, w_out, vec, l, stream, xs)
        by = gather_lo(normed_two, xs)
        all_two = [by[s] for s in slots]
        near, far = all_two[:CORES], all_two[CORES:]
        if l == 0:
            near = tie(near, ffn_work.step(middle))
            while (hs - 1, ts - 1) not in ffn_out:
                ffn_work.step()
            ffn_pieces = pieces_of(ffn_out, hs, ts)
        w_up, w_down = place_ffn(me, ffn_pieces, hs, ts, xs)
        hid_a, gel_a, part_a = ffn_fwd(near, w_up, up_vec, l, w_down, [F32] + [BF] * (CORES - 1))
        far = tie(far, part_a)
        if more:
            attn_stack, ffn_stack = stacks[l]
            attn_pieces = with_hi(tie(attn_stack, all_two))
        if l + 2 == layers:
            grad_own = turned(tie(out_grad[0], all_two))
        hid_b, gel_b, part_b = ffn_fwd(far, w_up, up_vec, l, w_down, [BF] * len(far))
        terms, sent = scatter_lo(dict(zip(slots, part_a + part_b)), xs)
        stored.append((stream, all_one, qkv, out_t, lse, own, middle, all_two, hid_a + hid_b, gel_a + gel_b))
        weights.append((w_qkv, w_out, w_up, w_down))
        if more:
            stream, normed = layer_end(terms, middle, vec, l, False)
            by = gather_lo(normed, xs)
            given = [by[s] for s in slots]
            ffn_pieces = with_hi(tie(ffn_stack, normed))
            if l + 2 == layers:
                grad_x = [grad_own] + [shift(tie(grad_own, given), XX, xs, k) for k in range(1, xs)]
            w_qkv, out_near = place_attn(me, attn_pieces, rows, hs, ts, xs, True)
        else:
            (final,) = layer_end(terms, middle, vec, l, True)
    grad_by = {}
    for k in range(xs):
        grad_by[k, 0] = grad_x[k]
        grad_by[k, 1] = shift(grad_x[k], CORE, CORES, 1)

    dh, dz = grad_own, grad_own
    down_sum = jnp.sum(grad_own.astype(F32), axis=0, keepdims=True)
    mine_sums, shared_sums = [None] * layers, [None] * layers
    q_grads, u_grads, d_grads, o_grads = [[None] * layers for _ in range(4)]

    def send_cols(terms, at=slice(None)):
        blocks = {s: total_of(terms, (j, slice(None), at)).astype(BF) for j, s in enumerate(slots)}
        return exchange_lo(blocks, xs, 1)

    def unfolded(terms, at=slice(None), count=D // cols):
        total = total_of(terms, (slice(None), slice(None), at))
        total = total.reshape(count, -1, total.shape[-1])
        return jnp.concatenate([total[p] for p in range(count)], 1)

    def added(own, got):
        total = own.astype(F32)
        for g in got:
            total = total + g.astype(F32)
        return total.astype(BF)

    def scattered(x):
        x = x.reshape((hs * ts,) + x.shape[2:])
        return lax.psum_scatter(x, (HI, BLK), scatter_dimension=0, tiled=False)

    def add_up(own, got, *after):
        got = tie(got, after)
        total = []
        for kb in range(ts):
            block = own[kb].astype(F32)
            for g in got:
                block = block + g[kb].astype(F32)
            total.append(block.astype(BF) if kb else block)
        return total

    def send_blk(total):
        return [shift(total[kb], BLK, ts, kb) for kb in range(1, ts)]

    f_sums, a_sums = [None] * layers, [None] * layers
    for l in reversed(range(layers)):
        w_qkv, w_out, w_up, w_down = weights[l]
        stream, all_one, qkv, out_t, lse, own, middle, all_two, hidden, gel = stored[l]
        first_layer, last = l == 0, l + 1 == layers
        by = grad_by if last else gather_lo(dz, xs)
        all_dz = [by[s] for s in slots]
        near, far = all_dz[:CORES], all_dz[CORES:]
        if last:
            near = tie(near, final)
        du_a, part_a = ffn_bwd(near, gel[:CORES], w_up, w_down, [F32] + [BF] * (CORES - 1))
        far = tie(far, part_a)
        du_b, part_b = ffn_bwd(far, gel[CORES:], w_up, w_down, [BF] * (ts - CORES))
        all_du = du_a + du_b
        terms, sent = scatter_lo(dict(zip(slots, part_a + part_b)), xs)
        up_sum, f_parts = wgrad_ffn(me, all_two, tie(all_du, sent), hidden, all_dz, hs, xs, not first_layer)
        terms = tie(terms, up_sum)
        if first_layer:
            f_way = [shift(g, HI, hs, kh + 1) for kh, g in enumerate(f_parts[1:])]
        else:
            f_sums[l] = scattered(f_parts[0])
        dh1, dy, mid_sums, d_heads = mid_back(me, terms, dh, middle, vec, l, w_out, ts, xs)
        same, other = d_heads
        other = shift(other, CORE, CORES, 1)
        pairs = [jnp.stack([same[k], other[k]]) for k in range(1, xs)]
        d_out = [same[0], other[0]]
        for k in range(1, xs):
            pair = shift(pairs[k - 1], XX, xs, k)
            d_out += [pair[0], pair[1]]
        out_part = wgrad_out(me, tie(own, pairs), dy, hs, xs)
        got = shift(out_part[1], CORE, CORES, 1)
        both = [(out_part[0, k].astype(F32) + got[k].astype(F32)) for k in range(xs)]
        o_sent = [both[k].astype(BF) for k in range(1, xs)]
        d_out = tie(d_out, o_sent)
        dqkv, parts = attn_bwd(me, slopes, d_out, qkv, out_t, lse, w_qkv, *segs, xs)
        terms, sent = scatter_lo(dict(zip(slots, parts)), xs)
        o_got = [shift(tie(o_sent[k - 1], sent), XX, xs, k) for k in range(1, xs)]
        o_near = both[0]
        for g in tie(o_got, sent):
            o_near = o_near + g.astype(F32)
        if first_layer:
            qkv_sum, a_parts = wgrad_cols(me, all_one, tie(dqkv, sent), hs, xs, False, o_near.astype(BF))
            terms = tie(terms, qkv_sum)
            f_total = add_up(f_parts[0], f_way, qkv_sum)
            terms = tie(terms, f_total)
            f_got = send_blk(f_total)
            a_way = [shift(g, HI, hs, kh + 1) for kh, g in enumerate(a_parts[1:])]
        else:
            qkv_sum, a_parts = wgrad_cols(me, all_one, tie(dqkv, sent), hs, xs, True, o_near.astype(BF))
            a_sums[l] = scattered(tie(a_parts[0], f_sums[l]))
            terms = tie(terms, qkv_sum)
        dh, dz, start_sums = start_back(terms, dh1, stream, vec, l)
        mine_sums[l] = jnp.concatenate([down_sum, mid_sums, start_sums[:2]], 0)
        third = wide // 3
        shared_sums[l] = (up_sum, qkv_sum[:, :third], qkv_sum[:, 2 * third :])
        down_sum = start_sums[2:3]
    full = max(D, shared_sums[0][0].shape[1])
    pad = lambda x: jnp.pad(x, ((0, 0), (0, full - x.shape[1])))
    both = []
    for l in range(layers):
        up_sum, q_sum, v_sum = shared_sums[l]
        both += [pad(up_sum), pad(jnp.concatenate([q_sum, v_sum], 1))]
    mine = jnp.concatenate(mine_sums, 0)
    mine = mine + shift(mine, CORE, CORES, 1)
    mine_x = [shift(mine, XX, xs, k) for k in range(1, xs)]
    a_total = add_up(a_parts[0], a_way, f_got)
    a_got = send_blk(a_total)
    for x in tie(mine_x, a_total):
        mine = mine + x
    small = jnp.concatenate([mine] + both, 0)
    small_y = [shift(small, HI, hs, kh) for kh in range(1, hs)]
    both_turned = turned(jnp.stack([tie(dz, a_total), final]))
    input_grad, result = both_turned[0], both_turned[1]
    for y in small_y:
        small = small + y
    small_z = send_blk([small] * ts)
    f_all = [[f_total[0]] + f_got] + [[f_sums[l]] for l in range(1, layers)]
    a_all = [[a_total[0]] + a_got] + [[a_sums[l]] for l in range(1, layers)]
    blocks, out_grad_all, down_grad_all = finish(f_all, a_all, wide, ts, xs)
    q_grad, u_grad = join(me, exchange_lo(blocks, xs, 1), layers, ts, xs)
    sums = small
    for z in small_z:
        sums = sums + z

    device = (hi * ts + lo) * ts + blk
    vectors = lax.dynamic_slice(sums[: 6 * layers, :D], (0, device * each), (6 * layers, each))
    vectors = vectors.reshape(layers, 6, each)
    shared = sums[6 * layers :].reshape(layers, 2, full)
    up_each, qv_each = up_bias.shape[1], qv_bias.shape[1]
    up_grad = lax.dynamic_slice(shared[:, 0], (0, (hi * ts + blk) * up_each), (layers, up_each))
    qv_grad = lax.dynamic_slice(shared[:, 1], (0, (hi * ts + blk) * qv_each), (layers, qv_each))
    return (
        result[None],
        input_grad[None],
        q_grad,
        qv_grad,
        out_grad_all,
        vectors[:, 3],
        u_grad,
        up_grad,
        down_grad_all,
        vectors[:, 0],
        jnp.stack([vectors[:, 4], vectors[:, 1]], 1),
        jnp.stack([vectors[:, 5], vectors[:, 2]], 1),
    )


def solution(mesh):
    ts = mesh.shape["blk"]
    hs = mesh.shape["rows"] // ts
    xs = ts // CORES
    fine = Mesh(mesh.devices.reshape(hs, xs, CORES, ts), (HI, XX, CORE, BLK))
    rows, every = (HI, XX, CORE), (HI, XX, CORE, BLK)
    row_cut = P(None, every, None)
    vec_cut = P(None, every)
    norm_cut = P(None, None, every)
    cuts = (row_cut, vec_cut, row_cut, vec_cut, row_cut, vec_cut, row_cut, vec_cut, norm_cut, norm_cut)
    acts = P(rows, BLK, None)
    return jax.shard_map(
        functools.partial(on_device, hs, ts, xs),
        mesh=fine,
        in_specs=(acts, P(rows, BLK), acts) + cuts,
        out_specs=(acts, acts) + cuts,
        check_vma=False,
    )
```

```python
import functools

import jax
import jax.numpy as jnp
from jax import lax
from jax.experimental import pallas as pl
from jax.experimental.pallas import tpu as pltpu
from jax.sharding import Mesh
from jax.sharding import PartitionSpec as P

D = 1024
HEADS = 8
HEAD_DIM = 128
CORES = 2
norm_eps = 1e-05
masked_score = -1e30
BF = jnp.bfloat16
F32 = jnp.float32
TILE = 16
VMEM_BYTES = 32 * 1024 * 1024

HI, XX, CORE, BLK = "hi", "xx", "core", "blk"


def nn(a, b):
    return lax.dot_general(a, b, (((1,), (0,)), ((), ())), preferred_element_type=F32)


def nt(a, b):
    return lax.dot_general(a, b, (((1,), (1,)), ((), ())), preferred_element_type=F32)


def tn(a, b):
    return lax.dot_general(a, b, (((0,), (0,)), ((), ())), preferred_element_type=F32)


def shape(dims, dtype):
    return jax.ShapeDtypeStruct(tuple(dims), dtype)


def run(kernel, outs, smem, arrays, scratch=(), flops=0, trans=0):
    size = lambda s: s.size * s.dtype.itemsize
    moved = sum(size(a) for a in arrays) + sum(size(o) for o in outs)
    return pl.pallas_call(
        kernel,
        out_shape=tuple(outs),
        in_specs=[pl.BlockSpec(memory_space=pltpu.SMEM)] * len(smem)
        + [pl.BlockSpec(memory_space=pltpu.VMEM)] * len(arrays),
        out_specs=tuple(pl.BlockSpec(memory_space=pltpu.VMEM) for _ in outs),
        scratch_shapes=list(scratch),
        compiler_params=pltpu.CompilerParams(vmem_limit_bytes=VMEM_BYTES),
        cost_estimate=pl.CostEstimate(flops=flops, bytes_accessed=moved, transcendentals=trans),
    )(*smem, *arrays)


def slots_of(xs):
    return [(k, dc) for k in range(xs) for dc in range(CORES)]


def lo_minus(me, xs, k, dc):
    return lax.rem(me[1] - k + xs, xs) * CORES + lax.rem(me[2] + dc, CORES)


def lo_plus(me, xs, k, dc):
    return lax.rem(me[1] + k, xs) * CORES + lax.rem(me[2] + dc, CORES)


def block_minus(me, xs, k, dc):
    return lax.rem(me[2] + dc, CORES) * xs + lax.rem(me[1] - k + xs, xs)


def tie(x, *after):
    return lax.optimization_barrier((x, after))[0]


def shift(x, axis, size, step):
    return lax.ppermute(x, axis, [(i, (i + step) % size) for i in range(size)])


def gather_lo(x, xs):
    out = {}
    for k in range(xs):
        out[k, 0] = x if k == 0 else shift(x, XX, xs, k)
    for k in range(xs):
        out[k, 1] = shift(out[k, 0], CORE, CORES, 1)
    return out


def scatter_lo(parts, xs):
    got = {}
    for k in list(range(1, xs)) + [0]:
        got[k] = shift(parts[k, 1].astype(BF), CORE, CORES, 1)
    terms, sent = [parts[0, 0]], []
    for k in range(1, xs):
        both = (parts[k, 0].astype(F32) + got[k].astype(F32)).astype(BF)
        sent.append(both)
        terms.append(shift(both, XX, xs, -k))
    return terms + [got[0]], sent


def send_lo(x, xs, k, dc):
    if k == 0 and dc == 0:
        return x
    pairs = [
        (a * CORES + c, ((a + k) % xs) * CORES + (c + dc) % CORES) for a in range(xs) for c in range(CORES)
    ]
    return lax.ppermute(x, (XX, CORE), pairs)


def exchange_lo(blocks, xs, sign):
    order = [s for s in slots_of(xs) if s[0]] + [s for s in slots_of(xs) if not s[0]]
    return {(k, dc): send_lo(blocks[k, dc], xs, sign * k, dc) for k, dc in order}


class Work:
    def __init__(self, steps):
        self.steps = steps
        next(steps)

    def step(self, *after):
        try:
            return self.steps.send(after)
        except StopIteration as end:
            return end.value


def fetch(x, out, hs, ts):
    out[0, 0] = way = x
    behind = None
    for kb in range(ts):
        came = way
        up = [shift(came, HI, hs, kh) for kh in range(1, hs)]
        if kb + 1 < ts:
            way = shift(came, BLK, ts, 1)
        after = yield came
        if after:
            behind, way = tie((behind, way), after)
        if behind is not None:
            for kh in range(1, hs):
                out[kh, kb - 1] = behind[kh - 1]
        behind = up
        if kb + 1 < ts:
            out[0, kb + 1] = way
    for kh in range(1, hs):
        out[kh, ts - 1] = up[kh - 1]
    return up


def pieces_of(out, hs, ts):
    return [out[kh, kb] for kh in range(hs) for kb in range(ts)]


def total_of(terms, at=slice(None)):
    total = terms[0][at].astype(F32)
    for t in terms[1:]:
        total = total + t[at].astype(F32)
    return total


def norm_parts(values):
    centre = values - jnp.mean(values, axis=-1, keepdims=True)
    spread = jnp.mean(centre * centre, axis=-1, keepdims=True)
    rstd = lax.rsqrt(spread + norm_eps)
    return centre * rstd, rstd


def near_kernel(xs, ts, each, me, wq, *refs):
    given, outs, line = refs[:6], refs[6:-9], refs[-9]
    weight, fields, sems = refs[-8], refs[-7:-1], refs[-1]
    copies = [pltpu.make_async_copy(wq.at[0], weight, sems.at[0])]
    for j in range(6):
        copies.append(pltpu.make_async_copy(given[j], fields[j], sems.at[j + 1]))
    for c in copies:
        c.start()
    line[...] = jnp.zeros_like(line)
    for c in copies:
        c.wait()
    layers, rows, _ = wq.shape
    for layer in range(layers):
        at = layer * each * 12
        for f in fields[:4]:
            wide = f.shape[1]
            line[0:1, at : at + wide] = f[layer : layer + 1, :].astype(F32)
            at += wide
        for f in fields[4:]:
            for j in range(2):
                line[0:1, at : at + each] = f[layer, j : j + 1, :].astype(F32)
                at += each
    small = line[...].astype(BF)
    chunk = outs[0].shape[1] // 3
    for out, (k, dc) in zip(outs, slots_of(xs)):
        lo = lo_plus(me, xs, k, dc)
        for j in range(3):
            off = pl.multiple_of((j * ts + lo) * chunk, 128)
            out[:rows, j * chunk : (j + 1) * chunk] = weight[:, pl.ds(off, chunk)]
        out[rows:, :] = small


def near_cuts_of(me, wq, fields, xs, ts):
    _, rows, full = wq.shape
    outs = [shape((rows + TILE, full // ts), BF)] * ts
    got = pl.pallas_call(
        functools.partial(near_kernel, xs, ts, fields[1].shape[1]),
        out_shape=tuple(outs),
        in_specs=[pl.BlockSpec(memory_space=pltpu.SMEM)] + [pl.BlockSpec(memory_space=pl.ANY)] * 7,
        out_specs=tuple(pl.BlockSpec(memory_space=pltpu.VMEM) for _ in outs),
        scratch_shapes=[pltpu.VMEM((TILE, full // ts), F32), pltpu.VMEM(wq.shape[1:], BF)]
        + [pltpu.VMEM(f.shape, BF) for f in fields]
        + [pltpu.SemaphoreType.DMA((7,))],
        compiler_params=pltpu.CompilerParams(vmem_limit_bytes=VMEM_BYTES),
    )(me, wq, *fields)
    return dict(zip(slots_of(xs), got))


def message_kernel(tok, ids, msg):
    n = tok.shape[0]
    msg[:n, :] = tok[...]
    high = ids[...] // 256
    below = jnp.concatenate([high, ids[...] - high * 256], 0).astype(F32)
    fill = jnp.concatenate([below, jnp.zeros((TILE - 2, n), F32)], 0)
    msg[n:, :] = jnp.zeros((TILE, D), BF)
    msg[n:, :n] = fill.astype(BF)


def message_of(tok, ids):
    (got,) = run(message_kernel, [shape((tok.shape[0] + TILE, D), BF)], [], [tok, ids])
    return got


def rest_kernel(xs, ts, me, wq, wu, *outs):
    layers = wq.shape[0]
    chunk = wq.shape[2] // (3 * ts)
    half = wu.shape[2] // (2 * ts)
    for k, dc in slots_of(xs):
        lo = lo_plus(me, xs, k, dc)
        rest = outs[dc].at[k]
        at = 0
        for layer in range(layers):
            if layer:
                for j in range(3):
                    got = wq[layer, :, pl.ds(pl.multiple_of((j * ts + lo) * chunk, 128), chunk)]
                    rest[:, at : at + chunk] = got
                    at += chunk
            for j in range(2):
                got = wu[layer, :, pl.ds(pl.multiple_of((j * ts + lo) * half, 128), half)]
                rest[:, at : at + half] = got
                at += half


def rest_cuts_of(me, wq, wu, xs, ts):
    layers, rows, full = wu.shape
    wide = 3 * D // ts
    return run(
        functools.partial(rest_kernel, xs, ts),
        [shape((xs, rows, layers * (wide + full // ts) - wide), BF)] * CORES,
        [me],
        [wq, wu],
    )


def fold_in(out, block, at, cols):
    rows = block.shape[0]
    for p in range(block.shape[1] // cols):
        out[p * rows : (p + 1) * rows, at : at + cols] = block[:, p * cols : (p + 1) * cols]


def pack_first_kernel(count, rows, *refs):
    blocks, out_w, out = refs[:count], refs[count], refs[count + 1]
    wide = blocks[0].shape[1]
    for j, block in enumerate(blocks):
        out[j * rows : (j + 1) * rows, :wide] = block[:rows, :]
    fold_in(out, out_w.at[0], wide, out.shape[1] - wide)
    tail = jnp.concatenate([b[rows : rows + 1, :].astype(F32) for b in blocks], 0)
    tail = jnp.concatenate([tail, jnp.zeros((TILE - count, wide), F32)], 0)
    out[count * rows :, :wide] = tail.astype(BF)
    out[count * rows :, wide:] = jnp.zeros((TILE, out.shape[1] - wide), BF)


def pack_first(blocks, out_w):
    count = len(blocks)
    rows, wide = blocks[0].shape[0] - TILE, blocks[0].shape[1]
    (got,) = run(
        functools.partial(pack_first_kernel, count, rows),
        [shape((count * rows + TILE, wide + D // count), BF)],
        [],
        blocks + [out_w],
    )
    return got


def pack_rest_kernel(count, layers, wide, *refs):
    blocks, down, out_w = refs[:count], refs[count], refs[count + 1]
    outs = refs[count + 2 :]
    rows = blocks[0].shape[0]
    cols = outs[0].shape[1] // 2
    at = 0
    for layer in range(layers):
        if layer:
            attn = outs[2 * layer - 1]
            for j, block in enumerate(blocks):
                attn[j * rows : (j + 1) * rows, :wide] = block[:, at : at + wide]
            fold_in(attn, out_w.at[layer], wide, D // count)
            at += wide
        ffn = outs[2 * layer]
        for j, block in enumerate(blocks):
            ffn[j * rows : (j + 1) * rows, :cols] = block[:, at : at + cols]
        fold_in(ffn, down.at[layer], cols, cols)
        at += cols


def pack_rest(blocks, down, out_w, wide, cols):
    count = len(blocks)
    rows = blocks[0].shape[0]
    layers = down.shape[0]
    outs = []
    for layer in range(layers):
        if layer:
            outs.append(shape((count * rows, wide + D // count), BF))
        outs.append(shape((count * rows, 2 * cols), BF))
    return run(
        functools.partial(pack_rest_kernel, count, layers, wide), outs, [], blocks + [down, out_w]
    )


def params_kernel(hs, ts, xs, rows, layers, each, me, *refs):
    pieces = refs[: hs * ts]
    vec, up, qkv = refs[hs * ts :]
    count = hs * ts * ts
    values = jnp.concatenate([p[ts * rows : ts * rows + ts, : qkv.shape[1]].astype(F32) for p in pieces], 0).astype(BF)
    at = lax.broadcasted_iota(jnp.int32, (1, count), 1)
    kh, kb, slot = at // (ts * ts), (at // ts) % ts, at % ts
    k, dc = slot // CORES, slot % CORES
    h = lax.rem(me[0] - kh + hs, hs)
    l = lax.rem(me[1] - k + xs, xs) * CORES + lax.rem(me[2] + dc, CORES)
    b = lax.rem(me[3] - kb + ts, ts)
    owner = (h * ts + l) * ts + b
    pick = (lax.broadcasted_iota(jnp.int32, (count, count), 0) == owner).astype(BF)
    table = nn(pick, values).astype(BF)
    lo = me[1] * CORES + me[2]

    def spread(first, size, wide):
        tile = lax.broadcasted_iota(jnp.int32, (size, wide), 1) % size
        same = (tile == lax.broadcasted_iota(jnp.int32, (size, wide), 0)).astype(BF)
        return nn(table[:, first : first + size], same)

    def keep(x, mask):
        return jnp.sum(jnp.where(mask, x, 0.0), axis=0, keepdims=True)

    row = lambda wide: lax.broadcasted_iota(jnp.int32, (count, wide), 0)
    col = lambda wide: lax.broadcasted_iota(jnp.int32, (count, wide), 1)
    full = each * count
    own_up, own_q = full * up.shape[1] // D, qkv.shape[1] // 3
    for layer in range(layers):
        first = layer * each * 12
        member = row(own_q) // ts % ts == lo
        part = row(own_q) % ts == col(own_q) // (2 * each)
        half = row(own_q) // (ts * ts)
        q = spread(first, 2 * each, own_q)
        qkv[layer : layer + 1, :own_q] = keep(q, member & part & (half == 0))
        qkv[layer : layer + 1, own_q : 2 * own_q] = jnp.zeros((1, own_q), F32)
        qkv[layer : layer + 1, 2 * own_q :] = keep(q, member & part & (half == 1))
        first = first + 2 * each
        mine = col(full) // each == row(full)
        for f, skip in enumerate((0, 5, 6, 7, 8, 9)):
            vec[layer * 6 + f : layer * 6 + f + 1, :] = keep(spread(first + skip * each, each, full), mine)
        here = (row(own_up) // ts % ts == lo) & (
            (row(own_up) // (ts * ts)) * ts + row(own_up) % ts == col(own_up) // (4 * each)
        )
        up[layer : layer + 1, :] = keep(spread(first + each, 4 * each, own_up), here)


def params(me, pieces, rows, layers, each, own_up, own_q, hs, ts, xs):
    return run(
        functools.partial(params_kernel, hs, ts, xs, rows, layers, each),
        [shape((layers * 6, D), F32), shape((layers, own_up), F32), shape((layers, 3 * own_q), F32)],
        [me],
        pieces,
    )


def fold_out(piece, rows, at, cols, parts):
    return jnp.concatenate([piece[p * rows : (p + 1) * rows, at : at + cols] for p in range(parts)], 1)


def piece_at(refs, at, whole, hs, ts, me):
    kh, kb = at // ts, at % ts
    h = lax.rem(me[0] - kh + hs, hs)
    if whole:
        return refs[kh].at[kb], h, kb
    return refs[at], h, lax.rem(me[3] - kb + ts, ts)


def place_attn_kernel(hs, ts, xs, whole, with_out, me, *refs):
    qkv = refs[-2] if with_out else refs[-1]
    rows, wide = qkv.shape[3:]
    for at in range(hs * ts):
        piece, h, b = piece_at(refs, at, whole, hs, ts, me)
        for j, (k, dc) in enumerate(slots_of(xs)):
            qkv[h, lo_minus(me, xs, k, dc), b] = piece[j * rows : (j + 1) * rows, :wide]
        if with_out:
            out = refs[-1]
            cols = out.shape[3] // ts
            for p in range(ts):
                out[h, b, :, p * cols : (p + 1) * cols] = piece[p * rows : (p + 1) * rows, wide : wide + cols]


def place_attn(me, pieces, rows, hs, ts, xs, with_out):
    whole = len(pieces) == hs
    wide = 3 * D // ts
    got = run(
        functools.partial(place_attn_kernel, hs, ts, xs, whole, with_out),
        [shape((hs, ts, ts, rows, wide), BF)] + ([shape((hs, ts, rows, D), BF)] if with_out else []),
        [me],
        pieces,
    )
    return (got[0].reshape(D, wide),) + tuple(got[1:])


def place_ffn_kernel(hs, ts, xs, whole, me, *refs):
    up, down = refs[-2:]
    rows, cols = up.shape[3:]
    tall = down.shape[2]
    for at in range(hs * ts):
        piece, h, b = piece_at(refs, at, whole, hs, ts, me)
        for j, (k, dc) in enumerate(slots_of(xs)):
            up[h, lo_minus(me, xs, k, dc), b] = piece[j * rows : (j + 1) * rows, :cols]
        for p in range(D // cols):
            down[h, b, :, p * cols : (p + 1) * cols] = piece[p * tall : (p + 1) * tall, cols:]


def place_ffn(me, pieces, hs, ts, xs):
    whole = len(pieces) == hs
    tall, wide = pieces[0].shape[-2:]
    cols = wide // 2
    up, down = run(
        functools.partial(place_ffn_kernel, hs, ts, xs, whole),
        [shape((hs, ts, ts, tall // ts, cols), BF), shape((hs, ts, tall * cols // D, D), BF)],
        [me],
        pieces,
    )
    return up.reshape(D, cols), down.reshape(-1, D)


def place_out_kernel(hs, ts, xs, me, *refs):
    out = refs[-1]
    for j, (k, dc) in enumerate(slots_of(xs)):
        out[:, lo_minus(me, xs, k, dc)] = refs[j][...]


def place_out(me, group, hs, ts, xs):
    _, _, rows, wide = group[0].shape
    (got,) = run(
        functools.partial(place_out_kernel, hs, ts, xs), [shape((hs, ts, ts, rows, wide), BF)], [me], group
    )
    return got.reshape(-1, wide)


def attn_fwd_kernel(ts, xs, heads, raw, layer, me, slopes, *refs):
    given = refs[:ts]
    if raw:
        w, bias, vec = refs[ts : ts + 3]
        qkv, out_t, lse, seg_row, seg_col = refs[ts + 3 : ts + 8]
        outs, normed = refs[ts + 8 : 2 * ts + 8], refs[2 * ts + 8 : 3 * ts + 8]
    else:
        normed = given
        w, bias, seg_row, seg_col = refs[ts : ts + 4]
        qkv, out_t, lse = refs[ts + 4 : ts + 7]
        outs = refs[ts + 7 :]
    n = normed[0].shape[0]
    width = heads * HEAD_DIM
    for j, (k, dc) in enumerate(slots_of(xs)):
        off = pl.multiple_of(block_minus(me, xs, k, dc) * n, n)
        if raw:
            unit, _ = norm_parts(given[j][:n, :].astype(F32))
            normed[j][...] = (unit * vec[2:3, :] + vec[4:5, :]).astype(BF)
            ids = given[j][n : n + 8, :n].astype(F32)
            ids = ids[0:1, :] * 256.0 + ids[1:2, :]
            seg_row[:, pl.ds(off, n)] = ids
            seg_col[pl.ds(off, n), :] = jnp.broadcast_to(ids, (128, n)).T
        got = nn(normed[j][...], w[...]) + bias[layer : layer + 1, :]
        qkv[pl.ds(off, n), :] = got.astype(BF)
    scale = HEAD_DIM ** (-0.5)
    for i in range(ts):
        length = (i + 1) * n
        key_at = lax.broadcasted_iota(jnp.int32, (length, n), 0)
        query_at = lax.broadcasted_iota(jnp.int32, (length, n), 1) + i * n
        allowed = (seg_col[:length, 0:1] == seg_row[:, i * n : length]) & (key_at <= query_at)
        distance = (query_at - key_at).astype(F32)
        for h in range(heads):
            here = h * HEAD_DIM
            q = qkv[i * n : length, here : here + HEAD_DIM]
            keys = qkv[:length, width + here : width + here + HEAD_DIM]
            values = qkv[:length, 2 * width + here : 2 * width + here + HEAD_DIM]
            s = nt(keys, q) * scale - slopes[h] * distance
            s = jnp.where(allowed, s, masked_score)
            top = jnp.max(s, axis=0, keepdims=True)
            p = jnp.exp(s - top)
            total = jnp.sum(p, axis=0, keepdims=True)
            out_t[here : here + HEAD_DIM, i * n : length] = tn(values, p.astype(BF)) / total
            lse[h : h + 1, i * n : length] = top + jnp.log(total)
    for j, (k, dc) in enumerate(slots_of(xs)):
        off = pl.multiple_of(block_minus(me, xs, k, dc) * n, n)
        outs[j][...] = out_t[:, pl.ds(off, n)].T.astype(BF)


def attn_fwd(me, slopes, given, w, bias, layer, xs, vec=None, segs=None):
    ts = len(given)
    raw = vec is not None
    heads = slopes.shape[0]
    n = given[0].shape[0] - (TILE if raw else 0)
    length, width = ts * n, heads * HEAD_DIM
    got = run(
        functools.partial(attn_fwd_kernel, ts, xs, heads, raw, layer),
        [shape((length, 3 * width), BF), shape((width, length), F32), shape((heads, length), F32)]
        + ([shape((1, length), F32), shape((length, 128), F32)] if raw else [])
        + [shape((n, width), BF)] * ts
        + ([shape((n, D), BF)] * ts if raw else []),
        [me, slopes],
        given + [w, bias] + ([vec] if raw else list(segs)),
        flops=2 * length * D * 3 * width + 3 * length * length * width,
    )
    if raw:
        return got[0], got[1], got[2], list(got[5 : 5 + ts]), list(got[5 + ts :]), (got[3], got[4])
    return got[0], got[1], got[2], list(got[3:]), given, segs


def attn_bwd_kernel(ts, xs, heads, me, slopes, *refs):
    grads = refs[:ts]
    qkv, out_t, lse, w, seg_row, seg_col = refs[ts : ts + 6]
    parts = refs[ts + 6 : 2 * ts + 6]
    souts = refs[2 * ts + 6 : 3 * ts + 6]
    gbuf, dq_buf, dk_buf, dv_buf = refs[3 * ts + 6 :]
    n = grads[0].shape[0]
    width = heads * HEAD_DIM
    scale = HEAD_DIM ** (-0.5)
    for j, (k, dc) in enumerate(slots_of(xs)):
        off = pl.multiple_of(block_minus(me, xs, k, dc) * n, n)
        gbuf[pl.ds(off, n), :] = grads[j][...]
    dk_buf[...] = jnp.zeros_like(dk_buf)
    dv_buf[...] = jnp.zeros_like(dv_buf)
    for i in range(ts):
        length = (i + 1) * n
        key_at = lax.broadcasted_iota(jnp.int32, (length, n), 0)
        query_at = lax.broadcasted_iota(jnp.int32, (length, n), 1) + i * n
        allowed = (seg_col[:length, 0:1] == seg_row[:, i * n : length]) & (key_at <= query_at)
        distance = (query_at - key_at).astype(F32)
        for h in range(heads):
            here = h * HEAD_DIM
            q = qkv[i * n : length, here : here + HEAD_DIM]
            keys = qkv[:length, width + here : width + here + HEAD_DIM]
            values = qkv[:length, 2 * width + here : 2 * width + here + HEAD_DIM]
            g = gbuf[i * n : length, here : here + HEAD_DIM]
            delta = jnp.sum(
                g.astype(F32).T * out_t[here : here + HEAD_DIM, i * n : length], axis=0, keepdims=True
            )
            s = nt(keys, q) * scale - slopes[h] * distance
            p = jnp.where(allowed, jnp.exp(s - lse[h : h + 1, i * n : length]), 0.0)
            ds = (p * (nt(values, g) - delta)).astype(BF)
            dq_buf[i * n : length, here : here + HEAD_DIM] = tn(ds, keys) * scale
            dk_buf[:length, here : here + HEAD_DIM] += nn(ds, q)
            dv_buf[:length, here : here + HEAD_DIM] += nn(p.astype(BF), g)
    for j, (k, dc) in enumerate(slots_of(xs)):
        off = pl.multiple_of(block_minus(me, xs, k, dc) * n, n)
        rows = pl.ds(off, n)
        parts[j][:, :width] = dq_buf[rows, :].astype(BF)
        parts[j][:, width : 2 * width] = (dk_buf[rows, :] * scale).astype(BF)
        parts[j][:, 2 * width :] = dv_buf[rows, :].astype(BF)
        souts[j][...] = nt(parts[j][...], w[...]).astype(souts[j].dtype)


def attn_bwd(me, slopes, grads, qkv, out_t, lse, w, seg_row, seg_col, xs):
    ts = len(grads)
    heads = slopes.shape[0]
    n = grads[0].shape[0]
    length, width = ts * n, heads * HEAD_DIM
    got = run(
        functools.partial(attn_bwd_kernel, ts, xs, heads),
        [shape((n, 3 * width), BF)] * ts + [shape((n, D), F32)] + [shape((n, D), BF)] * (ts - 1),
        [me, slopes],
        grads + [qkv, out_t, lse, w, seg_row, seg_col],
        scratch=[pltpu.VMEM((length, width), BF)] + [pltpu.VMEM((length, width), F32)] * 3,
        flops=2 * length * D * 3 * width + 6 * length * length * width,
    )
    return list(got[:ts]), list(got[ts:])


def out_kernel(ts, xs, at, me, *refs):
    heads = refs[:ts]
    w, vec, stream, middle, normed = refs[ts:]
    width = heads[0].shape[1]
    total = stream[: middle.shape[0], :].astype(F32) + vec[at : at + 1, :]
    for j, (k, dc) in enumerate(slots_of(xs)):
        off = pl.multiple_of(lo_plus(me, xs, k, dc) * width, width)
        total = total + nn(heads[j][...], w[pl.ds(off, width), :])
    middle[...] = total
    unit, _ = norm_parts(total)
    normed[...] = (unit * vec[at + 3 : at + 4, :] + vec[at + 5 : at + 6, :]).astype(BF)


def out_project(me, heads, w, vec, layer, stream, xs):
    n = heads[0].shape[0]
    return run(
        functools.partial(out_kernel, len(heads), xs, 6 * layer),
        [shape((n, D), F32), shape((n, D), BF)],
        [me],
        heads + [w, vec, stream],
        flops=2 * n * D * D,
    )


def ffn_fwd_kernel(count, layer, *refs):
    normed = refs[:count]
    up, bias, down = refs[count : count + 3]
    outs = refs[count + 3 :]
    root, cubic = 0.7978845608028654, 0.044715
    for j in range(count):
        hidden, slope, part = outs[3 * j : 3 * j + 3]
        u = nn(normed[j][...], up[...]) + bias[layer : layer + 1, :]
        square = u * u
        t = jnp.tanh(root * (u + cubic * square * u))
        half = 0.5 * (1.0 + t)
        hidden[...] = (u * half).astype(BF)
        slope[...] = (half + 0.5 * u * (1.0 - t * t) * (root * (1.0 + 3.0 * cubic * square))).astype(BF)
        part[...] = nn(hidden[...], down[...]).astype(part.dtype)


def ffn_fwd(normed, up, bias, layer, down, kinds):
    n = normed[0].shape[0]
    wide = up.shape[1]
    outs = []
    for kind in kinds:
        outs += [shape((n, wide), BF), shape((n, wide), BF), shape((n, D), kind)]
    got = run(
        functools.partial(ffn_fwd_kernel, len(normed), layer),
        outs,
        [],
        normed + [up, bias, down],
        flops=4 * n * D * wide * len(normed),
    )
    return list(got[0::3]), list(got[1::3]), list(got[2::3])


def ffn_bwd_kernel(count, *refs):
    grads, slopes = refs[:count], refs[count : 2 * count]
    up, down = refs[2 * count : 2 * count + 2]
    outs = refs[2 * count + 2 :]
    for j in range(count):
        du, part = outs[2 * j : 2 * j + 2]
        du[...] = (nt(grads[j][...], down[...]) * slopes[j][...].astype(F32)).astype(BF)
        part[...] = nt(du[...], up[...]).astype(part.dtype)


def ffn_bwd(grads, slopes, up, down, kinds):
    n = grads[0].shape[0]
    wide = up.shape[1]
    outs = []
    for kind in kinds:
        outs += [shape((n, wide), BF), shape((n, D), kind)]
    got = run(
        functools.partial(ffn_bwd_kernel, len(grads)),
        outs,
        [],
        grads + slopes + [up, down],
        flops=4 * n * D * wide * len(grads),
    )
    return list(got[0::2]), list(got[1::2])


def end_kernel(count, at, last, *refs):
    terms = refs[:count]
    middle, vec = refs[count : count + 2]
    total = middle[...] + vec[at + 1 : at + 2, :]
    for t in terms:
        total = total + t[...].astype(F32)
    if last:
        refs[-1][...] = total.astype(BF)
        return
    stream, normed = refs[count + 2 :]
    stream[...] = total
    unit, _ = norm_parts(total)
    normed[...] = (unit * vec[at + 8 : at + 9, :] + vec[at + 10 : at + 11, :]).astype(BF)


def layer_end(terms, middle, vec, layer, last):
    n = middle.shape[0]
    outs = [shape((n, D), BF)] if last else [shape((n, D), F32), shape((n, D), BF)]
    return run(functools.partial(end_kernel, len(terms), 6 * layer, last), outs, [], terms + [middle, vec])


def norm_back(values, gain, grad):
    unit, rstd = norm_parts(values)
    scaled = grad * gain
    lead = jnp.mean(scaled, axis=-1, keepdims=True)
    along = jnp.mean(scaled * unit, axis=-1, keepdims=True)
    back = rstd * (scaled - lead - unit * along)
    return back, jnp.sum(grad * unit, axis=0, keepdims=True), jnp.sum(grad, axis=0, keepdims=True)


def mid_back_kernel(count, ts, xs, at, me, *refs):
    terms = refs[:count]
    grad, middle, vec, w = refs[count : count + 4]
    dh, dy, sums = refs[count + 4 : count + 7]
    outs = refs[count + 7 :]
    total = terms[0][...].astype(F32)
    for t in terms[1:]:
        total = total + t[...].astype(F32)
    back, gains, shifts = norm_back(middle[...], vec[at : at + 1, :], total)
    now = grad[...].astype(F32) + back
    dh[...] = now
    dy[...] = now.astype(BF)
    sums[0:1, :] = gains
    sums[1:2, :] = shifts
    sums[2:3, :] = jnp.sum(dy[...].astype(F32), axis=0, keepdims=True)
    width = outs[0].shape[1]
    for j, (k, dc) in enumerate(slots_of(xs)):
        off = pl.multiple_of(lo_plus(me, xs, k, dc) * width, width)
        outs[j][...] = nt(dy[...], w[pl.ds(off, width), :]).astype(BF)


def mid_back(me, terms, grad, middle, vec, layer, w, ts, xs):
    n = middle.shape[0]
    got = run(
        functools.partial(mid_back_kernel, len(terms), ts, xs, 6 * layer + 3),
        [shape((n, D), F32), shape((n, D), BF), shape((3, D), F32)] + [shape((n, D // ts), BF)] * ts,
        [me],
        terms + [grad, middle, vec, w],
        flops=2 * n * D * D,
    )
    return got[0], got[1], got[2], list(got[3:])


def start_back_kernel(count, at, *refs):
    terms = refs[:count]
    grad, stream, vec, dh, dz, sums = refs[count:]
    total = terms[0][...].astype(F32)
    for t in terms[1:]:
        total = total + t[...].astype(F32)
    back, gains, shifts = norm_back(stream[: dh.shape[0], :].astype(F32), vec[at : at + 1, :], total)
    now = grad[...] + back
    dh[...] = now
    dz[...] = now.astype(BF)
    sums[0:1, :] = gains
    sums[1:2, :] = shifts
    sums[2:3, :] = jnp.sum(dz[...].astype(F32), axis=0, keepdims=True)


def start_back(terms, grad, stream, vec, layer):
    n = grad.shape[0]
    return run(
        functools.partial(start_back_kernel, len(terms), 6 * layer + 2),
        [shape((n, D), F32), shape((n, D), BF), shape((3, D), F32)],
        [],
        terms + [grad, stream, vec],
    )


def column_sums(refs):
    total = jnp.sum(refs[0][...].astype(F32), axis=0, keepdims=True)
    for b in refs[1:]:
        total = total + jnp.sum(b[...].astype(F32), axis=0, keepdims=True)
    return total


def cols_part(ts, xs, hs, rows, own, me, left, right, put):
    tile = CORES * ts * rows
    for kh in list(range(1, hs)) + [0]:
        h = kh if own else lax.rem(me[0] + kh, hs)
        for k in range(xs):
            place_at = (h * ts + lax.rem(me[1] + k, xs) * CORES) * ts * rows
            cols = pl.ds(pl.multiple_of(place_at, tile), tile)
            got = tn(left[0][:, cols], right[0][...])
            for j in range(1, ts):
                got = got + tn(left[j][:, cols], right[j][...])
            for c in range(CORES):
                dc = lax.rem(me[2] + c, CORES)
                for b in range(ts):
                    kb = b if own else lax.rem(b - me[3] + ts, ts)
                    at = (c * ts + b) * rows
                    put(kh, kb, dc, k, got[at : at + rows, :].astype(BF))


def wgrad_cols_kernel(ts, xs, hs, rows, beside, own, me, *refs):
    left, right = refs[:ts], refs[ts : 2 * ts]
    refs = refs[2 * ts :]
    if beside:
        near, refs = refs[0], refs[1:]
    refs[0][...] = column_sums(right)
    outs = refs[1:]
    wide = right[0].shape[1]

    def put(kh, kb, dc, k, block):
        outs[kh][kb, k * CORES + dc, :, :wide] = block

    cols_part(ts, xs, hs, rows, own, me, left, right, put)
    if beside:
        cols = outs[0].shape[3] - wide
        for kh in range(hs):
            for kb in range(ts):
                to = lax.rem(me[3] + kb, ts) if own else kb
                where = lax.rem(kh - me[0] + hs, hs) if own else kh
                for p in range(ts):
                    outs[kh][to, p, :, wide:] = near[where, kb, :, p * cols : (p + 1) * cols]


def wgrad_cols(me, left, right, hs, xs, own, near=None):
    ts = len(left)
    rows = D // (hs * ts * ts)
    n, wide = right[0].shape
    beside = near is not None
    outs = [shape((ts, ts, rows, wide + (D // ts if beside else 0)), BF)] * hs
    if own:
        outs = [shape((hs,) + outs[0].shape, BF)]
    got = run(
        functools.partial(whole_kernel(wgrad_cols_kernel) if own else wgrad_cols_kernel, ts, xs, hs, rows, beside, own),
        [shape((1, wide), F32)] + outs,
        [me],
        left + right + ([near] if beside else []),
        flops=2 * ts * n * D * wide,
    )
    return got[0], list(got[1:])


def wgrad_ffn_kernel(ts, xs, hs, rows, tall, own, me, *refs):
    normed, du, hidden, dz = [refs[j * ts : (j + 1) * ts] for j in range(4)]
    refs[4 * ts][...] = column_sums(du)
    outs = refs[4 * ts + 1 :]
    cols = du[0].shape[1]

    def put(kh, kb, dc, k, block):
        outs[kh][kb, k * CORES + dc] = block

    cols_part(ts, xs, hs, rows, own, me, normed, du, put)
    group = min(ts, max(1, 256 // tall))
    for kh in list(range(1, hs)) + [0]:
        h = kh if own else lax.rem(me[0] + kh, hs)
        for first in range(0, ts, group):
            take = pl.ds(pl.multiple_of((h * ts + first) * tall, group * tall), group * tall)
            got = tn(hidden[0][:, take], dz[0][...])
            for j in range(1, ts):
                got = got + tn(hidden[j][:, take], dz[j][...])
            for b in range(group):
                kb = first + b if own else lax.rem(first + b - me[3] + ts, ts)
                for g in range(ts):
                    p, low = (g * rows) // tall, (g * rows) % tall
                    outs[kh][kb, ts + g] = got[
                        b * tall + low : b * tall + low + rows, p * cols : (p + 1) * cols
                    ].astype(BF)


def wgrad_ffn(me, normed, du, hidden, dz, hs, xs, own):
    ts = len(normed)
    rows = D // (hs * ts * ts)
    n, wide = du[0].shape
    outs = [shape((ts, 2 * ts, rows, wide), BF)] * hs
    if own:
        outs = [shape((hs, ts, 2 * ts, rows, wide), BF)]
    got = run(
        functools.partial(wgrad_ffn_kernel if not own else whole_kernel(wgrad_ffn_kernel), ts, xs, hs, rows, wide // (hs * ts), own),
        [shape((1, wide), F32)] + outs,
        [me],
        normed + du + hidden + dz,
        flops=4 * ts * n * D * wide,
    )
    return got[0], list(got[1:])


def whole_kernel(kernel):
    def wrapped(ts, xs, hs, *rest):
        return kernel(ts, xs, hs, *rest[:-1], *[rest[-1].at[h] for h in range(hs)])

    return wrapped


def wgrad_out_kernel(ts, xs, hs, rows, me, *refs):
    left = refs[:ts]
    right, out = refs[ts], refs[ts + 1]
    width = left[0].shape[1]
    for j, (k, dc) in enumerate(slots_of(xs)):
        got = tn(left[j][...], right[...])
        first = lo_plus(me, xs, k, dc) * (width // rows)
        for g in range(width // rows):
            i = first + g
            h = lax.div(i, ts * ts)
            lo = lax.rem(lax.div(i, ts), ts)
            b = lax.rem(i, ts)
            kk = lax.rem(lax.div(lo, CORES) - me[1] + xs, xs)
            dd = lax.rem(lax.rem(lo, CORES) + me[2], CORES)
            kh = lax.rem(h - me[0] + hs, hs)
            kb = lax.rem(b - me[3] + ts, ts)
            out[dd, kk, kh, kb] = got[g * rows : (g + 1) * rows, :].astype(BF)


def wgrad_out(me, left, right, hs, xs):
    ts = len(left)
    rows = D // (hs * ts * ts)
    (got,) = run(
        functools.partial(wgrad_out_kernel, ts, xs, hs, rows),
        [shape((CORES, xs, hs, ts, rows, D), BF)],
        [me],
        left + [right],
        flops=2 * right.shape[0] * D * D,
    )
    return got


def finish_kernel(counts, wide, ts, xs, *refs):
    layers = len(counts)
    outs = refs[-ts - 2 : -2]
    out_out, out_down = refs[-2:]
    rows, cols = refs[0].shape[1:]
    at = 0

    def total(count, j):
        got = refs[at][j].astype(F32)
        for t in refs[at + 1 : at + count]:
            got = got + t[j].astype(F32)
        return got

    for layer in range(layers):
        for j in range(ts):
            got = total(counts[layer], j)
            outs[j][layer * rows : (layer + 1) * rows, wide:] = got.astype(BF)
            got = total(counts[layer], ts + j)
            tall = out_down.shape[1]
            p, low = (j * rows) // tall, (j * rows) % tall
            out_down[layer, low : low + rows, p * cols : (p + 1) * cols] = got
        at += counts[layer]
    for layer in range(layers):
        for j in range(ts):
            got = total(counts[layer], j)
            outs[j][layer * rows : (layer + 1) * rows, :wide] = got[:, :wide].astype(BF)
            more = got.shape[1] - wide
            out_out[layer, :, j * more : (j + 1) * more] = got[:, wide:]
        at += counts[layer]


def finish(f_all, a_all, wide, ts, xs):
    layers = len(f_all)
    rows, cols = f_all[0][0].shape[1:]
    tall = ts * rows * cols // D
    got = run(
        functools.partial(finish_kernel, [len(f) for f in f_all], wide, ts, xs),
        [shape((layers * rows, wide + cols), BF)] * ts
        + [shape((layers, rows, D), F32), shape((layers, tall, D), F32)],
        [],
        [x for terms in f_all + a_all for x in terms],
    )
    return dict(zip(slots_of(xs), got)), got[ts], got[ts + 1]


def join_kernel(ts, xs, layers, me, *refs):
    out_q, out_u = refs[-2:]
    wide = out_q.shape[2] // (3 * ts)
    chunk = out_u.shape[2] // (2 * ts)
    rows = out_q.shape[1]
    for block, (k, dc) in zip(refs, slots_of(xs)):
        lo = lo_minus(me, xs, k, dc)
        for layer in range(layers):
            at = pl.ds(layer * rows, rows)
            for j in range(3):
                off = pl.multiple_of((j * ts + lo) * wide, 128)
                out_q[layer, :, pl.ds(off, wide)] = block[at, j * wide : (j + 1) * wide].astype(F32)
            for j in range(2):
                off = pl.multiple_of((j * ts + lo) * chunk, 128)
                have = 3 * wide + j * chunk
                out_u[layer, :, pl.ds(off, chunk)] = block[at, have : have + chunk].astype(F32)


def join(me, blocks, layers, ts, xs):
    arrays = [blocks[s] for s in slots_of(xs)]
    rows = arrays[0].shape[0] // layers
    wide = 3 * D // ts
    return run(
        functools.partial(join_kernel, ts, xs, layers),
        [shape((layers, rows, 3 * D), F32), shape((layers, rows, (arrays[0].shape[1] - wide) * ts), F32)],
        [me],
        arrays,
    )


def on_device(
    hs,
    ts,
    xs,
    tokens,
    segment_ids,
    out_grad,
    qkv_weight,
    qv_bias,
    out_weight,
    out_bias,
    up_weight,
    up_bias,
    down_weight,
    down_bias,
    norm_gain,
    norm_shift,
):
    layers = qkv_weight.shape[0]
    n = tokens.shape[1]
    length = ts * n
    heads = HEADS // ts
    index = tuple(lax.axis_index(a) for a in (HI, XX, CORE, BLK))
    hi, xx, core, blk = index
    lo = xx * CORES + core
    me = jnp.stack(index).astype(jnp.int32)
    slots = slots_of(xs)
    place_of = [(a % xs) * CORES + a // xs for a in range(ts)]
    turn = [(place_of[a] * ts + b, place_of[b] * ts + a) for a in range(ts) for b in range(ts)]
    turned = lambda x: lax.ppermute(x, (XX, CORE, BLK), turn)
    rows, each = qkv_weight.shape[1], out_bias.shape[1]
    wide, cols = 3 * D // ts, up_weight.shape[2] // ts
    fields = (qv_bias, out_bias, up_bias, down_bias, norm_gain, norm_shift)
    slopes = jnp.exp2(-8.0 * (lo * heads + jnp.arange(heads, dtype=F32) + 1.0) / HEADS)

    def own_columns(cuts):
        mine = exchange_lo(cuts, xs, 1)
        return [mine[s] for s in slots]

    def gather_out(near):
        group = gather_lo(near, xs)
        return place_out(me, [group[s] for s in slots], hs, ts, xs)

    def along_blk(x):
        return lax.all_gather(x, BLK, axis=0, tiled=False)

    def with_hi(x):
        return [x] + [shift(x, HI, hs, kh) for kh in range(1, hs)]

    tokens_own = turned(message_of(tokens[0], segment_ids))
    attn_out, ffn_out = {}, {}
    mine = own_columns(near_cuts_of(me, qkv_weight, fields, xs, ts))
    attn_work = Work(fetch(pack_first(mine, out_weight), attn_out, hs, ts))
    late_q, late_u = tie((qkv_weight, up_weight), mine)
    same, other = rest_cuts_of(me, late_q, late_u, xs, ts)
    other = shift(other, CORE, CORES, 1)
    rest = [same[0], other[0]]
    for k in range(1, xs):
        pair = shift(jnp.stack([same[k], other[k]]), XX, xs, k)
        rest += [pair[0], pair[1]]
    packed = pack_rest(rest, down_weight, out_weight, wide, cols)
    attn_work.step(tokens_own)
    by = gather_lo(tokens_own, xs)
    given = [by[s] for s in slots]
    for kb in range(1, ts):
        attn_work.step(*([packed[0]] if kb == 1 else [by[xs - 1, 0]] if kb == 2 else []))
    attn_pieces = pieces_of(attn_out, hs, ts)
    ffn_work = Work(fetch(packed[0], ffn_out, hs, ts))
    stacks = []
    for l in range(1, layers):
        attn_stack = along_blk(packed[2 * l - 1])
        stacks.append((attn_stack, along_blk(tie(packed[2 * l], attn_stack))))
    w_qkv, out_near = place_attn(me, attn_pieces, rows, hs, ts, xs, True)
    vec, up_vec, qkv_vec = params(me, attn_pieces, rows, layers, each, cols, wide // 3, hs, ts, xs)

    stream = tokens_own
    stored, weights = [], []
    segs = None
    for l in range(layers):
        more = l + 1 < layers
        if l == 0:
            given = tie(given, ffn_work.step(w_qkv))
        w_out = gather_out(out_near)
        qkv, out_t, lse, heads_by, all_one, segs = attn_fwd(
            me, slopes, given, w_qkv, qkv_vec, l, xs, vec if l == 0 else None, segs
        )
        own = exchange_lo({s: heads_by[j] for j, s in enumerate(slots)}, xs, -1)
        own = [own[s] for s in slots]
        if l == 0:
            own = tie(own, ffn_work.step(heads_by))
        if not more:
            own = tie(own, grad_x)
        middle, normed_two = out_project(me, own, w_out, vec, l, stream, xs)
        by = gather_lo(normed_two, xs)
        all_two = [by[s] for s in slots]
        near, far = all_two[:CORES], all_two[CORES:]
        if l == 0:
            near = tie(near, ffn_work.step(middle))
            while (hs - 1, ts - 1) not in ffn_out:
                ffn_work.step()
            ffn_pieces = pieces_of(ffn_out, hs, ts)
        w_up, w_down = place_ffn(me, ffn_pieces, hs, ts, xs)
        hid_a, gel_a, part_a = ffn_fwd(near, w_up, up_vec, l, w_down, [F32] + [BF] * (CORES - 1))
        far = tie(far, part_a)
        if more:
            attn_stack, ffn_stack = stacks[l]
            attn_pieces = with_hi(tie(attn_stack, all_two))
        if l + 2 == layers:
            grad_own = turned(tie(out_grad[0], all_two))
        hid_b, gel_b, part_b = ffn_fwd(far, w_up, up_vec, l, w_down, [BF] * len(far))
        terms, sent = scatter_lo(dict(zip(slots, part_a + part_b)), xs)
        stored.append((stream, all_one, qkv, out_t, lse, own, middle, all_two, hid_a + hid_b, gel_a + gel_b))
        weights.append((w_qkv, w_out, w_up, w_down))
        if more:
            stream, normed = layer_end(terms, middle, vec, l, False)
            by = gather_lo(normed, xs)
            given = [by[s] for s in slots]
            ffn_pieces = with_hi(tie(ffn_stack, normed))
            if l + 2 == layers:
                grad_x = [grad_own] + [shift(tie(grad_own, given), XX, xs, k) for k in range(1, xs)]
            w_qkv, out_near = place_attn(me, attn_pieces, rows, hs, ts, xs, True)
        else:
            (final,) = layer_end(terms, middle, vec, l, True)
    grad_by = {}
    for k in range(xs):
        grad_by[k, 0] = grad_x[k]
        grad_by[k, 1] = shift(grad_x[k], CORE, CORES, 1)

    dh, dz = grad_own, grad_own
    down_sum = jnp.sum(grad_own.astype(F32), axis=0, keepdims=True)
    mine_sums, shared_sums = [None] * layers, [None] * layers
    q_grads, u_grads, d_grads, o_grads = [[None] * layers for _ in range(4)]

    def send_cols(terms, at=slice(None)):
        blocks = {s: total_of(terms, (j, slice(None), at)).astype(BF) for j, s in enumerate(slots)}
        return exchange_lo(blocks, xs, 1)

    def unfolded(terms, at=slice(None), count=D // cols):
        total = total_of(terms, (slice(None), slice(None), at))
        total = total.reshape(count, -1, total.shape[-1])
        return jnp.concatenate([total[p] for p in range(count)], 1)

    def added(own, got):
        total = own.astype(F32)
        for g in got:
            total = total + g.astype(F32)
        return total.astype(BF)

    def scattered(x):
        x = x.reshape((hs * ts,) + x.shape[2:])
        return lax.psum_scatter(x, (HI, BLK), scatter_dimension=0, tiled=False)

    def add_up(own, got, *after):
        got = tie(got, after)
        total = []
        for kb in range(ts):
            block = own[kb].astype(F32)
            for g in got:
                block = block + g[kb].astype(F32)
            total.append(block.astype(BF) if kb else block)
        return total

    def send_blk(total):
        return [shift(total[kb], BLK, ts, kb) for kb in range(1, ts)]

    f_sums, a_sums = [None] * layers, [None] * layers
    for l in reversed(range(layers)):
        w_qkv, w_out, w_up, w_down = weights[l]
        stream, all_one, qkv, out_t, lse, own, middle, all_two, hidden, gel = stored[l]
        first_layer, last = l == 0, l + 1 == layers
        by = grad_by if last else gather_lo(dz, xs)
        all_dz = [by[s] for s in slots]
        near, far = all_dz[:CORES], all_dz[CORES:]
        if last:
            near = tie(near, final)
        du_a, part_a = ffn_bwd(near, gel[:CORES], w_up, w_down, [F32] + [BF] * (CORES - 1))
        far = tie(far, part_a)
        du_b, part_b = ffn_bwd(far, gel[CORES:], w_up, w_down, [BF] * (ts - CORES))
        all_du = du_a + du_b
        terms, sent = scatter_lo(dict(zip(slots, part_a + part_b)), xs)
        up_sum, f_parts = wgrad_ffn(me, all_two, tie(all_du, sent), hidden, all_dz, hs, xs, not first_layer)
        terms = tie(terms, up_sum)
        if first_layer:
            f_way = [shift(g, HI, hs, kh + 1) for kh, g in enumerate(f_parts[1:])]
        else:
            f_sums[l] = scattered(f_parts[0])
        dh1, dy, mid_sums, d_heads = mid_back(me, terms, dh, middle, vec, l, w_out, ts, xs)
        by = exchange_lo(dict(zip(slots, d_heads)), xs, 1)
        d_out = [by[s] for s in slots]
        out_part = wgrad_out(me, own, dy, hs, xs)
        got = shift(out_part[1], CORE, CORES, 1)
        both = [(out_part[0, k].astype(F32) + got[k].astype(F32)) for k in range(xs)]
        o_sent = [both[k].astype(BF) for k in range(1, xs)]
        d_out = tie(d_out, o_sent)
        dqkv, parts = attn_bwd(me, slopes, d_out, qkv, out_t, lse, w_qkv, *segs, xs)
        terms, sent = scatter_lo(dict(zip(slots, parts)), xs)
        o_got = [shift(tie(o_sent[k - 1], sent), XX, xs, k) for k in range(1, xs)]
        o_near = both[0]
        for g in tie(o_got, sent):
            o_near = o_near + g.astype(F32)
        if first_layer:
            qkv_sum, a_parts = wgrad_cols(me, all_one, tie(dqkv, sent), hs, xs, False, o_near.astype(BF))
            terms = tie(terms, qkv_sum)
            f_total = add_up(f_parts[0], f_way, qkv_sum)
            terms = tie(terms, f_total)
            f_got = send_blk(f_total)
            a_way = [shift(g, HI, hs, kh + 1) for kh, g in enumerate(a_parts[1:])]
        else:
            qkv_sum, a_parts = wgrad_cols(me, all_one, tie(dqkv, sent), hs, xs, True, o_near.astype(BF))
            a_sums[l] = scattered(tie(a_parts[0], f_sums[l]))
            terms = tie(terms, qkv_sum)
        dh, dz, start_sums = start_back(terms, dh1, stream, vec, l)
        mine_sums[l] = jnp.concatenate([down_sum, mid_sums, start_sums[:2]], 0)
        third = wide // 3
        shared_sums[l] = (up_sum, qkv_sum[:, :third], qkv_sum[:, 2 * third :])
        down_sum = start_sums[2:3]
    full = max(D, shared_sums[0][0].shape[1])
    pad = lambda x: jnp.pad(x, ((0, 0), (0, full - x.shape[1])))
    both = []
    for l in range(layers):
        up_sum, q_sum, v_sum = shared_sums[l]
        both += [pad(up_sum), pad(jnp.concatenate([q_sum, v_sum], 1))]
    mine = jnp.concatenate(mine_sums, 0)
    mine = mine + shift(mine, CORE, CORES, 1)
    mine_x = [shift(mine, XX, xs, k) for k in range(1, xs)]
    a_total = add_up(a_parts[0], a_way, f_got)
    a_got = send_blk(a_total)
    for x in tie(mine_x, a_total):
        mine = mine + x
    small = jnp.concatenate([mine] + both, 0)
    small_y = [shift(small, HI, hs, kh) for kh in range(1, hs)]
    both_turned = turned(jnp.stack([tie(dz, a_total), final]))
    input_grad, result = both_turned[0], both_turned[1]
    for y in small_y:
        small = small + y
    small_z = send_blk([small] * ts)
    f_all = [[f_total[0]] + f_got] + [[f_sums[l]] for l in range(1, layers)]
    a_all = [[a_total[0]] + a_got] + [[a_sums[l]] for l in range(1, layers)]
    blocks, out_grad_all, down_grad_all = finish(f_all, a_all, wide, ts, xs)
    q_grad, u_grad = join(me, exchange_lo(blocks, xs, 1), layers, ts, xs)
    sums = small
    for z in small_z:
        sums = sums + z

    device = (hi * ts + lo) * ts + blk
    vectors = lax.dynamic_slice(sums[: 6 * layers, :D], (0, device * each), (6 * layers, each))
    vectors = vectors.reshape(layers, 6, each)
    shared = sums[6 * layers :].reshape(layers, 2, full)
    up_each, qv_each = up_bias.shape[1], qv_bias.shape[1]
    up_grad = lax.dynamic_slice(shared[:, 0], (0, (hi * ts + blk) * up_each), (layers, up_each))
    qv_grad = lax.dynamic_slice(shared[:, 1], (0, (hi * ts + blk) * qv_each), (layers, qv_each))
    return (
        result[None],
        input_grad[None],
        q_grad,
        qv_grad,
        out_grad_all,
        vectors[:, 3],
        u_grad,
        up_grad,
        down_grad_all,
        vectors[:, 0],
        jnp.stack([vectors[:, 4], vectors[:, 1]], 1),
        jnp.stack([vectors[:, 5], vectors[:, 2]], 1),
    )


def solution(mesh):
    ts = mesh.shape["blk"]
    hs = mesh.shape["rows"] // ts
    xs = ts // CORES
    fine = Mesh(mesh.devices.reshape(hs, xs, CORES, ts), (HI, XX, CORE, BLK))
    rows, every = (HI, XX, CORE), (HI, XX, CORE, BLK)
    row_cut = P(None, every, None)
    vec_cut = P(None, every)
    norm_cut = P(None, None, every)
    cuts = (row_cut, vec_cut, row_cut, vec_cut, row_cut, vec_cut, row_cut, vec_cut, norm_cut, norm_cut)
    acts = P(rows, BLK, None)
    return jax.shard_map(
        functools.partial(on_device, hs, ts, xs),
        mesh=fine,
        in_specs=(acts, P(rows, BLK), acts) + cuts,
        out_specs=(acts, acts) + cuts,
        check_vma=False,
    )
```
